32 devices in a mesh: wide: 8 (over y, x, core), narrow: 4 (over z).
Axes of the slice: x: 2, y: 2, z: 4, core: 2. Of those that a mesh axis runs over, the one named last changes fastest.
Arguments:
- video_clips: bfloat16 [32, 1569, 768], P(('wide', 'narrow')), may hold values from -6 to 6
- time_gain: bfloat16 [768], replicated, may hold values from 0.5 to 1.5
- time_shift: bfloat16 [768], replicated, may hold values from -1 to 1
- time_qkv: bfloat16 [768, 2304], replicated, may hold values from -0.21875 to 0.21875
- time_bias: bfloat16 [2, 768], replicated, may hold values from -1 to 1
- time_proj: bfloat16 [768, 768], replicated, may hold values from -0.4375 to 0.4375
- time_offset: bfloat16 [768], replicated, may hold values from -1 to 1
- space_gain: bfloat16 [768], replicated, may hold values from 0.5 to 1.5
- space_shift: bfloat16 [768], replicated, may hold values from -1 to 1
- space_qkv: bfloat16 [768, 2304], replicated, may hold values from -0.21875 to 0.21875
- space_bias: bfloat16 [2, 768], replicated, may hold values from -1 to 1
- space_proj: bfloat16 [768, 768], replicated, may hold values from -1.75 to 1.75
- space_offset: bfloat16 [768], replicated, may hold values from -1 to 1
- mlp_gain: bfloat16 [768], replicated, may hold values from 0.5 to 1.5
- mlp_shift: bfloat16 [768], replicated, may hold values from -1 to 1
- fc_in: bfloat16 [768, 3072], P(None, 'narrow'), may hold values from -0.21875 to 0.21875
- in_bias: bfloat16 [3072], P('narrow'), may hold values from -1 to 1
- fc_out: bfloat16 [3072, 768], P('narrow'), may hold values from -0.109375 to 0.109375
- out_bias: bfloat16 [768], replicated, may hold values from -1 to 1
- cotangent: bfloat16 [32, 1569, 768], P(('wide', 'narrow')), may hold values from -6 to 6
Outputs:
- layer_out: bfloat16 [32, 1569, 768], P(('wide', 'narrow'))
- grad_clips: float32 [32, 1569, 768], P(('wide', 'narrow'))
- grad_time_gain: float32 [768], P('narrow')
- grad_time_shift: float32 [768], P('narrow')
- grad_time_qkv: float32 [768, 2304], P('narrow', 'wide')
- grad_time_bias: float32 [2, 768], P(None, 'narrow')
- grad_time_proj: float32 [768, 768], P('narrow', 'wide')
- grad_time_offset: float32 [768], P('narrow')
- grad_space_gain: float32 [768], P('narrow')
- grad_space_shift: float32 [768], P('narrow')
- grad_space_qkv: float32 [768, 2304], P('narrow', 'wide')
- grad_space_bias: float32 [2, 768], P(None, 'narrow')
- grad_space_proj: float32 [768, 768], P('narrow', 'wide')
- grad_space_offset: float32 [768], P('narrow')
- grad_mlp_gain: float32 [768], P('narrow')
- grad_mlp_shift: float32 [768], P('narrow')
- grad_fc_in: float32 [768, 3072], P('wide', 'narrow')
- grad_in_bias: float32 [3072], P('narrow')
- grad_fc_out: float32 [3072, 768], P('narrow', 'wide')
- grad_out_bias: float32 [768], P('narrow')
The draws below stay inside these ranges and needn't reach their ends.
All inputs are finite; a program needn't handle non-finite values.
Results may differ from the reference program's by a relative error of at most 0.02.
Values may be sent and summed in bfloat16 or wider, within the bound.
A program may use at most 384 MiB of HBM per device.

```python
import jax
import jax.numpy as jnp
from jax import lax

D = 768
HEADS = 12
HEAD_DIM = 64
FF = 3072
FRAMES = 8
PATCHES = 196
TOK = 1569
CLIPS = 32


def shard_levels(rng, extent, pieces, low, largest):
    def one(axis_at, blocks):
        steps = jax.random.uniform(jax.random.fold_in(jax.random.fold_in(rng, 6), axis_at), (blocks,), jnp.float32, low / len(pieces), largest / len(pieces))
        return jnp.repeat(jnp.exp(steps), extent[axis_at] // blocks).reshape((-1,) + (1,) * (len(extent) - axis_at - 1))

    gain = one(*pieces[0])
    for cut in pieces[1:]:
        gain = gain * one(*cut)
    return gain


def noise(rng, shape, deviation, bound, pieces=(), held_as=jnp.bfloat16):
    entries = jax.random.normal(rng, shape, jnp.float32) * deviation
    if len(pieces) > 0:
        entries = shard_levels(rng, shape, pieces, -0.22, 0.18) * entries
    return jnp.clip(entries, min=-bound, max=bound).astype(held_as)


def setup_inputs(seed: int = 0) -> dict:
    arg_keys = jax.random.split(jax.random.key(seed), 21)
    video_clips = noise(arg_keys[0], (CLIPS, TOK, D), 1.0, 6.0, ((0, 32),))
    time_gain = jnp.clip(1.0 + 0.1 * jax.random.normal(arg_keys[1], (D,), jnp.float32), 0.5, 1.5).astype(jnp.bfloat16)
    time_shift = noise(arg_keys[2], (D,), 0.2, 1.0)
    time_qkv = noise(arg_keys[3], (D, 3 * D), D ** -0.5, 0.21875)
    time_bias = noise(arg_keys[4], (2, D), 0.2, 1.0)
    time_proj = noise(arg_keys[5], (D, D), (D // 4) ** -0.5, 0.4375)
    time_offset = noise(arg_keys[6], (D,), 0.2, 1.0)
    space_gain = jnp.clip(1.0 + 0.1 * jax.random.normal(arg_keys[7], (D,), jnp.float32), 0.5, 1.5).astype(jnp.bfloat16)
    space_shift = noise(arg_keys[8], (D,), 0.2, 1.0)
    space_qkv = noise(arg_keys[9], (D, 3 * D), D ** -0.5, 0.21875)
    space_bias = noise(arg_keys[10], (2, D), 0.2, 1.0)
    space_proj = noise(arg_keys[11], (D, D), (D // 64) ** -0.5, 1.75)
    space_offset = noise(arg_keys[12], (D,), 0.2, 1.0)
    mlp_gain = jnp.clip(1.0 + 0.1 * jax.random.normal(arg_keys[13], (D,), jnp.float32), 0.5, 1.5).astype(jnp.bfloat16)
    mlp_shift = noise(arg_keys[14], (D,), 0.2, 1.0)
    fc_in = noise(arg_keys[15], (D, FF), D ** -0.5, 0.21875, ((1, 4),))
    in_bias = noise(arg_keys[16], (FF,), 0.2, 1.0, ((0, 4),))
    fc_out = noise(arg_keys[17], (FF, D), FF ** -0.5, 0.109375, ((0, 4),))
    out_bias = noise(arg_keys[18], (D,), 0.2, 1.0)
    cotangent = noise(arg_keys[19], (CLIPS, TOK, D), 1.0, 6.0, ((0, 32),))
    return dict(video_clips=video_clips, time_gain=time_gain, time_shift=time_shift, time_qkv=time_qkv, time_bias=time_bias, time_proj=time_proj, time_offset=time_offset, space_gain=space_gain, space_shift=space_shift, space_qkv=space_qkv, space_bias=space_bias, space_proj=space_proj, space_offset=space_offset, mlp_gain=mlp_gain, mlp_shift=mlp_shift, fc_in=fc_in, in_bias=in_bias, fc_out=fc_out, out_bias=out_bias, cotangent=cotangent)


EPSILON = 1e-06
HIGHEST = lax.Precision.HIGHEST

@jax.custom_vjp
def low(v):
    return lax.optimization_barrier(v.astype(jnp.bfloat16)).astype(jnp.float32)

@jax.custom_vjp
def low_back(v):
    return v

def low_keep(v):
    return (low(v), None)

def low_pass(kept, grad):
    return (grad,)

def back_keep(v):
    return (v, None)

def back_low(kept, grad):
    return (low(grad),)
low.defvjp(low_keep, low_pass)
low_back.defvjp(back_keep, back_low)

def layer_norm(values, gain_vec, shift_vec):
    center = values - lax.optimization_barrier(jnp.mean(values, axis=-1, keepdims=True))
    spread = lax.optimization_barrier(jnp.mean(center * center, axis=-1, keepdims=True))
    return center * lax.rsqrt(spread + EPSILON) * gain_vec + shift_vec

def product(left_op, right_op):
    return jnp.dot(left_op, right_op, precision=HIGHEST)

def both_ways(values):
    return low_back(low(values))

def qkv_bias(bias_pair, model_width):
    return jnp.concatenate([bias_pair[0], jnp.zeros((model_width,), jnp.float32), bias_pair[1]])

def frame_view(row_block, model_width):
    head_rows = jnp.broadcast_to(row_block[0:1][None], (FRAMES, 1, model_width))
    rest_rows = row_block[1:].reshape(FRAMES, PATCHES, model_width)
    return jnp.concatenate([head_rows, rest_rows], axis=1).reshape(FRAMES, PATCHES + 1, HEADS, HEAD_DIM)

def clip_forward(clip_rows, params):
    t_gain, t_shift, t_qkv, t_bias, t_proj, t_offset, s_gain, s_shift, s_qkv, s_bias, s_proj, s_offset, m_gain, m_shift, w_in, b_in, w_out, b_out = params
    model_width = clip_rows.shape[1]
    score_scale = HEAD_DIM ** (-0.5)
    patches = clip_rows[1:]
    t_normed = low(layer_norm(patches, t_gain, t_shift))
    t_packed = both_ways(product(t_normed, t_qkv) + qkv_bias(t_bias, model_width))
    shape_four = (FRAMES, PATCHES, HEADS, HEAD_DIM)
    t_query = t_packed[:, :model_width].reshape(shape_four)
    t_key = t_packed[:, model_width:2 * model_width].reshape(shape_four)
    t_value = t_packed[:, 2 * model_width:].reshape(shape_four)
    t_scores = low_back(jnp.einsum('fphd,gphd->phfg', t_query, t_key, precision=HIGHEST) * score_scale)
    t_probs = low(jax.nn.softmax(t_scores, axis=-1))
    t_attn = jnp.einsum('phfg,gphd->fphd', t_probs, t_value, precision=HIGHEST)
    t_attn = both_ways(t_attn.reshape(FRAMES * PATCHES, model_width))
    mixed_t = patches + low_back(product(t_attn, t_proj) + t_offset)
    full_rows = jnp.concatenate([clip_rows[0:1], mixed_t], axis=0)
    s_normed = low(layer_norm(full_rows, s_gain, s_shift))
    s_packed = both_ways(product(s_normed, s_qkv) + qkv_bias(s_bias, model_width))
    s_query = frame_view(s_packed[:, :model_width], model_width)
    s_key = frame_view(s_packed[:, model_width:2 * model_width], model_width)
    s_value = frame_view(s_packed[:, 2 * model_width:], model_width)
    s_scores = low_back(jnp.einsum('fihd,fjhd->fhij', s_query, s_key, precision=HIGHEST) * score_scale)
    s_probs = low(jax.nn.softmax(s_scores, axis=-1))
    s_attn = jnp.einsum('fhij,fjhd->fihd', s_probs, s_value, precision=HIGHEST)
    s_attn = both_ways(s_attn.reshape(FRAMES * (PATCHES + 1), model_width))
    s_out = low_back(product(s_attn, s_proj) + s_offset).reshape(FRAMES, PATCHES + 1, model_width)
    mixed_s = jnp.concatenate([full_rows[0:1] + lax.optimization_barrier(jnp.mean(s_out[:, 0], axis=0))[None], mixed_t + s_out[:, 1:].reshape(FRAMES * PATCHES, model_width)], axis=0)
    m_normed = low(layer_norm(mixed_s, m_gain, m_shift))
    pre_act = low_back(product(m_normed, w_in) + b_in)
    activation = low(jax.nn.gelu(pre_act, approximate=False))
    branch = low_back(product(activation, w_out) + b_out)
    return mixed_s + branch

def reference(video_clips, time_gain, time_shift, time_qkv, time_bias, time_proj, time_offset, space_gain, space_shift, space_qkv, space_bias, space_proj, space_offset, mlp_gain, mlp_shift, fc_in, in_bias, fc_out, out_bias, cotangent):
    params = tuple((entry.astype(jnp.float32) for entry in (time_gain, time_shift, time_qkv, time_bias, time_proj, time_offset, space_gain, space_shift, space_qkv, space_bias, space_proj, space_offset, mlp_gain, mlp_shift, fc_in, in_bias, fc_out, out_bias)))

    def one_clip(totals, inputs):
        clip_rows, grad_out = inputs
        result, pull_back = jax.vjp(clip_forward, clip_rows.astype(jnp.float32), params)
        grad_rows, grad_params = pull_back(grad_out.astype(jnp.float32))
        totals = tuple((first + second for first, second in zip(totals, grad_params)))
        return (totals, (result.astype(jnp.bfloat16), grad_rows))
    start_sums = tuple((jnp.zeros(entry.shape, jnp.float32) for entry in params))
    totals, (outputs, grad_clips) = lax.scan(one_clip, start_sums, (video_clips, cotangent))
    return (outputs, grad_clips, totals[0], totals[1], totals[2], totals[3], totals[4], totals[5], totals[6], totals[7], totals[8], totals[9], totals[10], totals[11], totals[12], totals[13], totals[14], totals[15], totals[16], totals[17])
```

```python
from functools import partial

import jax
import jax.numpy as jnp
from jax import lax
from jax.experimental import pallas as pl
from jax.experimental.pallas import tpu as pltpu
from jax.sharding import PartitionSpec as P

HEADS = 12
HEAD_DIM = 64
FRAMES = 8
PATCHES = 196
ROWS = 208
CLASS = 196
TILE = 16
WIDTH = 768
GROUP = 4
GW = GROUP * HEAD_DIM
GROUPS = HEADS // GROUP
FPS = 2
STEP = FPS * ROWS
EPSILON = 1e-06
F32 = jnp.float32
BF = jnp.bfloat16
NEG = -1e30
VMEM_LIMIT = 60 * 2**20


def dg(a, b, ca, cb):
    return lax.dot_general(a, b, (((ca,), (cb,)), ((), ())), preferred_element_type=F32)


def nn(a, b):
    return dg(a, b, 1, 0)


def nt(a, b):
    return dg(a, b, 1, 1)


def tn(a, b):
    return dg(a, b, 0, 0)


def call(kernel, name, grid, ins, outs, scratch=(), flops=0, nbytes=0):
    return pl.pallas_call(
        kernel,
        name=name,
        grid=grid,
        in_specs=[s for s in ins],
        out_specs=[s for s, _ in outs],
        out_shape=[t for _, t in outs],
        scratch_shapes=list(scratch),
        compiler_params=pltpu.CompilerParams(vmem_limit_bytes=VMEM_LIMIT),
        cost_estimate=pl.CostEstimate(flops=flops, bytes_accessed=nbytes, transcendentals=0),
    )


def whole(*shape):
    return pl.BlockSpec(shape, lambda *i: (0,) * len(shape))


def frames(width):
    return pl.BlockSpec((FPS, ROWS, width), lambda i: (i, 0, 0))


def frames_out(width, dtype):
    return frames(width), jax.ShapeDtypeStruct((FRAMES, ROWS, width), dtype)


def normed(v):
    center = v - jnp.mean(v, axis=-1, keepdims=True)
    scale = lax.rsqrt(jnp.mean(center * center, axis=-1, keepdims=True) + EPSILON)
    return center * scale, scale


def norm_back(grad, xhat, scale, gain):
    g = grad * gain
    m1 = jnp.mean(g, axis=-1, keepdims=True)
    m2 = jnp.mean(g * xhat, axis=-1, keepdims=True)
    return scale * (g - m1 - xhat * m2)


def colsum(v):
    return jnp.sum(v.astype(F32), axis=0, keepdims=True)


def head_masked(block):
    lane = lax.broadcasted_iota(jnp.int32, block.shape, 1) // HEAD_DIM
    zero = jnp.zeros_like(block)
    return jnp.concatenate([jnp.where(lane == h, block, zero) for h in range(GROUP)], axis=0)


def head_select(stacked):
    rows = stacked.shape[0] // GROUP
    lane = lax.broadcasted_iota(jnp.int32, (rows, GW), 1) // HEAD_DIM
    out = stacked[:rows]
    for h in range(1, GROUP):
        out = jnp.where(lane == h, stacked[h * rows : (h + 1) * rows], out)
    return out


def softmax(scores):
    e = jnp.exp(scores - jnp.max(scores, axis=-1, keepdims=True))
    return (e * (1.0 / jnp.sum(e, axis=-1, keepdims=True))).astype(BF)


def group_cols(g, which):
    start = which * WIDTH + g * GW
    return slice(start, start + GW)


def shifted(src_ref, frame, first_row, class_on):
    start = 1 + frame * PATCHES
    base = jnp.minimum(start // TILE * TILE, src_ref.shape[0] // TILE * TILE - ROWS - TILE)
    base = pl.multiple_of(base, TILE)
    chunk = src_ref[pl.ds(base, ROWS + TILE), :]
    row = lax.broadcasted_iota(jnp.int32, (ROWS, ROWS + TILE), 0)
    col = lax.broadcasted_iota(jnp.int32, (ROWS, ROWS + TILE), 1)
    pick = ((col == row + (start - base)) & (row < PATCHES)).astype(F32).astype(BF)
    got = nn(pick, chunk)
    last = src_ref.shape[0] - 1
    end_row = src_ref[last : last + 1, :].astype(F32)
    tail = got[ROWS - TILE :]
    trow = lax.broadcasted_iota(jnp.int32, tail.shape, 0) + (ROWS - TILE)
    tail = jnp.where((trow == PATCHES - 1) & (frame == FRAMES - 1), end_row, tail)
    tail = jnp.where((trow == CLASS) & class_on, first_row, tail)
    return jnp.concatenate([got[: ROWS - TILE], tail], axis=0)


def time_in_kernel(clip_ref, cot_ref, vec_ref, bias_ref, w_ref, p_ref, g_ref, h_ref, z_ref):
    step = pl.program_id(0)
    parts = []
    for j in range(FPS):
        frame = step * FPS + j
        p = shifted(clip_ref, frame, clip_ref[0:1, :].astype(F32), frame >= 0)
        p_ref[j] = p.astype(BF)
        xhat, _ = normed(p)
        parts.append((xhat * vec_ref[0:1] + vec_ref[1:2]).astype(BF))
        g_ref[j] = shifted(cot_ref, frame, cot_ref[0:1, :].astype(F32), frame == 0).astype(BF)
    h = jnp.concatenate(parts, axis=0)
    h_ref[...] = h.reshape(FPS, ROWS, WIDTH)
    project(h, w_ref, bias_ref, z_ref)


def project(h, w_ref, bias_ref, z_ref):
    for which in range(3):
        cols = slice(which * WIDTH, (which + 1) * WIDTH)
        z = nn(h, w_ref[:, cols])
        if which != 1:
            z = z + bias_ref[which // 2 : which // 2 + 1]
        z = z.astype(BF)
        if which == 0:
            z = z * jnp.asarray(HEAD_DIM**-0.5, BF)
        z_ref[:, :, cols] = z.reshape(FPS, ROWS, WIDTH)


def time_attention_kernel(z_ref, o_ref, a_ref):
    z = z_ref[...].reshape(FRAMES * TILE, 3 * WIDTH)
    row = lax.broadcasted_iota(jnp.int32, (GROUP * FRAMES * TILE, FRAMES * TILE), 0)
    col = lax.broadcasted_iota(jnp.int32, (GROUP * FRAMES * TILE, FRAMES * TILE), 1)
    same = (row % TILE) == (col % TILE)
    for g in range(GROUPS):
        q = head_masked(z[:, group_cols(g, 0)])
        s = jnp.where(same, nt(q, z[:, group_cols(g, 1)]), NEG)
        a = softmax(s)
        a_ref[0, g] = a
        o = head_select(nn(a, z[:, group_cols(g, 2)])).astype(BF)
        o_ref[:, :, g * GW : (g + 1) * GW] = o.reshape(FRAMES, TILE, GW)


def space_kernel(
    p_ref, ot_ref, vec_ref, bias_ref, wt_ref, w_ref, wo_ref,
    full_ref, h_ref, z_ref, a_ref, o_ref, x_ref, cls_ref,
):
    p = p_ref[...].reshape(STEP, WIDTH).astype(F32)
    mixed = p + nn(ot_ref[...].reshape(STEP, WIDTH), wt_ref[...]) + vec_ref[2:3]
    row = lax.broadcasted_iota(jnp.int32, (STEP, WIDTH), 0) % ROWS
    full = jnp.where(row == CLASS, p, mixed)
    full_ref[...] = full.reshape(FPS, ROWS, WIDTH)
    xhat, _ = normed(full)
    h = (xhat * vec_ref[3:4] + vec_ref[4:5]).astype(BF)
    h_ref[...] = h.reshape(FPS, ROWS, WIDTH)
    project(h, w_ref, bias_ref, z_ref)
    key = lax.broadcasted_iota(jnp.int32, (GROUP * ROWS, ROWS), 1)
    for j in range(FPS):
        for g in range(GROUPS):
            q = head_masked(z_ref[j, :, group_cols(g, 0)])
            s = jnp.where(key <= CLASS, nt(q, z_ref[j, :, group_cols(g, 1)]), NEG)
            a = softmax(s)
            a_ref[j, g] = a
            o = head_select(nn(a, z_ref[j, :, group_cols(g, 2)])).astype(BF)
            o_ref[j, :, g * GW : (g + 1) * GW] = o
    y = nn(o_ref[...].reshape(STEP, WIDTH), wo_ref[...]) + vec_ref[5:6]
    x_ref[...] = (full + y).reshape(FPS, ROWS, WIDTH)
    for j in range(FPS):
        at = j * ROWS + CLASS - CLASS % 8
        cls_ref[j] = y[at : at + 8]


def mlp_kernel(
    x_ref, cls_ref, p_ref, g_ref, vec_ref, b_ref, wi_ref, wo_ref,
    out_ref, h_ref, act_ref, dpre_ref, dx_ref, gv_ref, gb_ref,
):
    slices = wi_ref.shape[0]
    step = pl.program_id(0)

    @pl.when(step == 0)
    def _():
        gv_ref[...] = jnp.zeros_like(gv_ref)
        gb_ref[...] = jnp.zeros_like(gb_ref)

    mean_cls = jnp.mean(cls_ref[:, CLASS % 8, :], axis=0, keepdims=True)
    first = p_ref[0, CLASS % TILE : CLASS % TILE + 1, :].astype(F32) + mean_cls
    row = lax.broadcasted_iota(jnp.int32, (STEP, WIDTH), 0) % ROWS
    x = jnp.where(row == CLASS, first, x_ref[...].reshape(STEP, WIDTH))
    g = g_ref[...].reshape(STEP, WIDTH)
    xhat, scale = normed(x)
    h = (xhat * vec_ref[6:7] + vec_ref[7:8]).astype(BF)
    h_ref[...] = h.reshape(FPS, ROWS, WIDTH)
    out = x + vec_ref[8:9]
    dh = jnp.zeros((STEP, WIDTH), F32)
    for s in range(slices):
        cols = slice(s * WIDTH, (s + 1) * WIDTH)
        pre = nn(h, wi_ref[s]) + b_ref[:, cols]
        cdf = 0.5 + 0.5 * lax.erf(pre * (0.5**0.5))
        act = (pre * cdf).astype(BF)
        slope = cdf + pre * (jnp.exp(-0.5 * pre * pre) * 0.3989422804014327)
        act_ref[:, :, cols] = act.reshape(FPS, ROWS, WIDTH)
        dpre = (nt(g, wo_ref[s]) * slope).astype(BF)
        dpre_ref[:, :, cols] = dpre.reshape(FPS, ROWS, WIDTH)
        gb_ref[0:1, cols] += colsum(dpre)
        out = out + nn(act, wo_ref[s])
        dh = dh + nt(dpre, wi_ref[s])
    out_ref[...] = out.astype(BF).reshape(FPS, ROWS, WIDTH)
    gf = g.astype(F32)
    dx_ref[...] = (gf + norm_back(dh, xhat, scale, vec_ref[6:7])).reshape(FPS, ROWS, WIDTH)
    gv_ref[0:1] += colsum(dh * xhat)
    gv_ref[1:2] += colsum(dh)
    gv_ref[2:3] += colsum(gf)


def space_back_kernel(
    dx_ref, dcls_ref, full_ref, z_ref, a_ref, vec_ref, wo_ref, w_ref, wt_ref,
    dy_ref, dz_ref, df_ref, dyt_ref, dot_ref, gv_ref, do_ref,
):
    step = pl.program_id(0)

    @pl.when(step == 0)
    def _():
        gv_ref[...] = jnp.zeros_like(gv_ref)

    dx = dx_ref[...].reshape(STEP, WIDTH)
    row = lax.broadcasted_iota(jnp.int32, (STEP, WIDTH), 0) % ROWS
    dcls = dcls_ref[0, CLASS % 8 : CLASS % 8 + 1, :] * (1.0 / FRAMES)
    dy = jnp.where(row == CLASS, dcls, jnp.where(row < CLASS, dx, 0.0)).astype(BF)
    dy_ref[...] = dy.reshape(FPS, ROWS, WIDTH)
    gv_ref[0:1, :WIDTH] += colsum(dy)
    do_ref[...] = nt(dy, wo_ref[...]).astype(BF)
    for j in range(FPS):
        for g in range(GROUPS):
            a = a_ref[j, g]
            q = head_masked(z_ref[j, :, group_cols(g, 0)])
            k = z_ref[j, :, group_cols(g, 1)]
            do = head_masked(do_ref[j * ROWS : (j + 1) * ROWS, g * GW : (g + 1) * GW])
            da = nt(do, z_ref[j, :, group_cols(g, 2)])
            af = a.astype(F32)
            ds = (af * (da - jnp.sum(af * da, axis=-1, keepdims=True))).astype(BF)
            dz_ref[j, :, group_cols(g, 0)] = (head_select(nn(ds, k)) * HEAD_DIM**-0.5).astype(BF)
            dz_ref[j, :, group_cols(g, 1)] = tn(ds, q).astype(BF)
            dz_ref[j, :, group_cols(g, 2)] = tn(a, do).astype(BF)
    dz = dz_ref[...].reshape(STEP, 3 * WIDTH)
    gv_ref[1:2, :] += colsum(dz)
    dh = nt(dz, w_ref[...])
    xhat, scale = normed(full_ref[...].reshape(STEP, WIDTH))
    gv_ref[2:3, :WIDTH] += colsum(dh * xhat)
    gv_ref[3:4, :WIDTH] += colsum(dh)
    df = dx + norm_back(dh, xhat, scale, vec_ref[3:4])
    df_ref[...] = df.reshape(FPS, ROWS, WIDTH)
    dyt = jnp.where(row < CLASS, df, 0.0).astype(BF)
    dyt_ref[...] = dyt.reshape(FPS, ROWS, WIDTH)
    gv_ref[4:5, :WIDTH] += colsum(dyt)
    dot_ref[...] = nt(dyt, wt_ref[...]).astype(BF).reshape(FPS, ROWS, WIDTH)


def time_back_kernel(z_ref, a_ref, do_ref, dz_ref):
    z = z_ref[...].reshape(FRAMES * TILE, 3 * WIDTH)
    dot = do_ref[...].reshape(FRAMES * TILE, WIDTH)
    for g in range(GROUPS):
        a = a_ref[0, g]
        q = head_masked(z[:, group_cols(g, 0)])
        do = head_masked(dot[:, g * GW : (g + 1) * GW])
        da = nt(do, z[:, group_cols(g, 2)])
        af = a.astype(F32)
        ds = (af * (da - jnp.sum(af * da, axis=-1, keepdims=True))).astype(BF)
        dq = head_select(nn(ds, z[:, group_cols(g, 1)])) * HEAD_DIM**-0.5
        for which, v in enumerate((dq, tn(ds, q), tn(a, do))):
            dz_ref[:, :, group_cols(g, which)] = v.astype(BF).reshape(FRAMES, TILE, GW)


def time_out_kernel(dz_ref, p_ref, df_ref, vec_ref, w_ref, dp_ref, gv_ref):
    step = pl.program_id(0)

    @pl.when(step == 0)
    def _():
        gv_ref[...] = jnp.zeros_like(gv_ref)

    dz = dz_ref[...].reshape(STEP, 3 * WIDTH)
    gv_ref[0:1, :] += colsum(dz)
    dh = nt(dz, w_ref[...])
    xhat, scale = normed(p_ref[...].reshape(STEP, WIDTH).astype(F32))
    gv_ref[1:2, :WIDTH] += colsum(dh * xhat)
    gv_ref[2:3, :WIDTH] += colsum(dh)
    dp = df_ref[...].reshape(STEP, WIDTH) + norm_back(dh, xhat, scale, vec_ref[0:1])
    dp_ref[...] = dp.reshape(FPS, ROWS, WIDTH)


def weight_grad(a, b, name, tile):
    rows, width = a.shape
    out_width = b.shape[1]

    def kernel(a_ref, b_ref, o_ref):
        o_ref[...] = tn(a_ref[...], b_ref[...]).astype(BF)

    return call(
        kernel,
        name,
        (width // tile,),
        [pl.BlockSpec((rows, tile), lambda i: (0, i)), whole(rows, out_width)],
        [(pl.BlockSpec((tile, out_width), lambda i: (i, 0)), jax.ShapeDtypeStruct((width, out_width), BF))],
        flops=2 * rows * width * out_width,
        nbytes=2 * (rows * width + rows * out_width + width * out_width),
    )(a, b)[0]


def unpad(padded, first):
    body = padded[:, :PATCHES].reshape(FRAMES * PATCHES, WIDTH)
    return jnp.concatenate([first, body], axis=0)[None]


def local(
    video_clips, time_gain, time_shift, time_qkv, time_bias, time_proj, time_offset,
    space_gain, space_shift, space_qkv, space_bias, space_proj, space_offset,
    mlp_gain, mlp_shift, fc_in, in_bias, fc_out, out_bias, cotangent,
):
    slices = lax.axis_size("narrow")
    hidden = slices * WIDTH
    tokens = video_clips.shape[1]
    clip = video_clips[0]
    cot = cotangent[0]
    vec = jnp.stack(
        [time_gain, time_shift, time_offset, space_gain, space_shift, space_offset, mlp_gain, mlp_shift, out_bias]
    ).astype(F32)
    nvec = vec.shape[0]
    t_bias = time_bias.astype(F32)
    s_bias = space_bias.astype(F32)
    wi = lax.all_gather(fc_in, "narrow", axis=0)
    wo = lax.all_gather(fc_out, "narrow", axis=0)
    b_in = lax.all_gather(in_bias.astype(F32), "narrow", axis=0, tiled=True)[None]

    chunks = ROWS // TILE
    a_time = (pl.BlockSpec((1, GROUPS, GROUP * FRAMES * TILE, FRAMES * TILE), lambda i: (i, 0, 0, 0)),
              jax.ShapeDtypeStruct((chunks, GROUPS, GROUP * FRAMES * TILE, FRAMES * TILE), BF))
    a_space = (pl.BlockSpec((FPS, GROUPS, GROUP * ROWS, ROWS), lambda i: (i, 0, 0, 0)),
               jax.ShapeDtypeStruct((FRAMES, GROUPS, GROUP * ROWS, ROWS), BF))

    def chunk(width):
        return pl.BlockSpec((FRAMES, TILE, width), lambda i: (0, i, 0))

    def chunk_out(width):
        return chunk(width), jax.ShapeDtypeStruct((FRAMES, ROWS, width), BF)

    rows = FRAMES * ROWS
    steps = (FRAMES // FPS,)
    p, g, ht, zt = call(
        time_in_kernel, "time_in", steps,
        [whole(tokens, WIDTH), whole(tokens, WIDTH), whole(nvec, WIDTH), whole(2, WIDTH), whole(WIDTH, 3 * WIDTH)],
        [frames_out(WIDTH, BF), frames_out(WIDTH, BF), frames_out(WIDTH, BF), frames_out(3 * WIDTH, BF)],
        flops=6 * rows * WIDTH * WIDTH, nbytes=24 * 2**20,
    )(clip, cot, vec, t_bias, time_qkv)
    ot, at = call(
        time_attention_kernel, "time_attention", (chunks,),
        [chunk(3 * WIDTH)], [chunk_out(WIDTH), a_time],
        flops=10**10, nbytes=16 * 2**20,
    )(zt)
    full, hs, zs, a_s, o_s, xs, ycls = call(
        space_kernel, "space", steps,
        [frames(WIDTH), frames(WIDTH), whole(nvec, WIDTH), whole(2, WIDTH),
         whole(WIDTH, WIDTH), whole(WIDTH, 3 * WIDTH), whole(WIDTH, WIDTH)],
        [frames_out(WIDTH, F32), frames_out(WIDTH, BF), frames_out(3 * WIDTH, BF), a_space,
         frames_out(WIDTH, BF), frames_out(WIDTH, F32),
         (pl.BlockSpec((FPS, 8, WIDTH), lambda i: (i, 0, 0)), jax.ShapeDtypeStruct((FRAMES, 8, WIDTH), F32))],
        flops=3 * 10**10, nbytes=40 * 2**20,
    )(p, ot, vec, s_bias, time_proj, space_qkv, space_proj)
    out, hm, act, dpre, dxs, gv_m, gb_m = call(
        mlp_kernel, "mlp", steps,
        [frames(WIDTH), whole(FRAMES, 8, WIDTH),
         pl.BlockSpec((1, TILE, WIDTH), lambda i: (0, CLASS // TILE, 0)), frames(WIDTH),
         whole(nvec, WIDTH), whole(1, hidden), whole(slices, WIDTH, WIDTH), whole(slices, WIDTH, WIDTH)],
        [frames_out(WIDTH, BF), frames_out(WIDTH, BF), frames_out(hidden, BF), frames_out(hidden, BF),
         frames_out(WIDTH, F32),
         (whole(8, WIDTH), jax.ShapeDtypeStruct((8, WIDTH), F32)),
         (whole(8, hidden), jax.ShapeDtypeStruct((8, hidden), F32))],
        flops=8 * rows * WIDTH * hidden, nbytes=50 * 2**20,
    )(xs, ycls, p, g, vec, b_in, wi, wo)
    g_fc_in = weight_grad(hm.reshape(rows, WIDTH), dpre.reshape(rows, hidden), "grad_fc_in", 256)
    g_fc_out = weight_grad(g.reshape(rows, WIDTH), act.reshape(rows, hidden), "grad_fc_out", 256)
    dys, dzs, df, dyt, dot, gv_s = call(
        space_back_kernel, "space_back", steps,
        [frames(WIDTH), pl.BlockSpec((1, 8, WIDTH), lambda i: (0, CLASS // 8, 0)), frames(WIDTH),
         frames(3 * WIDTH), a_space[0], whole(nvec, WIDTH),
         whole(WIDTH, WIDTH), whole(WIDTH, 3 * WIDTH), whole(WIDTH, WIDTH)],
        [frames_out(WIDTH, BF), frames_out(3 * WIDTH, BF), frames_out(WIDTH, F32),
         frames_out(WIDTH, BF), frames_out(WIDTH, BF),
         (whole(8, 3 * WIDTH), jax.ShapeDtypeStruct((8, 3 * WIDTH), F32))],
        scratch=[pltpu.VMEM((STEP, WIDTH), BF)],
        flops=3 * 10**10, nbytes=50 * 2**20,
    )(dxs, dxs, full, zs, a_s, vec, space_proj, space_qkv, time_proj)
    g_s_proj = weight_grad(o_s.reshape(rows, WIDTH), dys.reshape(rows, WIDTH), "grad_space_proj", 384)
    g_s_qkv = weight_grad(dzs.reshape(rows, 3 * WIDTH), hs.reshape(rows, WIDTH), "grad_space_qkv", 768)
    dzt, = call(
        time_back_kernel, "time_back", (chunks,),
        [chunk(3 * WIDTH), a_time[0], chunk(WIDTH)], [chunk_out(3 * WIDTH)],
        flops=10**10, nbytes=24 * 2**20,
    )(zt, at, dot)
    g_t_proj = weight_grad(ot.reshape(rows, WIDTH), dyt.reshape(rows, WIDTH), "grad_time_proj", 384)
    g_t_qkv = weight_grad(dzt.reshape(rows, 3 * WIDTH), ht.reshape(rows, WIDTH), "grad_time_qkv", 768)
    dp, gv_t = call(
        time_out_kernel, "time_out", steps,
        [frames(3 * WIDTH), frames(WIDTH), frames(WIDTH), whole(nvec, WIDTH), whole(WIDTH, 3 * WIDTH)],
        [frames_out(WIDTH, F32), (whole(8, 3 * WIDTH), jax.ShapeDtypeStruct((8, 3 * WIDTH), F32))],
        flops=6 * rows * WIDTH * WIDTH, nbytes=28 * 2**20,
    )(dzt, p, df, vec, time_qkv)

    layer_out = unpad(out, out[0, CLASS : CLASS + 1])
    grad_clips = unpad(dp, jnp.sum(df[:, CLASS], axis=0, keepdims=True))

    def scatter(grad, swap):
        part = lax.psum_scatter(grad, "wide", scatter_dimension=0, tiled=True)
        part = lax.psum_scatter(part, "narrow", scatter_dimension=1, tiled=True)
        part = part.astype(F32)
        return part.T if swap else part

    vectors = jnp.stack(
        [gv_m[0], gv_m[1], gv_m[2],
         gv_s[0, :WIDTH], gv_s[1, :WIDTH], gv_s[1, 2 * WIDTH :], gv_s[2, :WIDTH], gv_s[3, :WIDTH], gv_s[4, :WIDTH],
         gv_t[0, :WIDTH], gv_t[0, 2 * WIDTH :], gv_t[1, :WIDTH], gv_t[2, :WIDTH]]
    )
    vectors = jnp.concatenate([vectors, gb_m[0].reshape(slices, WIDTH)], axis=0)
    vectors = lax.psum(vectors, ("wide", "narrow"))
    me = lax.axis_index("narrow")
    share = WIDTH // slices
    mine = lax.dynamic_slice(vectors, (0, me * share), (13, share))
    grad_in_bias = lax.dynamic_slice(vectors, (13 + me, 0), (1, WIDTH))[0]
    return (
        layer_out,
        grad_clips,
        mine[11],
        mine[12],
        scatter(g_t_qkv, True),
        mine[9:11],
        scatter(g_t_proj.T, True),
        mine[8],
        mine[6],
        mine[7],
        scatter(g_s_qkv, True),
        mine[4:6],
        scatter(g_s_proj.T, True),
        mine[3],
        mine[0],
        mine[1],
        scatter(g_fc_in, False),
        grad_in_bias,
        scatter(g_fc_out, True),
        mine[2],
    )


def solution(mesh):
    rows = P(("wide", "narrow"), None, None)
    return jax.shard_map(
        local,
        mesh=mesh,
        in_specs=(rows,) + (P(),) * 14 + (P(None, "narrow"), P("narrow"), P("narrow", None), P(), rows),
        out_specs=(
            rows,
            rows,
            P("narrow"),
            P("narrow"),
            P("narrow", "wide"),
            P(None, "narrow"),
            P("narrow", "wide"),
            P("narrow"),
            P("narrow"),
            P("narrow"),
            P("narrow", "wide"),
            P(None, "narrow"),
            P("narrow", "wide"),
            P("narrow"),
            P("narrow"),
            P("narrow"),
            P("wide", "narrow"),
            P("narrow"),
            P("narrow", "wide"),
            P("narrow"),
        ),
        check_vma=False,
    )
```

```python
from functools import partial

import jax
import jax.numpy as jnp
from jax import lax
from jax.experimental import pallas as pl
from jax.experimental.pallas import tpu as pltpu
from jax.sharding import PartitionSpec as P

HEADS = 12
HEAD_DIM = 64
FRAMES = 8
PATCHES = 196
ROWS = 208
CLASS = 196
TILE = 16
WIDTH = 768
GROUP = 4
GW = GROUP * HEAD_DIM
GROUPS = HEADS // GROUP
FPS = 2
STEP = FPS * ROWS
EPSILON = 1e-06
F32 = jnp.float32
BF = jnp.bfloat16
NEG = -1e30
VMEM_LIMIT = 62 * 2**20
CHUNKS = 8


def dg(a, b, ca, cb):
    return lax.dot_general(a, b, (((ca,), (cb,)), ((), ())), preferred_element_type=F32)


def nn(a, b):
    return dg(a, b, 1, 0)


def nt(a, b):
    return dg(a, b, 1, 1)


def tn(a, b):
    return dg(a, b, 0, 0)


def call(kernel, name, grid, ins, outs, scratch=(), flops=0, nbytes=0, remote=None):
    extra = {} if remote is None else dict(collective_id=remote, has_side_effects=True)
    return pl.pallas_call(
        kernel,
        name=name,
        grid=grid,
        in_specs=[s for s in ins],
        out_specs=[s for s, _ in outs],
        out_shape=[t for _, t in outs],
        scratch_shapes=list(scratch),
        compiler_params=pltpu.CompilerParams(vmem_limit_bytes=VMEM_LIMIT, **extra),
        cost_estimate=pl.CostEstimate(flops=flops, bytes_accessed=nbytes, transcendentals=0),
    )


def whole(*shape):
    return pl.BlockSpec(shape, lambda *i: (0,) * len(shape), pipeline_mode=pl.Buffered(1))


def frames(width):
    return pl.BlockSpec((FPS, ROWS, width), lambda i: (i, 0, 0))


def frames_out(width, dtype):
    return frames(width), jax.ShapeDtypeStruct((FRAMES, ROWS, width), dtype)


def normed(v):
    center = v - jnp.mean(v, axis=-1, keepdims=True)
    scale = lax.rsqrt(jnp.mean(center * center, axis=-1, keepdims=True) + EPSILON)
    return center * scale, scale


def norm_back(grad, xhat, scale, gain):
    g = grad * gain
    m1 = jnp.mean(g, axis=-1, keepdims=True)
    m2 = jnp.mean(g * xhat, axis=-1, keepdims=True)
    return scale * (g - m1 - xhat * m2)


def colsum(v):
    return jnp.sum(v.astype(F32), axis=0, keepdims=True)


def head_masked(block):
    lane = lax.broadcasted_iota(jnp.int32, block.shape, 1) // HEAD_DIM
    zero = jnp.zeros_like(block)
    return jnp.concatenate([jnp.where(lane == h, block, zero) for h in range(GROUP)], axis=0)


def head_select(stacked):
    rows = stacked.shape[0] // GROUP
    lane = lax.broadcasted_iota(jnp.int32, (rows, GW), 1) // HEAD_DIM
    out = stacked[:rows]
    for h in range(1, GROUP):
        out = jnp.where(lane == h, stacked[h * rows : (h + 1) * rows], out)
    return out


def softmax(scores):
    e = jnp.exp(scores - jnp.max(scores, axis=-1, keepdims=True))
    return (e * (1.0 / jnp.sum(e, axis=-1, keepdims=True))).astype(BF)


def group_cols(g, which):
    start = which * WIDTH + g * GW
    return slice(start, start + GW)


def hosted():
    return lax.axis_size("wide") == CHUNKS


def own_index():
    return lax.axis_index("wide") if hosted() else jnp.int32(0)


def peer(axis, bit):
    return {axis: jnp.bitwise_xor(lax.axis_index(axis), bit)}


PEERS = (("wide", 1), ("wide", 2), ("wide", 4), ("narrow", 1), ("narrow", 2), ("narrow", 3))


def greet():
    barrier = pltpu.get_barrier_semaphore()
    for axis, bit in PEERS:
        pl.semaphore_signal(barrier, inc=1, device_id=peer(axis, bit), device_id_type=pl.DeviceIdType.MESH)
    pl.semaphore_wait(barrier, len(PEERS))


def send(src, dst, sems, k, axis, bit):
    return pltpu.make_async_remote_copy(
        src_ref=src, dst_ref=dst, send_sem=sems.at[0, k], recv_sem=sems.at[1, k],
        device_id=peer(axis, bit), device_id_type=pl.DeviceIdType.MESH,
    )


def start(copies):
    for c in copies:
        c.start()


def wait(copies):
    for c in copies:
        c.wait()


def plus(a, b):
    return (a.astype(F32) + b.astype(F32)).astype(BF)


class PlaneSum:
    SEMS = 7

    @staticmethod
    def scratch(rows):
        half = rows // 2
        return [
            pltpu.VMEM((4, 2, half, WIDTH), BF),
            pltpu.VMEM((4, 2, half, WIDTH), BF),
            pltpu.VMEM((2, 2, half, WIDTH), BF),
            pltpu.SemaphoreType.DMA((2, PlaneSum.SEMS)),
            pltpu.SemaphoreType.DMA,
        ]

    def __init__(self, own, oth, recv, got, near, sems, own_sem):
        self.own, self.oth, self.recv, self.got, self.near, self.sems = own, oth, recv, got, near, sems
        self.own_sem = own_sem

    def load(self):
        return [pltpu.make_async_copy(self.own, self.got, self.own_sem)]

    def chip(self):
        return [send(self.oth, self.recv, self.sems, 0, "wide", 1)]

    def first(self):
        got, near, sems = self.got, self.near, self.sems
        return [
            send(got.at[1, 0], near.at[0, 0], sems, 1, "wide", 2),
            send(got.at[3, 0], near.at[0, 1], sems, 2, "wide", 2),
            send(got.at[2, 1], near.at[1, 0], sems, 3, "wide", 4),
            send(got.at[3, 1], near.at[1, 1], sems, 4, "wide", 4),
        ]

    def second(self):
        got, recv, sems = self.got, self.recv, self.sems
        return [
            send(got.at[2, 0], recv.at[0, 0], sems, 5, "wide", 4),
            send(got.at[1, 1], recv.at[0, 1], sems, 6, "wide", 2),
        ]

    def stage0(self):
        start(self.load())
        start(self.chip())

    def stage1(self):
        wait(self.load())
        wait(self.chip())

        @pl.loop(0, 4)
        def _(q):
            for h in range(2):
                self.got[q, h] = plus(self.got[q, h], self.recv[q, h])

        start(self.first())

    def stage2(self):
        wait(self.first())
        for q, h, way, i in ((0, 0, 0, 0), (2, 0, 0, 1), (0, 1, 1, 0), (1, 1, 1, 1)):
            self.got[q, h] = plus(self.got[q, h], self.near[way, i])
        start(self.second())

    def stage3(self):
        wait(self.second())
        for h in range(2):
            self.got[0, h] = plus(self.got[0, h], self.recv[0, h])


def halves(piece):
    return piece.reshape(4, 2, -1, WIDTH)


class LineSum:
    def __init__(self, parts, recv, sems):
        self.parts, self.recv, self.sems = parts, recv, sems

    @staticmethod
    def scratch(rows, width):
        return [pltpu.VMEM((3, rows, width), BF), pltpu.SemaphoreType.DMA((2, 3))]

    def copies(self):
        line = lax.axis_index("narrow")
        return [
            send(self.parts.at[jnp.bitwise_xor(line, b)], self.recv.at[b - 1], self.sems, b - 1, "narrow", b)
            for b in (1, 2, 3)
        ]

    def result(self):
        wait(self.copies())
        total = self.parts[lax.axis_index("narrow")].astype(F32)
        for b in range(3):
            total = total + self.recv[b].astype(F32)
        return total


def shifted(src_ref, frame, first_row, class_on):
    start = 1 + frame * PATCHES
    base = jnp.minimum(start // TILE * TILE, src_ref.shape[0] // TILE * TILE - ROWS - TILE)
    base = pl.multiple_of(base, TILE)
    chunk = src_ref[pl.ds(base, ROWS + TILE), :]
    row = lax.broadcasted_iota(jnp.int32, (ROWS, ROWS + TILE), 0)
    col = lax.broadcasted_iota(jnp.int32, (ROWS, ROWS + TILE), 1)
    pick = ((col == row + (start - base)) & (row < PATCHES)).astype(F32).astype(BF)
    got = nn(pick, chunk)
    last = src_ref.shape[0] - 1
    end_row = src_ref[last : last + 1, :].astype(F32)
    tail = got[ROWS - TILE :]
    trow = lax.broadcasted_iota(jnp.int32, tail.shape, 0) + (ROWS - TILE)
    tail = jnp.where((trow == PATCHES - 1) & (frame == FRAMES - 1), end_row, tail)
    tail = jnp.where((trow == CLASS) & class_on, first_row, tail)
    return jnp.concatenate([got[: ROWS - TILE], tail], axis=0)


def time_in_kernel(clip_ref, cot_ref, vec_ref, bias_ref, w_ref, p_ref, g_ref, h_ref, z_ref):
    step = pl.program_id(0)
    parts = []
    for j in range(FPS):
        frame = step * FPS + j
        p = shifted(clip_ref, frame, clip_ref[0:1, :].astype(F32), frame >= 0)
        p_ref[j] = p.astype(BF)
        xhat, _ = normed(p)
        parts.append((xhat * vec_ref[0:1] + vec_ref[1:2]).astype(BF))
        g_ref[j] = shifted(cot_ref, frame, cot_ref[0:1, :].astype(F32), frame == 0).astype(BF)
    h = jnp.concatenate(parts, axis=0)
    h_ref[...] = h.reshape(FPS, ROWS, WIDTH)
    project(h, w_ref, bias_ref, z_ref)


def project(h, w_ref, bias_ref, z_ref):
    for which in range(3):
        cols = slice(which * WIDTH, (which + 1) * WIDTH)
        z = nn(h, w_ref[:, cols])
        if which != 1:
            z = z + bias_ref[which // 2 : which // 2 + 1]
        z = z.astype(BF)
        if which == 0:
            z = z * jnp.asarray(HEAD_DIM**-0.5, BF)
        z_ref[:, :, cols] = z.reshape(FPS, ROWS, WIDTH)


def time_attention_kernel(z_ref, o_ref, a_ref):
    z = z_ref[...].reshape(FRAMES * TILE, 3 * WIDTH)
    row = lax.broadcasted_iota(jnp.int32, (GROUP * FRAMES * TILE, FRAMES * TILE), 0)
    col = lax.broadcasted_iota(jnp.int32, (GROUP * FRAMES * TILE, FRAMES * TILE), 1)
    same = (row % TILE) == (col % TILE)
    for g in range(GROUPS):
        q = head_masked(z[:, group_cols(g, 0)])
        s = jnp.where(same, nt(q, z[:, group_cols(g, 1)]), NEG)
        a = softmax(s)
        a_ref[0, g] = a
        o = head_select(nn(a, z[:, group_cols(g, 2)])).astype(BF)
        o_ref[:, :, g * GW : (g + 1) * GW] = o.reshape(FRAMES, TILE, GW)


def space_kernel(
    p_ref, ot_ref, vec_ref, bias_ref, wt_ref, w_ref, wo_ref,
    full_ref, h_ref, z_ref, a_ref, o_ref, x_ref, cls_ref,
):
    p = p_ref[...].reshape(STEP, WIDTH).astype(F32)
    mixed = p + nn(ot_ref[...].reshape(STEP, WIDTH), wt_ref[...]) + vec_ref[2:3]
    row = lax.broadcasted_iota(jnp.int32, (STEP, WIDTH), 0) % ROWS
    full = jnp.where(row == CLASS, p, mixed)
    full_ref[...] = full.reshape(FPS, ROWS, WIDTH)
    xhat, _ = normed(full)
    h = (xhat * vec_ref[3:4] + vec_ref[4:5]).astype(BF)
    h_ref[...] = h.reshape(FPS, ROWS, WIDTH)
    project(h, w_ref, bias_ref, z_ref)
    key = lax.broadcasted_iota(jnp.int32, (GROUP * ROWS, ROWS), 1)
    for j in range(FPS):
        for g in range(GROUPS):
            q = head_masked(z_ref[j, :, group_cols(g, 0)])
            s = jnp.where(key <= CLASS, nt(q, z_ref[j, :, group_cols(g, 1)]), NEG)
            a = softmax(s)
            a_ref[j, g] = a
            o = head_select(nn(a, z_ref[j, :, group_cols(g, 2)])).astype(BF)
            o_ref[j, :, g * GW : (g + 1) * GW] = o
    y = nn(o_ref[...].reshape(STEP, WIDTH), wo_ref[...]) + vec_ref[5:6]
    x_ref[...] = (full + y).reshape(FPS, ROWS, WIDTH)
    for j in range(FPS):
        at = j * ROWS + CLASS - CLASS % 8
        cls_ref[j] = y[at : at + 8]


def mlp_kernel(first_call, *refs):
    if first_call:
        (x_ref, cls_ref, p_ref, g_ref, vec_ref, win_ref, wout_ref, bin_ref, wa_ref, wb_ref,
         h_ref, acc_ref, dh_ref, own_ref, oth_ref, gv_ref, gb_ref,
         w_buf, bias_buf, h_buf, g_buf, act_buf, dpre_buf, t_buf, sem) = refs
    else:
        (x_ref, cls_ref, p_ref, g_ref, vec_ref, h_ref, acc_ref, dh_ref, wa_ref, wb_ref, wc_ref, wd_ref,
         *refs) = refs
        refs = list(refs)
        near_refs = [refs.pop(0), refs.pop(0)] if hosted() else None
        out_ref, dx_ref, own_ref, oth_ref, gv_ref, gb_ref = refs[:6]
        refs = refs[6:]
        near_out = refs.pop(0) if hosted() else None
        w_buf, bias_buf, h_buf, g_buf, act_buf, dpre_buf, t_buf, out_buf, sem = refs[:9]
        refs = refs[9:]
    step = pl.program_id(0)
    me = own_index()
    core = lax.rem(lax.axis_index("wide"), 2)
    line = lax.axis_index("narrow")
    swap = jnp.int32(0) if first_call else ((line == 1) | (line == 2)).astype(jnp.int32)
    row_steps = FRAMES // FPS
    if not first_call and hosted():
        plane = PlaneSum(*near_refs, *refs[:5])
        rz, zsem = refs[5:]

        def line_copies():
            return [send(plane.got.at[0, m, pl.ds(96, 96)], rz.at[m], zsem, m, "narrow", 1) for m in range(2)]

        def near_total():
            wait(line_copies())
            for m in range(2):
                near_out[m] = plane.got[0, m, 0:96].astype(F32) + rz[m].astype(F32)

        def line_stage():
            plane.stage3()
            start(line_copies())

        plan = {1: plane.stage1, 3: plane.stage2, 4: line_stage}

        @pl.when(step == 0)
        def _():
            greet()
            plane.stage0()

        for k, action in plan.items():
            pl.when(step == k)(action)

    @pl.when(step == 0)
    def _():
        gv_ref[...] = jnp.zeros_like(gv_ref)
        gb_ref[...] = jnp.zeros_like(gb_ref)

        def fetch(src, dst, k):
            return pltpu.make_async_copy(src, dst, sem.at[k])

        pairs = [(wa_ref, wb_ref)] if first_call else [(wa_ref, wb_ref), (wc_ref, wd_ref)]
        base = 1 if first_call else 0
        for c in range(2):

            @pl.when(core == c)
            def _():
                todo = []
                for i, (mine, sib) in enumerate(pairs):
                    slot = base + i
                    into = (mine, sib) if c == 0 else (sib, mine)
                    for m in range(2):
                        todo.append(fetch(into[m].at[0:WIDTH], w_buf.at[m, slot], len(todo)))
                    todo.append(fetch(mine.at[WIDTH : WIDTH + TILE], bias_buf.at[slot], len(todo)))
                for t in todo:
                    t.start()
                for t in todo:
                    t.wait()

    if first_call:

        def weight(m, slot):
            return (win_ref, wout_ref)[m][...] if slot == 0 else w_buf[m, slot]

        def bias(slot):
            return bin_ref[...] if slot == 0 else bias_buf[slot, 0:1].astype(F32)
    else:

        def weight(m, slot):
            return w_buf[m, slot]

        def bias(slot):
            return bias_buf[slot, 0:1].astype(F32)

    @pl.when(step < row_steps)
    def _():
        at = pl.ds(pl.multiple_of(step * STEP, STEP), STEP)
        x = x_ref[...].reshape(STEP, WIDTH)
        mean_cls = jnp.mean(cls_ref[:, CLASS % 8, :], axis=0, keepdims=True)
        first = p_ref[0, CLASS % TILE : CLASS % TILE + 1, :].astype(F32) + mean_cls
        row = lax.broadcasted_iota(jnp.int32, (STEP, WIDTH), 0) % ROWS
        x = jnp.where(row == CLASS, first, x)
        xhat, scale = normed(x)
        g = g_ref[...].reshape(STEP, WIDTH)
        if first_call:
            h = (xhat * vec_ref[6:7] + vec_ref[7:8]).astype(BF)
            h_ref[...] = h.reshape(FPS, ROWS, WIDTH)
            acc = x + vec_ref[8:9]
            dh = None
        else:
            h = h_ref[...].reshape(STEP, WIDTH)
            acc = acc_ref[...].reshape(STEP, WIDTH)
            dh = dh_ref[...].reshape(STEP, WIDTH)
        h_buf[at, :] = h
        g_buf[at, :] = g
        for s in range(2):
            cols = slice(s * WIDTH, (s + 1) * WIDTH)
            pre = nn(h, weight(0, s)) + bias(s)
            cdf = 0.5 + 0.5 * lax.erf(pre * (0.5**0.5))
            act = (pre * cdf).astype(BF)
            slope = cdf + pre * (jnp.exp(-0.5 * pre * pre) * 0.3989422804014327)
            act_buf[at, cols] = act
            dpre = (nt(g, weight(1, s)) * slope).astype(BF)
            dpre_buf[at, cols] = dpre
            gb_ref[s : s + 1, :] += colsum(dpre)
            acc = acc + nn(act, weight(1, s))
            back = nt(dpre, weight(0, s))
            dh = back if dh is None else dh + back
        if first_call:
            acc_ref[...] = acc.reshape(FPS, ROWS, WIDTH)
            dh_ref[...] = dh.reshape(FPS, ROWS, WIDTH)
        else:
            for k in range(row_steps):

                @pl.when(step == k)
                def _():
                    if k == 0:
                        out_buf[0:1, :] = acc[CLASS : CLASS + 1]
                    for j in range(FPS):
                        start = 1 + (k * FPS + j) * PATCHES
                        out_buf[start : start + PATCHES, :] = acc[j * ROWS : j * ROWS + PATCHES]

            gf = g.astype(F32)
            dx_ref[...] = (gf + norm_back(dh, xhat, scale, vec_ref[6:7])).reshape(FPS, ROWS, WIDTH)
            gv_ref[0:1] += colsum(dh * xhat)
            gv_ref[1:2] += colsum(dh)
            gv_ref[2:3] += colsum(gf)

    def matrix(unit, left_ref, right_ref):
        t_buf[...] = left_ref[...].T
        for s in range(2):
            got = nn(t_buf[...], right_ref[:, s * WIDTH : (s + 1) * WIDTH]).astype(BF)
            for w in range(CHUNKS):
                put_chunk(own_ref, oth_ref, me, w, 2 * unit + jnp.bitwise_xor(s, swap), got[w * 96 : (w + 1) * 96])

    @pl.when(step == row_steps)
    def _():
        matrix(0, h_buf, dpre_buf)
        if not first_call:
            out_ref[0] = out_buf[...].astype(BF)

    @pl.when(step == row_steps + 1)
    def _():
        matrix(1, g_buf, act_buf)
        if not first_call and hosted():
            near_total()


def put_chunk(own_ref, oth_ref, me, w, unit, value):
    rel = jnp.bitwise_xor(me, w)
    place = rel // 2
    for c, ref in enumerate((own_ref, oth_ref)):

        @pl.when(rel % 2 == c)
        def _():
            ref[place, unit] = value


def space_back_kernel(
    dx_ref, dcls_ref, full_ref, z_ref, a_ref, vec_ref, wo_ref, w_ref, wt_ref,
    dy_ref, dz_ref, df_ref, dyt_ref, dot_ref, gv_ref, do_ref,
):
    step = pl.program_id(0)

    @pl.when(step == 0)
    def _():
        gv_ref[...] = jnp.zeros_like(gv_ref)

    dx = dx_ref[...].reshape(STEP, WIDTH)
    row = lax.broadcasted_iota(jnp.int32, (STEP, WIDTH), 0) % ROWS
    dcls = dcls_ref[0, CLASS % 8 : CLASS % 8 + 1, :] * (1.0 / FRAMES)
    dy = jnp.where(row == CLASS, dcls, jnp.where(row < CLASS, dx, 0.0)).astype(BF)
    dy_ref[...] = dy.reshape(FPS, ROWS, WIDTH)
    gv_ref[0:1, :WIDTH] += colsum(dy)
    do_ref[...] = nt(dy, wo_ref[...]).astype(BF)
    for j in range(FPS):
        for g in range(GROUPS):
            a = a_ref[j, g]
            q = head_masked(z_ref[j, :, group_cols(g, 0)])
            k = z_ref[j, :, group_cols(g, 1)]
            do = head_masked(do_ref[j * ROWS : (j + 1) * ROWS, g * GW : (g + 1) * GW])
            da = nt(do, z_ref[j, :, group_cols(g, 2)])
            af = a.astype(F32)
            ds = (af * (da - jnp.sum(af * da, axis=-1, keepdims=True))).astype(BF)
            dz_ref[j, :, group_cols(g, 0)] = (head_select(nn(ds, k)) * HEAD_DIM**-0.5).astype(BF)
            dz_ref[j, :, group_cols(g, 1)] = tn(ds, q).astype(BF)
            dz_ref[j, :, group_cols(g, 2)] = tn(a, do).astype(BF)
    dz = dz_ref[...].reshape(STEP, 3 * WIDTH)
    gv_ref[1:2, :] += colsum(dz)
    dh = nt(dz, w_ref[...])
    xhat, scale = normed(full_ref[...].reshape(STEP, WIDTH))
    gv_ref[2:3, :WIDTH] += colsum(dh * xhat)
    gv_ref[3:4, :WIDTH] += colsum(dh)
    df = dx + norm_back(dh, xhat, scale, vec_ref[3:4])
    df_ref[...] = df.reshape(FPS, ROWS, WIDTH)
    dyt = jnp.where(row < CLASS, df, 0.0).astype(BF)
    dyt_ref[...] = dyt.reshape(FPS, ROWS, WIDTH)
    gv_ref[4:5, :WIDTH] += colsum(dyt)
    dot_ref[...] = nt(dyt, wt_ref[...]).astype(BF).reshape(FPS, ROWS, WIDTH)


def time_back_kernel(z_ref, a_ref, do_ref, dz_ref):
    z = z_ref[...].reshape(FRAMES * TILE, 3 * WIDTH)
    dot = do_ref[...].reshape(FRAMES * TILE, WIDTH)
    for g in range(GROUPS):
        a = a_ref[0, g]
        q = head_masked(z[:, group_cols(g, 0)])
        do = head_masked(dot[:, g * GW : (g + 1) * GW])
        da = nt(do, z[:, group_cols(g, 2)])
        af = a.astype(F32)
        ds = (af * (da - jnp.sum(af * da, axis=-1, keepdims=True))).astype(BF)
        dq = head_select(nn(ds, z[:, group_cols(g, 1)])) * HEAD_DIM**-0.5
        for which, v in enumerate((dq, tn(ds, q), tn(a, do))):
            dz_ref[:, :, group_cols(g, which)] = v.astype(BF).reshape(FRAMES, TILE, GW)


def time_out_kernel(dz_ref, p_ref, df_ref, vec_ref, w_ref, dp_ref, gv_ref):
    step = pl.program_id(0)

    @pl.when(step == 0)
    def _():
        gv_ref[...] = jnp.zeros_like(gv_ref)
        dp_ref[0, 0:1, :] = jnp.zeros((1, WIDTH), F32)

    dz = dz_ref[...].reshape(STEP, 3 * WIDTH)
    gv_ref[0:1, :] += colsum(dz)
    dh = nt(dz, w_ref[...])
    xhat, scale = normed(p_ref[...].reshape(STEP, WIDTH).astype(F32))
    gv_ref[1:2, :WIDTH] += colsum(dh * xhat)
    gv_ref[2:3, :WIDTH] += colsum(dh)
    df = df_ref[...].reshape(STEP, WIDTH)
    dp = df + norm_back(dh, xhat, scale, vec_ref[0:1])
    for j in range(FPS):
        dp_ref[0, 0:1, :] += df[j * ROWS + CLASS : j * ROWS + CLASS + 1]
    for k in range(FRAMES // FPS):

        @pl.when(step == k)
        def _():
            for j in range(FPS):
                start = 1 + (k * FPS + j) * PATCHES
                dp_ref[0, start : start + PATCHES, :] = dp[j * ROWS : j * ROWS + PATCHES]


def pair_grad_kernel(dz_ref, h_ref, dy_ref, o_ref, own_ref, oth_ref):
    step = pl.program_id(0)
    me = lax.axis_index("wide") if lax.axis_size("wide") == CHUNKS else jnp.int32(0)
    half = CHUNKS // 2

    @pl.when(step < 2)
    def _():
        got = tn(dz_ref[...], h_ref[...]).astype(BF)
        for i in range(half):
            w = step * half + i
            put_rows(own_ref, oth_ref, me, w, 0, got[i * 288 : (i + 1) * 288])

    @pl.when(step == 2)
    def _():
        got = tn(dy_ref[...], o_ref[...]).astype(BF)
        for w in range(CHUNKS):
            put_rows(own_ref, oth_ref, me, w, 288, got[w * 96 : (w + 1) * 96])


def put_rows(own_ref, oth_ref, me, w, start, value):
    rel = jnp.bitwise_xor(me, w)
    place = rel // 2
    for c, ref in enumerate((own_ref, oth_ref)):

        @pl.when(rel % 2 == c)
        def _():
            ref[place, start : start + value.shape[0], :] = value


PIECE = (CHUNKS // 2, 384, WIDTH)


def pair_grad(dz, h, dy, o, name):
    rows = FRAMES * ROWS
    return call(
        pair_grad_kernel, name, (3,),
        [pl.BlockSpec((rows, 3 * WIDTH // 2), lambda i: (0, jnp.minimum(i, 1))),
         whole(rows, WIDTH), whole(rows, WIDTH), whole(rows, WIDTH)],
        [(whole(*PIECE), jax.ShapeDtypeStruct(PIECE, BF))] * 2,
    )(dz.reshape(rows, 3 * WIDTH), h.reshape(rows, WIDTH), dy.reshape(rows, WIDTH), o.reshape(rows, WIDTH))


def flip(value, axis, bit):
    return lax.ppermute(value, axis, [(i, i ^ bit) for i in range(lax.axis_size(axis))])


def hop(value, pairs):
    return lax.ppermute(value, "narrow", pairs)


def add(a, b):
    return (a.astype(F32) + b.astype(F32)).astype(BF)


def plane_sum(own, oth):
    got = add(own, flip(oth, "wide", 1))
    half = 192
    rx = flip(jnp.stack([got[1, :half], got[3, :half]]), "wide", 2)
    ry = flip(jnp.stack([got[2, half:], got[3, half:]]), "wide", 4)
    na, ya = add(got[0, :half], rx[0]), add(got[2, :half], rx[1])
    nb, xb = add(got[0, half:], ry[0]), add(got[1, half:], ry[1])
    ra = flip(ya, "wide", 4)
    rb = flip(xb, "wide", 2)
    return jnp.concatenate([add(na, ra), add(nb, rb)])


def unit_sum(own, oth):
    if lax.axis_size("wide") == CHUNKS:
        return plane_sum(own.reshape(PIECE), oth.reshape(PIECE)).reshape(2, 2, 96, WIDTH)
    both = jnp.stack([own, oth], axis=1).reshape(CHUNKS, 4, 96, WIDTH)
    both = both.transpose(1, 0, 2, 3).reshape(4, WIDTH, WIDTH)
    both = lax.psum_scatter(both, "wide", scatter_dimension=1, tiled=True)
    return both.reshape(2, 2, -1, WIDTH)


def pair_sum(own, oth, me):
    if lax.axis_size("wide") == CHUNKS:
        rows = plane_sum(own, oth)
        cut = 288
    else:
        both = jnp.stack([own, oth], axis=1).reshape(CHUNKS, 384, WIDTH)
        first = both[:, :288].reshape(3 * WIDTH, WIDTH)
        second = both[:, 288:].reshape(WIDTH, WIDTH)
        first = lax.psum_scatter(first, "wide", scatter_dimension=0, tiled=True)
        second = lax.psum_scatter(second, "wide", scatter_dimension=0, tiled=True)
        rows = jnp.concatenate([first, second])
        cut = first.shape[0]
    parts = rows.T.reshape(lax.axis_size("narrow"), -1, rows.shape[0])
    total = line_sum(parts, me)
    return total[:, :cut], total[:, cut:]


def line_sum(parts, me):
    total = lax.dynamic_index_in_dim(parts, me, 0, False).astype(F32)
    for bit in (1, 2, 3):
        other = lax.dynamic_index_in_dim(parts, jnp.bitwise_xor(me, bit), 0, False)
        total = total + flip(other, "narrow", bit).astype(F32)
    return total


def local(
    video_clips, time_gain, time_shift, time_qkv, time_bias, time_proj, time_offset,
    space_gain, space_shift, space_qkv, space_bias, space_proj, space_offset,
    mlp_gain, mlp_shift, fc_in, in_bias, fc_out, out_bias, cotangent,
):
    slices = lax.axis_size("narrow")
    tokens = video_clips.shape[1]
    clip = video_clips[0]
    cot = cotangent[0]
    vec = jnp.stack(
        [time_gain, time_shift, time_offset, space_gain, space_shift, space_offset, mlp_gain, mlp_shift, out_bias]
    ).astype(F32)
    nvec = vec.shape[0]
    t_bias = time_bias.astype(F32)
    s_bias = space_bias.astype(F32)
    me_n = lax.axis_index("narrow")
    me_w = lax.axis_index("wide")
    mine = jnp.where(me_w % 2 == 0, fc_in, fc_out)
    bias_rows = jnp.broadcast_to(in_bias[None], (TILE, WIDTH))
    mine = jnp.concatenate([mine, bias_rows], axis=0)
    near = flip(mine, "narrow", 1)
    mid1 = hop(mine, [(1, 2), (2, 1)])
    near_s = flip(near, "wide", 1)
    end1 = hop(mid1, [(1, 0), (2, 3)])
    mid2 = hop(near, [(1, 2), (2, 1)])
    end2 = hop(mid2, [(1, 0), (2, 3)])
    inner = (me_n == 1) | (me_n == 2)
    far1 = jnp.where(inner, mid1, end1)
    far1_s = flip(far1, "wide", 1)
    far2 = jnp.where(inner, mid2, end2)
    far2_s = flip(far2, "wide", 1)

    chunks = ROWS // TILE
    a_time = (pl.BlockSpec((1, GROUPS, GROUP * FRAMES * TILE, FRAMES * TILE), lambda i: (i, 0, 0, 0)),
              jax.ShapeDtypeStruct((chunks, GROUPS, GROUP * FRAMES * TILE, FRAMES * TILE), BF))
    a_space = (pl.BlockSpec((FPS, GROUPS, GROUP * ROWS, ROWS), lambda i: (i, 0, 0, 0)),
               jax.ShapeDtypeStruct((FRAMES, GROUPS, GROUP * ROWS, ROWS), BF))

    def chunk(width):
        return pl.BlockSpec((FRAMES, TILE, width), lambda i: (0, i, 0))

    def chunk_out(width):
        return chunk(width), jax.ShapeDtypeStruct((FRAMES, ROWS, width), BF)

    rows = FRAMES * ROWS
    steps = (FRAMES // FPS,)
    p, g, ht, zt = call(
        time_in_kernel, "time_in", steps,
        [whole(tokens, WIDTH), whole(tokens, WIDTH), whole(nvec, WIDTH), whole(2, WIDTH), whole(WIDTH, 3 * WIDTH)],
        [frames_out(WIDTH, BF), frames_out(WIDTH, BF), frames_out(WIDTH, BF), frames_out(3 * WIDTH, BF)],
        flops=6 * rows * WIDTH * WIDTH, nbytes=24 * 2**20,
    )(clip, cot, vec, t_bias, time_qkv)
    ot, at = call(
        time_attention_kernel, "time_attention", (chunks,),
        [chunk(3 * WIDTH)], [chunk_out(WIDTH), a_time],
        flops=10**10, nbytes=16 * 2**20,
    )(zt)
    full, hs, zs, a_s, o_s, xs, ycls = call(
        space_kernel, "space", steps,
        [frames(WIDTH), frames(WIDTH), whole(nvec, WIDTH), whole(2, WIDTH),
         whole(WIDTH, WIDTH), whole(WIDTH, 3 * WIDTH), whole(WIDTH, WIDTH)],
        [frames_out(WIDTH, F32), frames_out(WIDTH, BF), frames_out(3 * WIDTH, BF), a_space,
         frames_out(WIDTH, BF), frames_out(WIDTH, F32),
         (pl.BlockSpec((FPS, 8, WIDTH), lambda i: (i, 0, 0)), jax.ShapeDtypeStruct((FRAMES, 8, WIDTH), F32))],
        flops=3 * 10**10, nbytes=40 * 2**20,
    )(p, ot, vec, s_bias, time_proj, space_qkv, space_proj)
    any_ref = pl.BlockSpec(memory_space=pl.ANY)
    last = FRAMES // FPS - 1
    row_in = pl.BlockSpec((FPS, ROWS, WIDTH), lambda i: (jnp.minimum(i, last), 0, 0))

    def row_out(dtype):
        return row_in, jax.ShapeDtypeStruct((FRAMES, ROWS, WIDTH), dtype)

    unit_shape = (CHUNKS // 2, 4, 96, WIDTH)
    units = [(whole(*unit_shape), jax.ShapeDtypeStruct(unit_shape, BF))] * 2
    vec_out = [(whole(8, WIDTH), jax.ShapeDtypeStruct((8, WIDTH), F32))] * 2
    bufs = [
        pltpu.VMEM((2, 2, WIDTH, WIDTH), BF), pltpu.VMEM((2, TILE, WIDTH), BF),
        pltpu.VMEM((rows, WIDTH), BF), pltpu.VMEM((rows, WIDTH), BF),
        pltpu.VMEM((rows, 2 * WIDTH), BF), pltpu.VMEM((rows, 2 * WIDTH), BF), pltpu.VMEM((WIDTH, rows), BF),
    ]
    hm, acc, dh, a_own, a_oth, _, gb_a = call(
        partial(mlp_kernel, True), "mlp_near", (last + 3,),
        [row_in, whole(FRAMES, 8, WIDTH),
         pl.BlockSpec((1, TILE, WIDTH), lambda i: (0, CLASS // TILE, 0)), row_in,
         whole(nvec, WIDTH), whole(WIDTH, WIDTH), whole(WIDTH, WIDTH), whole(1, WIDTH), any_ref, any_ref],
        [row_out(BF), row_out(F32), row_out(F32)] + units + vec_out,
        scratch=bufs + [pltpu.SemaphoreType.DMA((8,))],
    )(xs, ycls, p, g, vec, fc_in, fc_out, in_bias.astype(F32)[None], near, near_s)
    units_in = []
    near_out = []
    near_args = []
    near_scratch = []
    if hosted():
        units_in = [any_ref, any_ref]
        near_args = [halves(a_own), halves(a_oth)]
        near_out = [(whole(2, 96, WIDTH), jax.ShapeDtypeStruct((2, 96, WIDTH), F32))]
        near_scratch = PlaneSum.scratch(384) + [pltpu.VMEM((2, 96, WIDTH), BF), pltpu.SemaphoreType.DMA((2, 2))]
    layer_out, dxs, b_own, b_oth, gv_m, gb_b, *near_sum = call(
        partial(mlp_kernel, False), "mlp_far", (last + 3,),
        [row_in, whole(FRAMES, 8, WIDTH),
         pl.BlockSpec((1, TILE, WIDTH), lambda i: (0, CLASS // TILE, 0)), row_in,
         whole(nvec, WIDTH), row_in, row_in, row_in, any_ref, any_ref, any_ref, any_ref] + units_in,
        [(whole(1, tokens, WIDTH), jax.ShapeDtypeStruct((1, tokens, WIDTH), BF)), row_out(F32)] + units + vec_out + near_out,
        scratch=bufs + [pltpu.VMEM((tokens, WIDTH), F32), pltpu.SemaphoreType.DMA((8,))] + near_scratch,
        remote=1 if hosted() else None,
    )(xs, ycls, p, g, vec, hm, acc, dh, far1, far1_s, far2, far2_s, *near_args)
    dys, dzs, df, dyt, dot, gv_s = call(
        space_back_kernel, "space_back", steps,
        [frames(WIDTH), pl.BlockSpec((1, 8, WIDTH), lambda i: (0, CLASS // 8, 0)), frames(WIDTH),
         frames(3 * WIDTH), a_space[0], whole(nvec, WIDTH),
         whole(WIDTH, WIDTH), whole(WIDTH, 3 * WIDTH), whole(WIDTH, WIDTH)],
        [frames_out(WIDTH, BF), frames_out(3 * WIDTH, BF), frames_out(WIDTH, F32),
         frames_out(WIDTH, BF), frames_out(WIDTH, BF),
         (whole(8, 3 * WIDTH), jax.ShapeDtypeStruct((8, 3 * WIDTH), F32))],
        scratch=[pltpu.VMEM((STEP, WIDTH), BF)],
        flops=3 * 10**10, nbytes=50 * 2**20,
    )(dxs, dxs, full, zs, a_s, vec, space_proj, space_qkv, time_proj)
    s_own, s_oth = pair_grad(dzs, hs, dys, o_s, "grad_space")
    dzt, = call(
        time_back_kernel, "time_back", (chunks,),
        [chunk(3 * WIDTH), a_time[0], chunk(WIDTH)], [chunk_out(3 * WIDTH)],
        flops=10**10, nbytes=24 * 2**20,
    )(zt, at, dot)
    t_own, t_oth = pair_grad(dzt, ht, dyt, ot, "grad_time")
    grad_clips, gv_t = call(
        time_out_kernel, "time_out", steps,
        [frames(3 * WIDTH), frames(WIDTH), frames(WIDTH), whole(nvec, WIDTH), whole(WIDTH, 3 * WIDTH)],
        [(whole(1, tokens, WIDTH), jax.ShapeDtypeStruct((1, tokens, WIDTH), F32)),
         (whole(8, 3 * WIDTH), jax.ShapeDtypeStruct((8, 3 * WIDTH), F32))],
        flops=6 * rows * WIDTH * WIDTH, nbytes=28 * 2**20,
    )(dzt, p, df, vec, time_qkv)

    if hosted():
        fc = near_sum[0]
    else:
        near_sum = unit_sum(a_own, a_oth)
        fc = near_sum[:, 0].astype(F32) + flip(near_sum[:, 1], "narrow", 1).astype(F32)
    far_sum = unit_sum(b_own, b_oth)
    fc = fc + flip(far_sum[:, 0], "narrow", 2).astype(F32) + flip(far_sum[:, 1], "narrow", 3).astype(F32)
    s_qkv, s_proj = pair_sum(s_own, s_oth, me_n)
    t_qkv, t_proj = pair_sum(t_own, t_oth, me_n)

    vectors = jnp.stack(
        [gv_m[0], gv_m[1], gv_m[2],
         gv_s[0, :WIDTH], gv_s[1, :WIDTH], gv_s[1, 2 * WIDTH :], gv_s[2, :WIDTH], gv_s[3, :WIDTH], gv_s[4, :WIDTH],
         gv_t[0, :WIDTH], gv_t[0, 2 * WIDTH :], gv_t[1, :WIDTH], gv_t[2, :WIDTH]]
    )
    lower = me_n < 2
    places = (me_n, jnp.bitwise_xor(me_n, 1), jnp.where(lower, 2, 1), jnp.where(lower, 3, 0))
    hidden_rows = jnp.zeros((slices, WIDTH), F32)
    for place, row in zip(places, (gb_a[0], gb_a[1], gb_b[0], gb_b[1])):
        hidden_rows = lax.dynamic_update_slice(hidden_rows, row[None], (place, 0))
    vectors = jnp.concatenate([vectors, hidden_rows], axis=0)
    vectors = lax.psum(vectors, ("wide", "narrow"))
    share = WIDTH // slices
    mine = lax.dynamic_slice(vectors, (0, me_n * share), (13, share))
    grad_in_bias = lax.dynamic_slice(vectors, (13 + me_n, 0), (1, WIDTH))[0]
    return (
        layer_out,
        grad_clips,
        mine[11],
        mine[12],
        t_qkv,
        mine[9:11],
        t_proj,
        mine[8],
        mine[6],
        mine[7],
        s_qkv,
        mine[4:6],
        s_proj,
        mine[3],
        mine[0],
        mine[1],
        fc[0],
        grad_in_bias,
        fc[1].T,
        mine[2],
    )


def solution(mesh):
    rows = P(("wide", "narrow"), None, None)
    return jax.shard_map(
        local,
        mesh=mesh,
        in_specs=(rows,) + (P(),) * 14 + (P(None, "narrow"), P("narrow"), P("narrow", None), P(), rows),
        out_specs=(
            rows,
            rows,
            P("narrow"),
            P("narrow"),
            P("narrow", "wide"),
            P(None, "narrow"),
            P("narrow", "wide"),
            P("narrow"),
            P("narrow"),
            P("narrow"),
            P("narrow", "wide"),
            P(None, "narrow"),
            P("narrow", "wide"),
            P("narrow"),
            P("narrow"),
            P("narrow"),
            P("wide", "narrow"),
            P("narrow"),
            P("narrow", "wide"),
            P("narrow"),
        ),
        check_vma=False,
    )
```

```python
from functools import partial

import jax
import jax.numpy as jnp
from jax import lax
from jax.experimental import pallas as pl
from jax.experimental.pallas import tpu as pltpu
from jax.sharding import PartitionSpec as P

HEADS = 12
HEAD_DIM = 64
FRAMES = 8
PATCHES = 196
ROWS = 208
CLASS = 196
TILE = 16
WIDTH = 768
GROUP = 4
GW = GROUP * HEAD_DIM
GROUPS = HEADS // GROUP
FPS = 2
STEP = FPS * ROWS
EPSILON = 1e-06
F32 = jnp.float32
BF = jnp.bfloat16
NEG = -1e30
VMEM_LIMIT = 62 * 2**20
CHUNKS = 8


def dg(a, b, ca, cb):
    return lax.dot_general(a, b, (((ca,), (cb,)), ((), ())), preferred_element_type=F32)


def nn(a, b):
    return dg(a, b, 1, 0)


def nt(a, b):
    return dg(a, b, 1, 1)


def tn(a, b):
    return dg(a, b, 0, 0)


def call(kernel, name, grid, ins, outs, scratch=(), flops=0, nbytes=0, remote=None):
    extra = {} if remote is None else dict(collective_id=remote, has_side_effects=True)
    return pl.pallas_call(
        kernel,
        name=name,
        grid=grid,
        in_specs=[s for s in ins],
        out_specs=[s for s, _ in outs],
        out_shape=[t for _, t in outs],
        scratch_shapes=list(scratch),
        compiler_params=pltpu.CompilerParams(vmem_limit_bytes=VMEM_LIMIT, **extra),
        cost_estimate=pl.CostEstimate(flops=flops, bytes_accessed=nbytes, transcendentals=0),
    )


def whole(*shape):
    return pl.BlockSpec(shape, lambda *i: (0,) * len(shape), pipeline_mode=pl.Buffered(1))


def frames(width):
    return pl.BlockSpec((FPS, ROWS, width), lambda i: (i, 0, 0))


def frames_out(width, dtype):
    return frames(width), jax.ShapeDtypeStruct((FRAMES, ROWS, width), dtype)


def normed(v):
    center = v - jnp.mean(v, axis=-1, keepdims=True)
    scale = lax.rsqrt(jnp.mean(center * center, axis=-1, keepdims=True) + EPSILON)
    return center * scale, scale


def norm_back(grad, xhat, scale, gain):
    g = grad * gain
    m1 = jnp.mean(g, axis=-1, keepdims=True)
    m2 = jnp.mean(g * xhat, axis=-1, keepdims=True)
    return scale * (g - m1 - xhat * m2)


def colsum(v):
    return jnp.sum(v.astype(F32), axis=0, keepdims=True)


def head_masked(block):
    lane = lax.broadcasted_iota(jnp.int32, block.shape, 1) // HEAD_DIM
    zero = jnp.zeros_like(block)
    return jnp.concatenate([jnp.where(lane == h, block, zero) for h in range(GROUP)], axis=0)


def head_select(stacked):
    rows = stacked.shape[0] // GROUP
    lane = lax.broadcasted_iota(jnp.int32, (rows, GW), 1) // HEAD_DIM
    out = stacked[:rows]
    for h in range(1, GROUP):
        out = jnp.where(lane == h, stacked[h * rows : (h + 1) * rows], out)
    return out


def softmax(scores):
    e = jnp.exp(scores - jnp.max(scores, axis=-1, keepdims=True))
    return (e * (1.0 / jnp.sum(e, axis=-1, keepdims=True))).astype(BF)


def group_cols(g, which):
    start = which * WIDTH + g * GW
    return slice(start, start + GW)


def hosted():
    return lax.axis_size("wide") == CHUNKS


def own_index():
    return lax.axis_index("wide") if hosted() else jnp.int32(0)


def peer(axis, bit):
    return {axis: jnp.bitwise_xor(lax.axis_index(axis), bit)}


RING = (("wide", 1), ("narrow", 1), ("narrow", 3))
PLANE = (("wide", 1), ("wide", 2), ("wide", 4))
LINE = (("narrow", 1), ("narrow", 2), ("narrow", 3))
PEERS = PLANE + LINE


def inner():
    line = lax.axis_index("narrow")
    return (line == 1) | (line == 2)


def greet(peers=PEERS):
    barrier = pltpu.get_barrier_semaphore()
    for axis, bit in peers:
        pl.semaphore_signal(barrier, inc=1, device_id=peer(axis, bit), device_id_type=pl.DeviceIdType.MESH)
    pl.semaphore_wait(barrier, len(peers))


def send(src, dst, sems, k, axis, bit):
    return pltpu.make_async_remote_copy(
        src_ref=src, dst_ref=dst, send_sem=sems.at[0, k], recv_sem=sems.at[1, k],
        device_id=peer(axis, bit), device_id_type=pl.DeviceIdType.MESH,
    )


def start(copies):
    for c in copies:
        c.start()


def wait(copies):
    for c in copies:
        c.wait()


def plus(a, b):
    return a + b


class PlaneSum:
    SEMS = 7

    @staticmethod
    def scratch(rows):
        half = rows // 2
        return [
            pltpu.VMEM((4, 2, half, WIDTH), BF),
            pltpu.VMEM((4, 2, half, WIDTH), BF),
            pltpu.VMEM((2, 2, half, WIDTH), BF),
            pltpu.SemaphoreType.DMA((2, PlaneSum.SEMS)),
            pltpu.SemaphoreType.DMA,
        ]

    def __init__(self, own, oth, recv, got, near, sems, own_sem):
        self.own, self.oth, self.recv, self.got, self.near, self.sems = own, oth, recv, got, near, sems
        self.own_sem = own_sem

    def load(self):
        return [pltpu.make_async_copy(self.own, self.got, self.own_sem)]

    def chip(self):
        return [send(self.oth, self.recv, self.sems, 0, "wide", 1)]

    def first(self):
        got, near, sems = self.got, self.near, self.sems
        return [
            send(got.at[1, 0], near.at[0, 0], sems, 1, "wide", 2),
            send(got.at[3, 0], near.at[0, 1], sems, 2, "wide", 2),
            send(got.at[2, 1], near.at[1, 0], sems, 3, "wide", 4),
            send(got.at[3, 1], near.at[1, 1], sems, 4, "wide", 4),
        ]

    def second(self):
        got, recv, sems = self.got, self.recv, self.sems
        return [
            send(got.at[2, 0], recv.at[0, 0], sems, 5, "wide", 4),
            send(got.at[1, 1], recv.at[0, 1], sems, 6, "wide", 2),
        ]

    def stage0(self):
        start(self.load())
        start(self.chip())

    def stage1(self):
        wait(self.load())
        wait(self.chip())

        @pl.loop(0, 4)
        def _(q):
            for h in range(2):
                self.got[q, h] = plus(self.got[q, h], self.recv[q, h])

        start(self.first())

    def stage2(self):
        wait(self.first())
        for q, h, way, i in ((0, 0, 0, 0), (2, 0, 0, 1), (0, 1, 1, 0), (1, 1, 1, 1)):
            self.got[q, h] = plus(self.got[q, h], self.near[way, i])
        start(self.second())

    def stage3(self):
        wait(self.second())
        for h in range(2):
            self.got[0, h] = plus(self.got[0, h], self.recv[0, h])


def halves(piece):
    return piece.reshape(4, 2, -1, WIDTH)


class LineSum:
    def __init__(self, parts, recv, sems):
        self.parts, self.recv, self.sems = parts, recv, sems

    @staticmethod
    def scratch(rows, width):
        return [pltpu.VMEM((3, rows, width), BF), pltpu.SemaphoreType.DMA((2, 3))]

    def copies(self):
        line = lax.axis_index("narrow")
        return [
            send(self.parts.at[jnp.bitwise_xor(line, b)], self.recv.at[b - 1], self.sems, b - 1, "narrow", b)
            for b in (1, 2, 3)
        ]

    def result(self):
        wait(self.copies())
        total = self.parts[lax.axis_index("narrow")].astype(F32)
        for b in range(3):
            total = total + self.recv[b].astype(F32)
        return total


def shifted(src_ref, frame, first_row, class_on):
    start = 1 + frame * PATCHES
    base = jnp.minimum(start // TILE * TILE, src_ref.shape[0] // TILE * TILE - ROWS - TILE)
    base = pl.multiple_of(base, TILE)
    chunk = src_ref[pl.ds(base, ROWS + TILE), :]
    row = lax.broadcasted_iota(jnp.int32, (ROWS, ROWS + TILE), 0)
    col = lax.broadcasted_iota(jnp.int32, (ROWS, ROWS + TILE), 1)
    pick = ((col == row + (start - base)) & (row < PATCHES)).astype(F32).astype(BF)
    got = nn(pick, chunk)
    last = src_ref.shape[0] - 1
    end_row = src_ref[last : last + 1, :].astype(F32)
    tail = got[ROWS - TILE :]
    trow = lax.broadcasted_iota(jnp.int32, tail.shape, 0) + (ROWS - TILE)
    tail = jnp.where((trow == PATCHES - 1) & (frame == FRAMES - 1), end_row, tail)
    tail = jnp.where((trow == CLASS) & class_on, first_row, tail)
    return jnp.concatenate([got[: ROWS - TILE], tail], axis=0)


def time_kernel(
    clip_ref, cot_ref, vec_ref, bias_ref, w_ref, mine_ref,
    p_ref, g_ref, h_ref, z_ref, o_ref, a_ref, near_ref, mid_ref, sib_ref,
    z_buf, sems,
):
    step = pl.program_id(0)
    row_steps = FRAMES // FPS
    steps = pl.num_programs(0)

    def near():
        return send(mine_ref, near_ref, sems, 0, "narrow", 1)

    def mid():
        return send(mine_ref, mid_ref, sems, 1, "narrow", 3)

    def sibling():
        return send(near_ref, sib_ref, sems, 2, "wide", 1)

    @pl.when(step == 0)
    def _():
        greet(RING)
        near().start()

        @pl.when(inner())
        def _():
            mid().start()

    @pl.when(step < row_steps)
    def _():
        parts = []
        for j in range(FPS):
            frame = step * FPS + j
            p = shifted(clip_ref, frame, clip_ref[0:1, :].astype(F32), frame >= 0)
            p_ref[j] = p.astype(BF)
            xhat, _ = normed(p)
            parts.append((xhat * vec_ref[0:1] + vec_ref[1:2]).astype(BF))
            g_ref[j] = shifted(cot_ref, frame, cot_ref[0:1, :].astype(F32), frame == 0).astype(BF)
        h = jnp.concatenate(parts, axis=0)
        h_ref[...] = h.reshape(FPS, ROWS, WIDTH)
        project(h, w_ref, bias_ref, z_ref)
        z_buf[pl.ds(step * FPS, FPS)] = z_ref[...]

    @pl.when(step >= row_steps)
    def _():
        at = pl.multiple_of((step - row_steps) * TILE, TILE)
        time_attention(z_buf[:, pl.ds(at, TILE), :], o_ref, a_ref)

    @pl.when(step == steps - 3)
    def _():
        near().wait()
        sibling().start()

    @pl.when(step == steps - 1)
    def _():
        sibling().wait()

        @pl.when(inner())
        def _():
            mid().wait()


def project(h, w_ref, bias_ref, z_ref):
    for which in range(3):
        cols = slice(which * WIDTH, (which + 1) * WIDTH)
        z = nn(h, w_ref[:, cols])
        if which != 1:
            z = z + bias_ref[which // 2 : which // 2 + 1]
        z = z.astype(BF)
        if which == 0:
            z = z * jnp.asarray(HEAD_DIM**-0.5, BF)
        z_ref[:, :, cols] = z.reshape(FPS, ROWS, WIDTH)


def time_attention(z, o_ref, a_ref):
    z = z.reshape(FRAMES * TILE, 3 * WIDTH)
    row = lax.broadcasted_iota(jnp.int32, (GROUP * FRAMES * TILE, FRAMES * TILE), 0)
    col = lax.broadcasted_iota(jnp.int32, (GROUP * FRAMES * TILE, FRAMES * TILE), 1)
    same = (row % TILE) == (col % TILE)
    for g in range(GROUPS):
        q = head_masked(z[:, group_cols(g, 0)])
        s = jnp.where(same, nt(q, z[:, group_cols(g, 1)]), NEG)
        a = softmax(s)
        a_ref[0, g] = a
        o = head_select(nn(a, z[:, group_cols(g, 2)])).astype(BF)
        o_ref[:, :, g * GW : (g + 1) * GW] = o.reshape(FRAMES, TILE, GW)


def space_kernel(
    p_ref, ot_ref, vec_ref, bias_ref, wt_ref, w_ref, wo_ref, near_ref, mid_ref,
    full_ref, h_ref, z_ref, a_ref, o_ref, x_ref, cls_ref, end_ref, mid2_ref, sems,
):
    step = pl.program_id(0)

    def end():
        return send(mid_ref, end_ref, sems, 0, "narrow", 1)

    def mid2():
        return send(near_ref, mid2_ref, sems, 1, "narrow", 3)

    @pl.when(step == 0)
    def _():
        greet(RING)

        @pl.when(inner())
        def _():
            end().start()
            mid2().start()

    p = p_ref[...].reshape(STEP, WIDTH).astype(F32)
    mixed = p + nn(ot_ref[...].reshape(STEP, WIDTH), wt_ref[...]) + vec_ref[2:3]
    row = lax.broadcasted_iota(jnp.int32, (STEP, WIDTH), 0) % ROWS
    full = jnp.where(row == CLASS, p, mixed)
    full_ref[...] = full.reshape(FPS, ROWS, WIDTH)
    xhat, _ = normed(full)
    h = (xhat * vec_ref[3:4] + vec_ref[4:5]).astype(BF)
    h_ref[...] = h.reshape(FPS, ROWS, WIDTH)
    project(h, w_ref, bias_ref, z_ref)
    key = lax.broadcasted_iota(jnp.int32, (GROUP * ROWS, ROWS), 1)
    for j in range(FPS):
        for g in range(GROUPS):
            q = head_masked(z_ref[j, :, group_cols(g, 0)])
            s = jnp.where(key <= CLASS, nt(q, z_ref[j, :, group_cols(g, 1)]), NEG)
            a = softmax(s)
            a_ref[j, g] = a
            o = head_select(nn(a, z_ref[j, :, group_cols(g, 2)])).astype(BF)
            o_ref[j, :, g * GW : (g + 1) * GW] = o
    y = nn(o_ref[...].reshape(STEP, WIDTH), wo_ref[...]) + vec_ref[5:6]
    x_ref[...] = (full + y).reshape(FPS, ROWS, WIDTH)
    for j in range(FPS):
        at = j * ROWS + CLASS - CLASS % 8
        cls_ref[j] = y[at : at + 8]

    @pl.when((step == pl.num_programs(0) - 1) & inner())
    def _():
        end().wait_send()
        mid2().wait()

    @pl.when((step == pl.num_programs(0) - 1) & jnp.logical_not(inner()))
    def _():
        end().wait_recv()


def mlp_kernel(first_call, *refs):
    refs = list(refs)

    def take(n):
        got = refs[:n]
        del refs[:n]
        return got

    step = pl.program_id(0)
    me = own_index()
    core = lax.rem(lax.axis_index("wide"), 2)
    row_steps = FRAMES // FPS
    chained = not first_call and hosted()
    x_ref, cls_ref, p_ref, g_ref, vec_ref = take(5)
    if first_call:
        win_ref, wout_ref, bin_ref, near_ref, near_s_ref, mid_ref, end_ref, mid2_ref = take(8)
        h_ref, acc_ref, dh_ref, own_ref, oth_ref, gv_ref, gb_ref, end2_ref, far_s_ref, far2_s_ref = take(10)
        swap = jnp.int32(0)
    else:
        h_ref, acc_ref, dh_ref, mid_ref, end_ref, far_s_ref, mid2_ref, end2_ref, far2_s_ref = take(9)
        near_refs = take(2) if chained else None
        out_ref, dx_ref, own_ref, oth_ref, gv_ref, gb_ref = take(6)
        near_out = take(1)[0] if chained else None
        swap = inner().astype(jnp.int32)
    w_buf, bias_buf, h_buf, g_buf, act_buf, dpre_buf, t_buf, sem = take(8)
    if first_call:
        (rsems,) = take(1)

        def end2():
            return send(mid2_ref, end2_ref, rsems, 0, "narrow", 1)

        def sibling(k, i):
            src = ((end_ref, mid_ref), (end2_ref, mid2_ref))[k][i]
            return send(src, (far_s_ref, far2_s_ref)[k], rsems, 1 + k, "wide", 1)

        def either(k, action):
            for i in range(2):

                @pl.when(inner() == (i == 1))
                def _():
                    action(sibling(k, i))

        @pl.when(step == 0)
        def _():
            greet(RING)

            @pl.when(inner())
            def _():
                end2().start()

            either(0, lambda c: c.start())

        @pl.when(step == row_steps)
        def _():
            @pl.when(inner())
            def _():
                end2().wait_send()

            @pl.when(jnp.logical_not(inner()))
            def _():
                end2().wait_recv()

            either(1, lambda c: c.start())

    else:
        (out_buf,) = take(1)
    if chained:
        plane = PlaneSum(*near_refs, *take(5))
        rz, zsem = take(2)

        def line_copies():
            return [send(plane.got.at[0, m, pl.ds(96, 96)], rz.at[m], zsem, m, "narrow", 1) for m in range(2)]

        def near_total():
            wait(line_copies())
            for m in range(2):
                near_out[m] = plane.got[0, m, 0:96].astype(F32) + rz[m].astype(F32)

        def line_stage():
            plane.stage3()
            start(line_copies())

        plan = {1: plane.stage1, 3: plane.stage2, 4: line_stage}

        @pl.when(step == 0)
        def _():
            greet()
            plane.stage0()

        for k, action in plan.items():
            pl.when(step == k)(action)

    @pl.when(step == 0)
    def _():
        gv_ref[...] = jnp.zeros_like(gv_ref)
        gb_ref[...] = jnp.zeros_like(gb_ref)
        for c in range(2):
            for i in range(2):

                @pl.when((core == c) & (inner() == (i == 1)))
                def _():
                    if first_call:
                        slots = [(1, near_ref, near_s_ref)]
                    else:
                        slots = [(0, (end_ref, mid_ref)[i], far_s_ref), (1, (end2_ref, mid2_ref)[i], far2_s_ref)]
                    todo = []
                    for slot, mine, sib in slots:
                        into = (mine, sib) if c == 0 else (sib, mine)
                        todo += [
                            pltpu.make_async_copy(into[m].at[0:WIDTH], w_buf.at[m, slot], sem.at[3 * slot + m])
                            for m in range(2)
                        ]
                        todo.append(
                            pltpu.make_async_copy(
                                mine.at[WIDTH : WIDTH + TILE], bias_buf.at[slot], sem.at[3 * slot + 2]
                            )
                        )
                    start(todo)
                    wait(todo)

    if first_call:

        def weight(m, slot):
            return (win_ref, wout_ref)[m][...] if slot == 0 else w_buf[m, slot]

        def bias(slot):
            return bin_ref[...] if slot == 0 else bias_buf[slot, 0:1].astype(F32)
    else:

        def weight(m, slot):
            return w_buf[m, slot]

        def bias(slot):
            return bias_buf[slot, 0:1].astype(F32)

    @pl.when(step < row_steps)
    def _():
        at = pl.ds(pl.multiple_of(step * STEP, STEP), STEP)
        x = x_ref[...].reshape(STEP, WIDTH)
        mean_cls = jnp.mean(cls_ref[:, CLASS % 8, :], axis=0, keepdims=True)
        first = p_ref[0, CLASS % TILE : CLASS % TILE + 1, :].astype(F32) + mean_cls
        row = lax.broadcasted_iota(jnp.int32, (STEP, WIDTH), 0) % ROWS
        x = jnp.where(row == CLASS, first, x)
        xhat, scale = normed(x)
        g = g_ref[...].reshape(STEP, WIDTH)
        if first_call:
            h = (xhat * vec_ref[6:7] + vec_ref[7:8]).astype(BF)
            h_ref[...] = h.reshape(FPS, ROWS, WIDTH)
            acc = x + vec_ref[8:9]
            dh = None
        else:
            h = h_ref[...].reshape(STEP, WIDTH)
            acc = acc_ref[...].reshape(STEP, WIDTH)
            dh = dh_ref[...].reshape(STEP, WIDTH)
        h_buf[at, :] = h
        g_buf[at, :] = g
        for s in range(2):
            cols = slice(s * WIDTH, (s + 1) * WIDTH)
            pre = nn(h, weight(0, s)) + bias(s)
            cdf = 0.5 + 0.5 * lax.erf(pre * (0.5**0.5))
            act = (pre * cdf).astype(BF)
            slope = cdf + pre * (jnp.exp(-0.5 * pre * pre) * 0.3989422804014327)
            act_buf[at, cols] = act
            dpre = (nt(g, weight(1, s)) * slope).astype(BF)
            dpre_buf[at, cols] = dpre
            gb_ref[s : s + 1, :] += colsum(dpre)
            acc = acc + nn(act, weight(1, s))
            back = nt(dpre, weight(0, s))
            dh = back if dh is None else dh + back
        if first_call:
            acc_ref[...] = acc.reshape(FPS, ROWS, WIDTH)
            dh_ref[...] = dh.reshape(FPS, ROWS, WIDTH)
        else:
            for k in range(row_steps):

                @pl.when(step == k)
                def _():
                    if k == 0:
                        out_buf[0:1, :] = acc[CLASS : CLASS + 1]
                    for j in range(FPS):
                        start = 1 + (k * FPS + j) * PATCHES
                        out_buf[start : start + PATCHES, :] = acc[j * ROWS : j * ROWS + PATCHES]

            gf = g.astype(F32)
            dx_ref[...] = (gf + norm_back(dh, xhat, scale, vec_ref[6:7])).reshape(FPS, ROWS, WIDTH)
            gv_ref[0:1] += colsum(dh * xhat)
            gv_ref[1:2] += colsum(dh)
            gv_ref[2:3] += colsum(gf)

    def matrix(unit, left_ref, right_ref):
        t_buf[...] = left_ref[...].T
        for s in range(2):
            got = nn(t_buf[...], right_ref[:, s * WIDTH : (s + 1) * WIDTH]).astype(BF)
            for w in range(CHUNKS):
                put_chunk(own_ref, oth_ref, me, w, 2 * unit + jnp.bitwise_xor(s, swap), got[w * 96 : (w + 1) * 96])

    @pl.when(step == row_steps)
    def _():
        matrix(0, h_buf, dpre_buf)
        if not first_call:
            out_ref[0] = out_buf[...].astype(BF)

    @pl.when(step == row_steps + 1)
    def _():
        matrix(1, g_buf, act_buf)
        if chained:
            near_total()
        if first_call:
            either(0, lambda c: c.wait())
            either(1, lambda c: c.wait())


def put_chunk(own_ref, oth_ref, me, w, unit, value):
    rel = jnp.bitwise_xor(me, w)
    place = rel // 2
    for c, ref in enumerate((own_ref, oth_ref)):

        @pl.when(rel % 2 == c)
        def _():
            ref[place, unit] = value


def space_back_kernel(*refs):
    refs = list(refs)

    def take(n):
        got = refs[:n]
        del refs[:n]
        return got

    dx_ref, dcls_ref, full_ref, z_ref, a_ref, vec_ref, wo_ref, w_ref, wt_ref = take(9)
    far_refs = take(2) if hosted() else None
    dy_ref, dz_ref, df_ref, dyt_ref, dot_ref, gv_ref = take(6)
    far_out = take(1)[0] if hosted() else None
    (do_ref,) = take(1)
    step = pl.program_id(0)
    plane = PlaneSum(*far_refs, *take(5)) if hosted() else None

    def begin():
        greet(PLANE)
        plane.stage0()

    def finish():
        plane.stage3()
        far_out[...] = plane.got[0]

    def checkpoint(j):
        if hosted():
            plan = {0: begin, FPS: plane.stage1, 2 * FPS + 1: plane.stage2, 4 * FPS: finish}
            for k, action in plan.items():
                if k % FPS == j % FPS and (j < FPS) == (k < 4 * FPS):
                    pl.when(step == (k - j) // FPS)(action)

    checkpoint(0)

    @pl.when(step == 0)
    def _():
        gv_ref[...] = jnp.zeros_like(gv_ref)

    dx = dx_ref[...].reshape(STEP, WIDTH)
    row = lax.broadcasted_iota(jnp.int32, (STEP, WIDTH), 0) % ROWS
    dcls = dcls_ref[0, CLASS % 8 : CLASS % 8 + 1, :] * (1.0 / FRAMES)
    dy = jnp.where(row == CLASS, dcls, jnp.where(row < CLASS, dx, 0.0)).astype(BF)
    dy_ref[...] = dy.reshape(FPS, ROWS, WIDTH)
    gv_ref[0:1, :WIDTH] += colsum(dy)
    do_ref[...] = nt(dy, wo_ref[...]).astype(BF)
    for j in range(FPS):
        if j > 0:
            checkpoint(j)
        for g in range(GROUPS):
            a = a_ref[j, g]
            q = head_masked(z_ref[j, :, group_cols(g, 0)])
            k = z_ref[j, :, group_cols(g, 1)]
            do = head_masked(do_ref[j * ROWS : (j + 1) * ROWS, g * GW : (g + 1) * GW])
            da = nt(do, z_ref[j, :, group_cols(g, 2)])
            af = a.astype(F32)
            ds = (af * (da - jnp.sum(af * da, axis=-1, keepdims=True))).astype(BF)
            dz_ref[j, :, group_cols(g, 0)] = (head_select(nn(ds, k)) * HEAD_DIM**-0.5).astype(BF)
            dz_ref[j, :, group_cols(g, 1)] = tn(ds, q).astype(BF)
            dz_ref[j, :, group_cols(g, 2)] = tn(a, do).astype(BF)
    dz = dz_ref[...].reshape(STEP, 3 * WIDTH)
    gv_ref[1:2, :] += colsum(dz)
    dh = nt(dz, w_ref[...])
    xhat, scale = normed(full_ref[...].reshape(STEP, WIDTH))
    gv_ref[2:3, :WIDTH] += colsum(dh * xhat)
    gv_ref[3:4, :WIDTH] += colsum(dh)
    df = dx + norm_back(dh, xhat, scale, vec_ref[3:4])
    df_ref[...] = df.reshape(FPS, ROWS, WIDTH)
    dyt = jnp.where(row < CLASS, df, 0.0).astype(BF)
    dyt_ref[...] = dyt.reshape(FPS, ROWS, WIDTH)
    gv_ref[4:5, :WIDTH] += colsum(dyt)
    dot_ref[...] = nt(dyt, wt_ref[...]).astype(BF).reshape(FPS, ROWS, WIDTH)
    checkpoint(FPS)


def space_grad_kernel(*refs):
    refs = list(refs)

    def take(n):
        got = refs[:n]
        del refs[:n]
        return got

    dz_ref, h_ref, dy_ref, o_ref, dyt_ref, ot_ref = take(6)
    near_ref, far_ref = take(2) if hosted() else (None, None)
    own_ref, oth_ref = take(2)
    fc_ref = take(1)[0] if hosted() else None
    step = pl.program_id(0)
    me = own_index()
    half = CHUNKS // 2
    if hosted():
        rz, zsem = take(2)

        def line_copies():
            return [
                send(far_ref.at[m, pl.ds(96 * i, 96)], rz.at[m, i], zsem, 2 * m + i, "narrow", 2 + i)
                for m in range(2) for i in range(2)
            ]

        @pl.when(step == 0)
        def _():
            greet(LINE)
            start(line_copies())

    @pl.when(step < 2)
    def _():
        got = tn(dz_ref[...], h_ref[...]).astype(BF)
        for i in range(half):
            w = step * half + i
            put_rows(own_ref, oth_ref, me, w, 0, got[i * 288 : (i + 1) * 288])

    for k, left, right in ((2, dy_ref, o_ref), (3, dyt_ref, ot_ref)):

        @pl.when(step == k)
        def _():
            got = tn(left[...], right[...]).astype(BF)
            for w in range(CHUNKS):
                put_rows(own_ref, oth_ref, me, w, 96 * (k + 1), got[w * 96 : (w + 1) * 96])

    if hosted():

        @pl.when(step == 3)
        def _():
            wait(line_copies())
            for m in range(2):
                fc_ref[m] = near_ref[m] + rz[m, 0].astype(F32) + rz[m, 1].astype(F32)


def put_rows(own_ref, oth_ref, me, w, start, value):
    rel = jnp.bitwise_xor(me, w)
    place = rel // 2
    for c, ref in enumerate((own_ref, oth_ref)):

        @pl.when(rel % 2 == c)
        def _():
            ref[place, start : start + value.shape[0], :] = value


PIECE = (CHUNKS // 2, 384, WIDTH)
SPACE_ROWS = 480
TIME_ROWS = 288


def time_back_kernel(*refs):
    refs = list(refs)

    def take(n):
        got = refs[:n]
        del refs[:n]
        return got

    z_ref, a_ref, do_ref, h_any = take(4)
    space_refs = take(2) if hosted() else None
    dz_ref, own_ref, oth_ref = take(3)
    parts_ref = take(1)[0] if hosted() else None
    dz_buf, h_buf, h_sem = take(3)
    step = pl.program_id(0)
    chunks = ROWS // TILE
    me = own_index()

    def load():
        return pltpu.make_async_copy(h_any, h_buf, h_sem)

    if hosted():
        plane = PlaneSum(*space_refs, *take(5))
        pad = take(1)[0]

        @pl.when(step == 0)
        def _():
            greet(PLANE)
            plane.stage0()

        pl.when(step == 5)(plane.stage1)
        pl.when(step == chunks + 1)(plane.stage2)

    pl.when(step == 0)(lambda: load().start())

    @pl.when(step < chunks)
    def _():
        z = z_ref[...].reshape(FRAMES * TILE, 3 * WIDTH)
        dot = do_ref[...].reshape(FRAMES * TILE, WIDTH)
        for g in range(GROUPS):
            a = a_ref[0, g]
            q = head_masked(z[:, group_cols(g, 0)])
            do = head_masked(dot[:, g * GW : (g + 1) * GW])
            da = nt(do, z[:, group_cols(g, 2)])
            af = a.astype(F32)
            ds = (af * (da - jnp.sum(af * da, axis=-1, keepdims=True))).astype(BF)
            dq = head_select(nn(ds, z[:, group_cols(g, 1)])) * HEAD_DIM**-0.5
            for which, v in enumerate((dq, tn(ds, q), tn(a, do))):
                dz_ref[:, :, group_cols(g, which)] = v.astype(BF).reshape(FRAMES, TILE, GW)
        dz_buf[:, pl.ds(pl.multiple_of(step * TILE, TILE), TILE), :] = dz_ref[...]

    pl.when(step == chunks)(lambda: load().wait())
    half = CHUNKS // 2
    for k in range(2):

        @pl.when(step == chunks + k)
        def _():
            left = dz_buf[:, :, k * half * 288 : (k + 1) * half * 288]
            got = tn(left.reshape(FRAMES * ROWS, half * 288), h_buf[...]).astype(BF)
            for i in range(half):
                put_rows(own_ref, oth_ref, me, k * half + i, 0, got[i * 288 : (i + 1) * 288])

    if hosted():

        @pl.when(step == chunks + 1)
        def _():
            plane.stage3()
            transposed(plane.got, pad, parts_ref)


def transposed(got, pad, parts_ref):
    half = got.shape[2]
    for h in range(2):
        pad[h * half : (h + 1) * half, :] = got[0, h]
    rest = pad.shape[0] - 2 * half
    pad[2 * half :, :] = jnp.zeros((rest, WIDTH), BF)
    cols = pad[...].T
    size = WIDTH // parts_ref.shape[0]
    for n in range(parts_ref.shape[0]):
        parts_ref[n] = cols[n * size : (n + 1) * size]


VEC_ROWS = 24


def time_out_kernel(*refs):
    refs = list(refs)

    def take(n):
        got = refs[:n]
        del refs[:n]
        return got

    dz_ref, p_ref, df_ref, vec_ref, w_ref = take(5)
    if hosted():
        time_refs = take(2)
        s_parts, gvm_ref, gvs_ref, gba_ref, gbb_ref = take(5)
    dp_ref, gv_ref = take(2)
    step = pl.program_id(0)
    row_steps = FRAMES // FPS
    line = lax.axis_index("narrow")
    if hosted():
        sq_ref, sp_ref, tp_ref, tq_ref, share_ref, hid_ref = take(6)
        plane = PlaneSum(*time_refs, *take(5))
        pad, parts = take(2)
        s_line = LineSum(s_parts, *take(2))
        t_line = LineSum(parts, *take(2))
        vbuf, vrecv, vsem = take(3)

        @pl.when(step == 0)
        def _():
            greet()
            plane.stage0()
            start(s_line.copies())

        pl.when(step == 2)(plane.stage1)

    @pl.when(step == 0)
    def _():
        gv_ref[...] = jnp.zeros_like(gv_ref)
        dp_ref[0:1, 0, :] = jnp.zeros((1, WIDTH), F32)

    @pl.when(step < row_steps)
    def _():
        dz = dz_ref[...].reshape(STEP, 3 * WIDTH)
        gv_ref[0:1, :] += colsum(dz)
        dh = nt(dz, w_ref[...])
        xhat, scale = normed(p_ref[...].reshape(STEP, WIDTH).astype(F32))
        gv_ref[1:2, :WIDTH] += colsum(dh * xhat)
        gv_ref[2:3, :WIDTH] += colsum(dh)
        df = df_ref[...].reshape(STEP, WIDTH)
        dp = df + norm_back(dh, xhat, scale, vec_ref[0:1])
        for j in range(FPS):
            dp_ref[0:1, 0, :] += df[j * ROWS + CLASS : j * ROWS + CLASS + 1]
        for k in range(row_steps):

            @pl.when(step == k)
            def _():
                for j in range(FPS):
                    begin = 1 + (k * FPS + j) * PATCHES
                    dp_ref[begin : begin + PATCHES, 0, :] = dp[j * ROWS : j * ROWS + PATCHES]

    if hosted():

        @pl.when(step == row_steps)
        def _():
            vbuf[...] = jnp.zeros_like(vbuf)
            vbuf[0:3, :] = gvm_ref[0:3, :]
            for i, r, c in ((3, 0, 0), (4, 1, 0), (5, 1, 2), (6, 2, 0), (7, 3, 0), (8, 4, 0)):
                vbuf[i : i + 1, :] = gvs_ref[r : r + 1, c * WIDTH : (c + 1) * WIDTH]
            for i, r, c in ((9, 0, 0), (10, 0, 2), (11, 1, 0), (12, 2, 0)):
                vbuf[i : i + 1, :] = gv_ref[r : r + 1, c * WIDTH : (c + 1) * WIDTH]
            low = line < 2
            places = (line, jnp.bitwise_xor(line, 1), jnp.where(low, 2, 1), jnp.where(low, 3, 0))
            for place, (ref, r) in zip(places, ((gba_ref, 0), (gba_ref, 1), (gbb_ref, 0), (gbb_ref, 1))):
                vbuf[pl.ds(13 + place, 1), :] = ref[r : r + 1, :]

            def exchange(k, axis, bit):
                return send(vbuf, vrecv.at[k], vsem, k, axis, bit)

            def added(k, axis, bit):
                exchange(k, axis, bit).wait()
                vbuf[...] += vrecv[k]

            exchange(0, "wide", 1).start()
            plane.stage2()
            added(0, "wide", 1)
            exchange(1, "wide", 2).start()
            added(1, "wide", 2)
            exchange(2, "wide", 4).start()
            added(2, "wide", 4)
            for b in (1, 2, 3):
                exchange(2 + b, "narrow", b).start()
            plane.stage3()
            transposed(plane.got, pad, parts)
            start(t_line.copies())
            total = s_line.result()
            sq_ref[...] = total[:, :288]
            sp_ref[...] = total[:, 288:384]
            tp_ref[...] = total[:, 384:480]
            for b in (1, 2, 3):
                exchange(2 + b, "narrow", b).wait()
            vectors = vbuf[...] + vrecv[3] + vrecv[4] + vrecv[5]
            size = WIDTH // 4
            share = vectors[:, :size]
            hidden = vectors[13:14, :]
            for n in range(1, 4):
                share = jnp.where(line == n, vectors[:, n * size : (n + 1) * size], share)
                hidden = jnp.where(line == n, vectors[13 + n : 14 + n, :], hidden)
            share_ref[...] = share
            hid_ref[...] = hidden
            tq_ref[...] = t_line.result()[:, :288]


def flip(value, axis, bit):
    return lax.ppermute(value, axis, [(i, i ^ bit) for i in range(lax.axis_size(axis))])


def unit_sum(own, oth):
    both = jnp.stack([own, oth], axis=1).reshape(CHUNKS, 4, 96, WIDTH)
    both = both.transpose(1, 0, 2, 3).reshape(4, WIDTH, WIDTH)
    both = lax.psum_scatter(both, "wide", scatter_dimension=1, tiled=True)
    return both.reshape(2, 2, -1, WIDTH)


def piece_sum(own, oth, sizes, me):
    both = jnp.stack([own, oth], axis=1).reshape(CHUNKS, -1, WIDTH)
    found, at = [], 0
    for size in sizes:
        rows = both[:, at * 96 : (at + size) * 96].reshape(size * WIDTH, WIDTH)
        at += size
        rows = lax.psum_scatter(rows, "wide", scatter_dimension=0, tiled=True)
        parts = rows.T.reshape(lax.axis_size("narrow"), -1, rows.shape[0])
        found.append(line_sum(parts, me))
    return found


def line_sum(parts, me):
    total = lax.dynamic_index_in_dim(parts, me, 0, False).astype(F32)
    for bit in (1, 2, 3):
        other = lax.dynamic_index_in_dim(parts, jnp.bitwise_xor(me, bit), 0, False)
        total = total + flip(other, "narrow", bit).astype(F32)
    return total


def local(
    video_clips, time_gain, time_shift, time_qkv, time_bias, time_proj, time_offset,
    space_gain, space_shift, space_qkv, space_bias, space_proj, space_offset,
    mlp_gain, mlp_shift, fc_in, in_bias, fc_out, out_bias, cotangent,
):
    slices = lax.axis_size("narrow")
    tokens = video_clips.shape[1]
    clip = video_clips[0]
    cot = cotangent[0]
    vec = jnp.stack(
        [time_gain, time_shift, time_offset, space_gain, space_shift, space_offset, mlp_gain, mlp_shift, out_bias]
    ).astype(F32)
    nvec = vec.shape[0]
    t_bias = time_bias.astype(F32)
    s_bias = space_bias.astype(F32)
    me_n = lax.axis_index("narrow")
    me_w = lax.axis_index("wide")
    mine = jnp.where(me_w % 2 == 0, fc_in, fc_out)
    mine = jnp.concatenate([mine, jnp.broadcast_to(in_bias[None], (TILE, WIDTH))], axis=0)
    any_ref = pl.BlockSpec(memory_space=pl.ANY)
    message = (any_ref, jax.ShapeDtypeStruct((WIDTH + TILE, WIDTH), BF))

    chunks = ROWS // TILE
    a_time = jax.ShapeDtypeStruct((chunks, GROUPS, GROUP * FRAMES * TILE, FRAMES * TILE), BF)

    def a_chunk(first):
        return pl.BlockSpec((1, *a_time.shape[1:]), lambda i: (jnp.clip(i - first, 0, chunks - 1), 0, 0, 0))

    a_space = (pl.BlockSpec((FPS, GROUPS, GROUP * ROWS, ROWS), lambda i: (i, 0, 0, 0)),
               jax.ShapeDtypeStruct((FRAMES, GROUPS, GROUP * ROWS, ROWS), BF))

    last = FRAMES // FPS - 1
    steps = last + 1
    rows = FRAMES * ROWS

    def row_in(width):
        return pl.BlockSpec((FPS, ROWS, width), lambda i: (jnp.minimum(i, last), 0, 0))

    def row_out(width, dtype):
        return row_in(width), jax.ShapeDtypeStruct((FRAMES, ROWS, width), dtype)

    def chunk(width, first):
        return pl.BlockSpec((FRAMES, TILE, width), lambda i: (0, jnp.clip(i - first, 0, chunks - 1), 0))

    def chunk_out(width, first):
        return chunk(width, first), jax.ShapeDtypeStruct((FRAMES, ROWS, width), BF)

    p, g, ht, zt, ot, at, near, mid, near_s = call(
        time_kernel, "time", (steps + chunks,),
        [whole(tokens, WIDTH), whole(tokens, WIDTH), whole(nvec, WIDTH), whole(2, WIDTH), whole(WIDTH, 3 * WIDTH),
         any_ref],
        [row_out(WIDTH, BF), row_out(WIDTH, BF), row_out(WIDTH, BF), row_out(3 * WIDTH, BF),
         chunk_out(WIDTH, steps), (a_chunk(steps), a_time)] + [message] * 3,
        scratch=[pltpu.VMEM((FRAMES, ROWS, 3 * WIDTH), BF), pltpu.SemaphoreType.DMA((2, 3))],
        remote=1,
    )(clip, cot, vec, t_bias, time_qkv, mine)
    full, hs, zs, a_s, o_s, xs, ycls, end, mid2 = call(
        space_kernel, "space", (steps,),
        [frames(WIDTH), frames(WIDTH), whole(nvec, WIDTH), whole(2, WIDTH),
         whole(WIDTH, WIDTH), whole(WIDTH, 3 * WIDTH), whole(WIDTH, WIDTH), any_ref, any_ref],
        [frames_out(WIDTH, F32), frames_out(WIDTH, BF), frames_out(3 * WIDTH, BF), a_space,
         frames_out(WIDTH, BF), frames_out(WIDTH, F32),
         (pl.BlockSpec((FPS, 8, WIDTH), lambda i: (i, 0, 0)), jax.ShapeDtypeStruct((FRAMES, 8, WIDTH), F32))]
        + [message] * 2,
        scratch=[pltpu.SemaphoreType.DMA((2, 2))],
        remote=2,
    )(p, ot, vec, s_bias, time_proj, space_qkv, space_proj, near, mid)
    unit_shape = (CHUNKS // 2, 4, 96, WIDTH)
    units = [(whole(*unit_shape), jax.ShapeDtypeStruct(unit_shape, BF))] * 2
    vec_out = [(whole(8, WIDTH), jax.ShapeDtypeStruct((8, WIDTH), F32))] * 2
    bufs = [
        pltpu.VMEM((2, 2, WIDTH, WIDTH), BF), pltpu.VMEM((2, TILE, WIDTH), BF),
        pltpu.VMEM((rows, WIDTH), BF), pltpu.VMEM((rows, WIDTH), BF),
        pltpu.VMEM((rows, 2 * WIDTH), BF), pltpu.VMEM((rows, 2 * WIDTH), BF), pltpu.VMEM((WIDTH, rows), BF),
        pltpu.SemaphoreType.DMA((6,)),
    ]
    mlp_in = [row_in(WIDTH), whole(FRAMES, 8, WIDTH),
              pl.BlockSpec((1, TILE, WIDTH), lambda i: (0, CLASS // TILE, 0)), row_in(WIDTH), whole(nvec, WIDTH)]
    hm, acc, dh, a_own, a_oth, _, gb_a, end2, far_s, far2_s = call(
        partial(mlp_kernel, True), "mlp_near", (last + 3,),
        mlp_in + [whole(WIDTH, WIDTH), whole(WIDTH, WIDTH), whole(1, WIDTH)] + [any_ref] * 5,
        [row_out(WIDTH, BF), row_out(WIDTH, F32), row_out(WIDTH, F32)] + units + vec_out + [message] * 3,
        scratch=bufs + [pltpu.SemaphoreType.DMA((2, 3))],
        remote=3,
    )(xs, ycls, p, g, vec, fc_in, fc_out, in_bias.astype(F32)[None], near, near_s, mid, end, mid2)
    units_in = []
    near_out = []
    near_args = []
    near_scratch = []
    if hosted():
        units_in = [any_ref] * 2
        near_args = [halves(a_own), halves(a_oth)]
        near_out = [(whole(2, 96, WIDTH), jax.ShapeDtypeStruct((2, 96, WIDTH), F32))]
        near_scratch = PlaneSum.scratch(384) + [pltpu.VMEM((2, 96, WIDTH), BF), pltpu.SemaphoreType.DMA((2, 2))]
    layer_out, dxs, b_own, b_oth, gv_m, gb_b, *near_sum = call(
        partial(mlp_kernel, False), "mlp_far", (last + 3,),
        mlp_in + [row_in(WIDTH), row_in(WIDTH), row_in(WIDTH)] + [any_ref] * 6 + units_in,
        [(whole(1, tokens, WIDTH), jax.ShapeDtypeStruct((1, tokens, WIDTH), BF)), row_out(WIDTH, F32)]
        + units + vec_out + near_out,
        scratch=bufs + [pltpu.VMEM((tokens, WIDTH), F32)] + near_scratch,
        remote=4 if hosted() else None,
    )(xs, ycls, p, g, vec, hm, acc, dh, mid, end, far_s, mid2, end2, far2_s, *near_args)

    far_in, far_args, far_out, far_scratch = [], [], [], []
    if hosted():
        far_in = [any_ref] * 2
        far_args = [halves(b_own), halves(b_oth)]
        far_out = [(whole(2, 192, WIDTH), jax.ShapeDtypeStruct((2, 192, WIDTH), BF))]
        far_scratch = PlaneSum.scratch(384)
    dys, dzs, df, dyt, dot, gv_s, *far_sum = call(
        space_back_kernel, "space_back", (steps,),
        [frames(WIDTH), pl.BlockSpec((1, 8, WIDTH), lambda i: (0, CLASS // 8, 0)), frames(WIDTH),
         frames(3 * WIDTH), a_space[0], whole(nvec, WIDTH),
         whole(WIDTH, WIDTH), whole(WIDTH, 3 * WIDTH), whole(WIDTH, WIDTH)] + far_in,
        [frames_out(WIDTH, BF), frames_out(3 * WIDTH, BF), frames_out(WIDTH, F32),
         frames_out(WIDTH, BF), frames_out(WIDTH, BF),
         (whole(8, 3 * WIDTH), jax.ShapeDtypeStruct((8, 3 * WIDTH), F32))] + far_out,
        scratch=[pltpu.VMEM((STEP, WIDTH), BF)] + far_scratch,
        remote=5 if hosted() else None,
    )(dxs, dxs, full, zs, a_s, vec, space_proj, space_qkv, time_proj, *far_args)

    def flat(value):
        return value.reshape(rows, value.shape[-1])

    piece = (CHUNKS // 2, SPACE_ROWS, WIDTH)
    line_in, line_args, line_out, line_scratch = [], [], [], []
    if hosted():
        line_in = [whole(2, 96, WIDTH), any_ref]
        line_args = [near_sum[0], far_sum[0]]
        line_out = [(whole(2, 96, WIDTH), jax.ShapeDtypeStruct((2, 96, WIDTH), F32))]
        line_scratch = [pltpu.VMEM((2, 2, 96, WIDTH), BF), pltpu.SemaphoreType.DMA((2, 4))]
    s_own, s_oth, *fc_sum = call(
        space_grad_kernel, "space_grad", (4,),
        [pl.BlockSpec((rows, 3 * WIDTH // 2), lambda i: (0, jnp.minimum(i, 1)))] + [whole(rows, WIDTH)] * 5 + line_in,
        [(whole(*piece), jax.ShapeDtypeStruct(piece, BF))] * 2 + line_out,
        scratch=line_scratch,
        remote=6 if hosted() else None,
    )(flat(dzs), flat(hs), flat(dys), flat(o_s), flat(dyt), flat(ot), *line_args)

    t_piece = (CHUNKS // 2, TIME_ROWS, WIDTH)
    share = WIDTH // slices
    back_in, back_args, back_out, back_scratch = [], [], [], []
    if hosted():
        back_in = [any_ref] * 2
        back_args = [halves(s_own), halves(s_oth)]
        back_out = [(whole(slices, share, 512), jax.ShapeDtypeStruct((slices, share, 512), BF))]
        back_scratch = PlaneSum.scratch(SPACE_ROWS) + [pltpu.VMEM((512, WIDTH), BF)]
    dzt, t_own, t_oth, *s_parts = call(
        time_back_kernel, "time_back", (chunks + 2,),
        [chunk(3 * WIDTH, 0), a_chunk(0), chunk(WIDTH, 0), any_ref] + back_in,
        [chunk_out(3 * WIDTH, 0)] + [(whole(*t_piece), jax.ShapeDtypeStruct(t_piece, BF))] * 2 + back_out,
        scratch=[pltpu.VMEM((FRAMES, ROWS, 3 * WIDTH), BF), pltpu.VMEM((rows, WIDTH), BF), pltpu.SemaphoreType.DMA]
        + back_scratch,
        remote=7 if hosted() else None,
    )(zt, at, dot, flat(ht), *back_args)

    out_in, out_args, out_out, out_scratch = [], [], [], []
    if hosted():
        out_in = [any_ref] * 2 + [whole(slices, share, 512), whole(8, WIDTH), whole(8, 3 * WIDTH)] + [whole(8, WIDTH)] * 2
        out_args = [halves(t_own), halves(t_oth), s_parts[0], gv_m, gv_s, gb_a, gb_b]
        out_out = [
            (whole(*shape), jax.ShapeDtypeStruct(shape, F32))
            for shape in ((share, 288), (share, 96), (share, 96), (share, 288), (VEC_ROWS, share), (1, WIDTH))
        ]
        out_scratch = (
            PlaneSum.scratch(TIME_ROWS)
            + [pltpu.VMEM((384, WIDTH), BF), pltpu.VMEM((slices, share, 384), BF)]
            + LineSum.scratch(share, 512) + LineSum.scratch(share, 384)
            + [pltpu.VMEM((VEC_ROWS, WIDTH), F32), pltpu.VMEM((6, VEC_ROWS, WIDTH), F32), pltpu.SemaphoreType.DMA((2, 6))]
        )
    grad_clips, gv_t, *sums = call(
        time_out_kernel, "time_out", (steps + (1 if hosted() else 0),),
        [row_in(3 * WIDTH), row_in(WIDTH), row_in(WIDTH), whole(nvec, WIDTH), whole(WIDTH, 3 * WIDTH)] + out_in,
        [(whole(tokens, 1, WIDTH), jax.ShapeDtypeStruct((tokens, 1, WIDTH), F32)),
         (whole(8, 3 * WIDTH), jax.ShapeDtypeStruct((8, 3 * WIDTH), F32))] + out_out,
        scratch=out_scratch,
        remote=8 if hosted() else None,
    )(dzt, p, df, vec, time_qkv, *out_args)
    grad_clips = grad_clips.reshape(1, tokens, WIDTH)

    if hosted():
        fc = fc_sum[0]
        s_qkv, s_proj, t_proj, t_qkv, mine, grad_in_bias = sums
        grad_in_bias = grad_in_bias[0]
    else:
        near_part = unit_sum(a_own, a_oth)
        far_part = unit_sum(b_own, b_oth)
        fc = near_part[:, 0].astype(F32) + flip(near_part[:, 1], "narrow", 1).astype(F32)
        fc = fc + flip(far_part[:, 0], "narrow", 2).astype(F32) + flip(far_part[:, 1], "narrow", 3).astype(F32)
        s_qkv, s_proj, t_proj = piece_sum(s_own, s_oth, (3, 1, 1), me_n)
        (t_qkv,) = piece_sum(t_own, t_oth, (3,), me_n)
        vectors = jnp.concatenate(
            [gv_m[0:3], gv_s[0:1, :WIDTH], gv_s[1:2, :WIDTH], gv_s[1:2, 2 * WIDTH :], gv_s[2:5, :WIDTH],
             gv_t[0:1, :WIDTH], gv_t[0:1, 2 * WIDTH :], gv_t[1:3, :WIDTH]]
        )
        lower = me_n < 2
        places = (me_n, jnp.bitwise_xor(me_n, 1), jnp.where(lower, 2, 1), jnp.where(lower, 3, 0))
        hidden_rows = jnp.zeros((slices, WIDTH), F32)
        for place, row in zip(places, (gb_a[0], gb_a[1], gb_b[0], gb_b[1])):
            hidden_rows = lax.dynamic_update_slice(hidden_rows, row[None], (place, 0))
        vectors = lax.psum(jnp.concatenate([vectors, hidden_rows], axis=0), ("wide", "narrow"))
        mine = lax.dynamic_slice(vectors, (0, me_n * share), (13, share))
        grad_in_bias = lax.dynamic_slice(vectors, (13 + me_n, 0), (1, WIDTH))[0]
    return (
        layer_out,
        grad_clips,
        mine[11],
        mine[12],
        t_qkv,
        mine[9:11],
        t_proj,
        mine[8],
        mine[6],
        mine[7],
        s_qkv,
        mine[4:6],
        s_proj,
        mine[3],
        mine[0],
        mine[1],
        fc[0],
        grad_in_bias,
        fc[1].T,
        mine[2],
    )


def solution(mesh):
    rows = P(("wide", "narrow"), None, None)
    return jax.shard_map(
        local,
        mesh=mesh,
        in_specs=(rows,) + (P(),) * 14 + (P(None, "narrow"), P("narrow"), P("narrow", None), P(), rows),
        out_specs=(
            rows,
            rows,
            P("narrow"),
            P("narrow"),
            P("narrow", "wide"),
            P(None, "narrow"),
            P("narrow", "wide"),
            P("narrow"),
            P("narrow"),
            P("narrow"),
            P("narrow", "wide"),
            P(None, "narrow"),
            P("narrow", "wide"),
            P("narrow"),
            P("narrow"),
            P("narrow"),
            P("wide", "narrow"),
            P("narrow"),
            P("narrow", "wide"),
            P("narrow"),
        ),
        check_vma=False,
    )
```

```python
from functools import partial

import jax
import jax.numpy as jnp
from jax import lax
from jax.experimental import pallas as pl
from jax.experimental.pallas import tpu as pltpu
from jax.sharding import PartitionSpec as P

HEADS = 12
HEAD_DIM = 64
FRAMES = 8
PATCHES = 196
ROWS = 208
CLASS = 196
TILE = 16
WIDTH = 768
GROUP = 4
GW = GROUP * HEAD_DIM
GROUPS = HEADS // GROUP
FPS = 2
STEP = FPS * ROWS
EPSILON = 1e-06
F32 = jnp.float32
BF = jnp.bfloat16
NEG = -1e30
VMEM_LIMIT = 62 * 2**20
CHUNKS = 8


def dg(a, b, ca, cb):
    return lax.dot_general(a, b, (((ca,), (cb,)), ((), ())), preferred_element_type=F32)


def nn(a, b):
    return dg(a, b, 1, 0)


def nt(a, b):
    return dg(a, b, 1, 1)


def tn(a, b):
    return dg(a, b, 0, 0)


def call(kernel, name, grid, ins, outs, scratch=(), flops=0, nbytes=0, remote=None):
    extra = {} if remote is None else dict(collective_id=remote, has_side_effects=True)
    return pl.pallas_call(
        kernel,
        name=name,
        grid=grid,
        in_specs=[s for s in ins],
        out_specs=[s for s, _ in outs],
        out_shape=[t for _, t in outs],
        scratch_shapes=list(scratch),
        compiler_params=pltpu.CompilerParams(vmem_limit_bytes=VMEM_LIMIT, **extra),
        cost_estimate=pl.CostEstimate(flops=flops, bytes_accessed=nbytes, transcendentals=0),
    )


def whole(*shape):
    return pl.BlockSpec(shape, lambda *i: (0,) * len(shape), pipeline_mode=pl.Buffered(1))


def frames(width):
    return pl.BlockSpec((FPS, ROWS, width), lambda i: (i, 0, 0))


def frames_out(width, dtype):
    return frames(width), jax.ShapeDtypeStruct((FRAMES, ROWS, width), dtype)


def row_of(ref):
    return ref[...].astype(F32).reshape(1, ref.shape[0])


def normed(v):
    center = v - jnp.mean(v, axis=-1, keepdims=True)
    scale = lax.rsqrt(jnp.mean(center * center, axis=-1, keepdims=True) + EPSILON)
    return center * scale, scale


def norm_back(grad, xhat, scale, gain):
    g = grad * gain
    m1 = jnp.mean(g, axis=-1, keepdims=True)
    m2 = jnp.mean(g * xhat, axis=-1, keepdims=True)
    return scale * (g - m1 - xhat * m2)


def colsum(v):
    return jnp.sum(v.astype(F32), axis=0, keepdims=True)


def head_masked(block):
    lane = lax.broadcasted_iota(jnp.int32, block.shape, 1) // HEAD_DIM
    zero = jnp.zeros_like(block)
    return jnp.concatenate([jnp.where(lane == h, block, zero) for h in range(GROUP)], axis=0)


def head_select(stacked):
    rows = stacked.shape[0] // GROUP
    lane = lax.broadcasted_iota(jnp.int32, (rows, GW), 1) // HEAD_DIM
    out = stacked[:rows]
    for h in range(1, GROUP):
        out = jnp.where(lane == h, stacked[h * rows : (h + 1) * rows], out)
    return out


def softmax(scores):
    e = jnp.exp(scores - jnp.max(scores, axis=-1, keepdims=True))
    return (e * (1.0 / jnp.sum(e, axis=-1, keepdims=True))).astype(BF)


def score_back(a, da):
    af = a.astype(F32)
    return (af * (da - jnp.sum(af * da, axis=-1, keepdims=True))).astype(BF)


def group_cols(g, which):
    start = which * WIDTH + g * GW
    return slice(start, start + GW)


def hosted():
    return lax.axis_size("wide") == CHUNKS


def own_index():
    return lax.axis_index("wide") if hosted() else jnp.int32(0)


def peer(axis, bit):
    return {axis: jnp.bitwise_xor(lax.axis_index(axis), bit)}


RING = (("wide", 1), ("wide", 2), ("narrow", 1), ("narrow", 3))
RING_ALL = RING + (("narrow", 2),)
PLANE = (("wide", 1), ("wide", 2), ("wide", 4))
LINE = (("narrow", 1), ("narrow", 2), ("narrow", 3))
PEERS = PLANE + LINE


def inner():
    line = lax.axis_index("narrow")
    return (line == 1) | (line == 2)


def greet(peers=PEERS):
    barrier = pltpu.get_barrier_semaphore()
    for axis, bit in peers:
        pl.semaphore_signal(barrier, inc=1, device_id=peer(axis, bit), device_id_type=pl.DeviceIdType.MESH)
    pl.semaphore_wait(barrier, len(peers))


def half_rows():
    size = WIDTH // 2
    return pl.ds(pl.multiple_of(lax.rem(lax.axis_index("wide") // 2, 2) * size, size), size)


def send(src, dst, sems, k, axis, bit):
    return pltpu.make_async_remote_copy(
        src_ref=src, dst_ref=dst, send_sem=sems.at[0, k], recv_sem=sems.at[1, k],
        device_id=peer(axis, bit), device_id_type=pl.DeviceIdType.MESH,
    )


def start(copies):
    for c in copies:
        c.start()


def wait(copies):
    for c in copies:
        c.wait()


def plus(a, b):
    return a + b


class PlaneSum:
    SEMS = 7

    @staticmethod
    def scratch(rows):
        half = rows // 2
        return [
            pltpu.VMEM((4, 2, half, WIDTH), BF),
            pltpu.VMEM((4, 2, half, WIDTH), BF),
            pltpu.VMEM((2, 2, half, WIDTH), BF),
            pltpu.SemaphoreType.DMA((2, PlaneSum.SEMS)),
            pltpu.SemaphoreType.DMA,
        ]

    def __init__(self, own, oth, recv, got, near, sems, own_sem):
        self.own, self.oth, self.recv, self.got, self.near, self.sems = own, oth, recv, got, near, sems
        self.own_sem = own_sem

    def load(self):
        return [pltpu.make_async_copy(self.own, self.got, self.own_sem)]

    def chip(self):
        return [send(self.oth, self.recv, self.sems, 0, "wide", 1)]

    def first(self):
        got, near, sems = self.got, self.near, self.sems
        return [
            send(got.at[1, 0], near.at[0, 0], sems, 1, "wide", 2),
            send(got.at[3, 0], near.at[0, 1], sems, 2, "wide", 2),
            send(got.at[2, 1], near.at[1, 0], sems, 3, "wide", 4),
            send(got.at[3, 1], near.at[1, 1], sems, 4, "wide", 4),
        ]

    def second(self):
        got, recv, sems = self.got, self.recv, self.sems
        return [
            send(got.at[2, 0], recv.at[0, 0], sems, 5, "wide", 4),
            send(got.at[1, 1], recv.at[0, 1], sems, 6, "wide", 2),
        ]

    def load_both(self):
        return self.load() + [pltpu.make_async_copy(self.oth, self.recv, self.sems.at[0, 0])]

    def stage0(self):
        start(self.load())
        start(self.chip())

    def arrived(self):
        wait(self.load_both())
        self.sum_chip()

    def stage1(self):
        wait(self.load())
        wait(self.chip())
        self.sum_chip()

    def sum_chip(self):
        @pl.loop(0, 4)
        def _(q):
            for h in range(2):
                self.got[q, h] = plus(self.got[q, h], self.recv[q, h])

        start(self.first())

    def stage2(self):
        wait(self.first())
        for q, h, way, i in ((0, 0, 0, 0), (2, 0, 0, 1), (0, 1, 1, 0), (1, 1, 1, 1)):
            self.got[q, h] = plus(self.got[q, h], self.near[way, i])
        start(self.second())

    def stage3(self):
        wait(self.second())
        for h in range(2):
            self.got[0, h] = plus(self.got[0, h], self.recv[0, h])


def halves(piece):
    return piece.reshape(4, 2, -1, WIDTH)


class LineSum:
    def __init__(self, parts, recv, sems):
        self.parts, self.recv, self.sems = parts, recv, sems

    @staticmethod
    def scratch(rows, width):
        return [pltpu.VMEM((3, rows, width), BF), pltpu.SemaphoreType.DMA((2, 3))]

    def copies(self):
        line = lax.axis_index("narrow")
        return [
            send(self.parts.at[jnp.bitwise_xor(line, b)], self.recv.at[b - 1], self.sems, b - 1, "narrow", b)
            for b in (1, 2, 3)
        ]

    def result(self):
        wait(self.copies())
        total = self.parts[lax.axis_index("narrow")].astype(F32)
        for b in range(3):
            total = total + self.recv[b].astype(F32)
        return total


def shifted(src_ref, frame, first_row, class_on):
    start = 1 + frame * PATCHES
    base = jnp.minimum(start // TILE * TILE, src_ref.shape[0] // TILE * TILE - ROWS - TILE)
    base = pl.multiple_of(base, TILE)
    chunk = src_ref[pl.ds(base, ROWS + TILE), :]
    row = lax.broadcasted_iota(jnp.int32, (ROWS, ROWS + TILE), 0)
    col = lax.broadcasted_iota(jnp.int32, (ROWS, ROWS + TILE), 1)
    pick = ((col == row + (start - base)) & (row < PATCHES)).astype(F32).astype(BF)
    got = nn(pick, chunk)
    last = src_ref.shape[0] - 1
    end_row = src_ref[last : last + 1, :].astype(F32)
    tail = got[ROWS - TILE :]
    trow = lax.broadcasted_iota(jnp.int32, tail.shape, 0) + (ROWS - TILE)
    tail = jnp.where((trow == PATCHES - 1) & (frame == FRAMES - 1), end_row, tail)
    tail = jnp.where((trow == CLASS) & class_on, first_row, tail)
    return jnp.concatenate([got[: ROWS - TILE], tail], axis=0)


def time_kernel(
    clip_ref, cot_ref, gain_ref, shift_ref, bias_ref, w_ref, win_ref, wout_ref, bin_ref,
    p_ref, g_ref, h_ref, z_ref, o_ref, a_ref, near_ref, near_x_ref, far_ref, mid_ref, rows_ref,
    z_buf, b_buf, sems, b_sems,
):
    step = pl.program_id(0)
    row_steps = FRAMES // FPS
    steps = pl.num_programs(0)
    core = lax.rem(lax.axis_index("wide"), 2)
    part = half_rows()

    def near(src):
        return send(src.at[part], near_ref, sems, 0, "narrow", 1)

    def middle(src):
        return send(src.at[part], far_ref, sems, 1, "narrow", 3)

    def across():
        return send(near_ref, near_x_ref, sems, 2, "wide", 2)

    def outward():
        return send(far_ref, far_ref, sems, 3, "narrow", 1)

    def middle2():
        return send(near_ref, mid_ref, sems, 4, "narrow", 3)

    def biases():
        return [send(b_buf, rows_ref.at[b], b_sems, b, "narrow", b) for b in (1, 2, 3)]

    def own_bias():
        return pltpu.make_async_copy(b_buf, rows_ref.at[0], b_sems.at[0, 0])

    @pl.when(step == 0)
    def _():
        b_buf[...] = jnp.broadcast_to(row_of(bin_ref), b_buf.shape).astype(BF)
        greet(RING_ALL)
        for c, src in enumerate((win_ref, wout_ref)):

            @pl.when(core == c)
            def _():
                near(src).start()

            @pl.when((core == c) & inner())
            def _():
                middle(src).start()

        start(biases())
        own_bias().start()

    @pl.when(step < row_steps)
    def _():
        parts = []
        for j in range(FPS):
            frame = step * FPS + j
            p = shifted(clip_ref, frame, clip_ref[0:1, :].astype(F32), frame >= 0)
            p_ref[j] = p.astype(BF)
            xhat, _ = normed(p)
            parts.append((xhat * row_of(gain_ref) + row_of(shift_ref)).astype(BF))
            g_ref[j] = shifted(cot_ref, frame, cot_ref[0:1, :].astype(F32), frame == 0).astype(BF)
        h = jnp.concatenate(parts, axis=0)
        h_ref[...] = h.reshape(FPS, ROWS, WIDTH)
        project(h, w_ref, bias_ref, z_ref)
        z_buf[pl.ds(step * FPS, FPS)] = z_ref[...]

    @pl.when(step >= row_steps)
    def _():
        at = pl.multiple_of((step - row_steps) * TILE, TILE)
        time_attention(z_buf[:, pl.ds(at, TILE), :], o_ref, a_ref)

    @pl.when(step == row_steps + 2)
    def _():
        near(win_ref).wait()
        across().start()

        @pl.when(inner())
        def _():
            middle2().start()
            middle(win_ref).wait()
            outward().start()

    @pl.when(step == steps - 1)
    def _():
        across().wait()
        wait(biases())
        own_bias().wait()

        @pl.when(inner())
        def _():
            middle2().wait()
            outward().wait_send()

        @pl.when(jnp.logical_not(inner()))
        def _():
            outward().wait_recv()


def project(h, w_ref, bias_ref, z_ref):
    for which in range(3):
        cols = slice(which * WIDTH, (which + 1) * WIDTH)
        z = nn(h, w_ref[:, cols])
        if which != 1:
            z = z + bias_ref[which // 2 : which // 2 + 1].astype(F32)
        z = z.astype(BF)
        if which == 0:
            z = z * jnp.asarray(HEAD_DIM**-0.5, BF)
        z_ref[:, :, cols] = z.reshape(FPS, ROWS, WIDTH)


def time_attention(z, o_ref, a_ref):
    z = z.reshape(FRAMES * TILE, 3 * WIDTH)
    row = lax.broadcasted_iota(jnp.int32, (GROUP * FRAMES * TILE, FRAMES * TILE), 0)
    col = lax.broadcasted_iota(jnp.int32, (GROUP * FRAMES * TILE, FRAMES * TILE), 1)
    same = (row % TILE) == (col % TILE)
    scores = [nt(head_masked(z[:, group_cols(g, 0)]), z[:, group_cols(g, 1)]) for g in range(GROUPS)]
    probs = [softmax(jnp.where(same, s, NEG)) for s in scores]
    mixed = [nn(probs[g], z[:, group_cols(g, 2)]) for g in range(GROUPS)]
    for g in range(GROUPS):
        a_ref[0, g] = probs[g]
        o = head_select(mixed[g]).astype(BF)
        o_ref[:, :, g * GW : (g + 1) * GW] = o.reshape(FRAMES, TILE, GW)


def space_kernel(
    p_ref, ot_ref, offset_ref, gain_ref, shift_ref, out_ref, bias_ref, wt_ref, w_ref, wo_ref,
    near_ref, near_x_ref, far_ref, mid_ref,
    full_ref, h_ref, z_ref, a_ref, o_ref, x_ref, cls_ref, near_s_ref, near_xs_ref, far_x_ref, far2_ref,
    sems,
):
    step = pl.program_id(0)

    def moves():
        return [
            send(far_ref, far_x_ref, sems, 0, "wide", 2),
            send(near_ref, near_s_ref, sems, 1, "wide", 1),
            send(near_x_ref, near_xs_ref, sems, 2, "wide", 1),
        ]

    def outward():
        return send(mid_ref, far2_ref, sems, 3, "narrow", 1)

    def keep():
        return pltpu.make_async_copy(mid_ref, far2_ref, sems.at[0, 4])

    @pl.when(step == 1)
    def _():
        greet(RING)
        start(moves())

        @pl.when(inner())
        def _():
            outward().start()
            keep().start()

    p = p_ref[...].reshape(STEP, WIDTH).astype(F32)
    mixed = p + nn(ot_ref[...].reshape(STEP, WIDTH), wt_ref[...]) + row_of(offset_ref)
    row = lax.broadcasted_iota(jnp.int32, (STEP, WIDTH), 0) % ROWS
    full = jnp.where(row == CLASS, p, mixed)
    full_ref[...] = full.reshape(FPS, ROWS, WIDTH)
    xhat, _ = normed(full)
    h = (xhat * row_of(gain_ref) + row_of(shift_ref)).astype(BF)
    h_ref[...] = h.reshape(FPS, ROWS, WIDTH)
    project(h, w_ref, bias_ref, z_ref)
    key = lax.broadcasted_iota(jnp.int32, (GROUP * ROWS, ROWS), 1)
    for j in range(FPS):
        units = [(j, g) for g in range(GROUPS)]
        scores = [nt(head_masked(z_ref[j, :, group_cols(g, 0)]), z_ref[j, :, group_cols(g, 1)]) for j, g in units]
        probs = [softmax(jnp.where(key <= CLASS, s, NEG)) for s in scores]
        mixed = [nn(a, z_ref[j, :, group_cols(g, 2)]) for a, (j, g) in zip(probs, units)]
        for a, m, (j, g) in zip(probs, mixed, units):
            a_ref[j, g] = a
            o_ref[j, :, g * GW : (g + 1) * GW] = head_select(m).astype(BF)
    y = nn(o_ref[...].reshape(STEP, WIDTH), wo_ref[...]) + row_of(out_ref)
    x_ref[...] = (full + y).reshape(FPS, ROWS, WIDTH)
    for j in range(FPS):
        at = j * ROWS + CLASS - CLASS % 8
        cls_ref[j] = y[at : at + 8]

    @pl.when(step == pl.num_programs(0) - 1)
    def _():
        wait(moves())

        @pl.when(inner())
        def _():
            outward().wait_send()
            keep().wait()

        @pl.when(jnp.logical_not(inner()))
        def _():
            outward().wait_recv()


def mlp_kernel(first_call, *refs):
    refs = list(refs)

    def take(n):
        got = refs[:n]
        del refs[:n]
        return got

    step = pl.program_id(0)
    me = own_index()
    core = lax.rem(lax.axis_index("wide"), 2)
    row_steps = FRAMES // FPS
    chained = not first_call and hosted()
    x_ref, cls_ref, p_ref, g_ref, gain_ref, shift_ref, out_bias_ref, rows_ref = take(8)
    if first_call:
        win_ref, wout_ref = take(2)
        near_refs = take(4)
        far_ref, far_x_ref, far2_ref = take(3)
        h_ref, acc_ref, dh_ref, own_ref, oth_ref, gb_ref = take(6)
        far_s_ref, far_xs_ref, far2_x_ref, far2_s_ref, far2_xs_ref = take(5)
        swap = jnp.int32(0)
        slots = [(1, *near_refs)]
    else:
        h_ref, acc_ref, dh_ref = take(3)
        slots = [(0, *take(4)), (1, *take(4))]
        near_refs = take(2) if chained else None
        out_ref, dx_ref, own_ref, oth_ref, gv_ref, gb_ref = take(6)
        near_out = take(1)[0] if chained else None
        swap = inner().astype(jnp.int32)
    w_buf, h_buf, g_buf, act_buf, dpre_buf, t_buf, sem = take(7)
    if first_call:
        (rsems,) = take(1)

        def moves():
            return [
                send(far_ref, far_s_ref, rsems, 0, "wide", 1),
                send(far_x_ref, far_xs_ref, rsems, 1, "wide", 1),
                send(far2_ref, far2_s_ref, rsems, 2, "wide", 1),
            ]

        def across():
            return send(far2_ref, far2_x_ref, rsems, 3, "wide", 2)

        def last_move():
            return send(far2_x_ref, far2_xs_ref, rsems, 4, "wide", 1)

        @pl.when(step == 1)
        def _():
            greet((("wide", 1), ("wide", 2)))
            across().start()
            start(moves())

        @pl.when(step == row_steps)
        def _():
            across().wait()
            last_move().start()

    else:
        (out_buf,) = take(1)
    if chained:
        plane = PlaneSum(*near_refs, *take(5))
        rz, zsem = take(2)

        def line_copies():
            return [send(plane.got.at[0, m, pl.ds(96, 96)], rz.at[m], zsem, m, "narrow", 1) for m in range(2)]

        def near_total():
            wait(line_copies())
            for m in range(2):
                near_out[m] = plane.got[0, m, 0:96].astype(F32) + rz[m].astype(F32)

        def line_stage():
            plane.stage3()
            start(line_copies())

        def begin():
            greet()
            plane.stage0()

    def checkpoint():
        if chained:
            for k, action in {0: begin, 1: plane.stage1, 3: plane.stage2}.items():
                pl.when(step == k)(action)

    @pl.when(step == 0)
    def _():
        if not first_call:
            gv_ref[...] = jnp.zeros_like(gv_ref)
        gb_ref[...] = jnp.zeros_like(gb_ref)

    part = half_rows()
    size = WIDTH // 2
    other = pl.ds(pl.multiple_of(size - part.start, size), size)

    def fetches(slot, mine, mine_x, sib, sib_x, c):
        into = ((mine, mine_x), (sib, sib_x)) if c == 0 else ((sib, sib_x), (mine, mine_x))
        return [
            pltpu.make_async_copy(into[m][i], w_buf.at[m, slot, rows], sem.at[4 * slot + 2 * m + i])
            for m in range(2) for i, rows in enumerate((part, other))
        ]

    @pl.when(step == 0)
    def _():
        for c in range(2):

            @pl.when(core == c)
            def _():
                for entry in slots:
                    start(fetches(*entry, c))

    def arrived(slot):
        for entry in slots:
            if entry[0] == slot:

                @pl.when(step == 0)
                def _():
                    wait(fetches(*entry, 0))

    def weight(m, slot):
        if first_call and slot == 0:
            return (win_ref, wout_ref)[m][...]
        return w_buf[m, slot]

    def bias(slot):
        if first_call:
            return rows_ref[slot, 0:1].astype(F32)
        return rows_ref[2 + jnp.bitwise_xor(slot, swap), 0:1].astype(F32)

    @pl.when(step < row_steps)
    def _():
        at = pl.ds(pl.multiple_of(step * STEP, STEP), STEP)
        x = x_ref[...].reshape(STEP, WIDTH)
        mean_cls = jnp.mean(cls_ref[:, CLASS % 8, :], axis=0, keepdims=True)
        first = p_ref[0, CLASS % TILE : CLASS % TILE + 1, :].astype(F32) + mean_cls
        row = lax.broadcasted_iota(jnp.int32, (STEP, WIDTH), 0) % ROWS
        x = jnp.where(row == CLASS, first, x)
        xhat, scale = normed(x)
        g = g_ref[...].reshape(STEP, WIDTH)
        if first_call:
            h = (xhat * row_of(gain_ref) + row_of(shift_ref)).astype(BF)
            h_ref[...] = h.reshape(FPS, ROWS, WIDTH)
            acc = x + row_of(out_bias_ref)
            dh = None
        else:
            h = h_ref[...].reshape(STEP, WIDTH)
            acc = acc_ref[...].reshape(STEP, WIDTH)
            dh = dh_ref[...].reshape(STEP, WIDTH)
        h_buf[at, :] = h
        g_buf[at, :] = g
        for s in range(2):
            arrived(s)
            if s == 1:
                checkpoint()
            cols = slice(s * WIDTH, (s + 1) * WIDTH)
            pre = nn(h, weight(0, s)) + bias(s)
            cdf = 0.5 + 0.5 * lax.erf(pre * (0.5**0.5))
            act = (pre * cdf).astype(BF)
            slope = cdf + pre * (jnp.exp(-0.5 * pre * pre) * 0.3989422804014327)
            act_buf[at, cols] = act
            dpre = (nt(g, weight(1, s)) * slope).astype(BF)
            dpre_buf[at, cols] = dpre
            gb_ref[s : s + 1, :] += colsum(dpre)
            acc = acc + nn(act, weight(1, s))
            back = nt(dpre, weight(0, s))
            dh = back if dh is None else dh + back
        if first_call:
            acc_ref[...] = acc.reshape(FPS, ROWS, WIDTH)
            dh_ref[...] = dh.reshape(FPS, ROWS, WIDTH)
        else:
            for k in range(row_steps):

                @pl.when(step == k)
                def _():
                    if k == 0:
                        out_buf[0:1, :] = acc[CLASS : CLASS + 1]
                    for j in range(FPS):
                        start = 1 + (k * FPS + j) * PATCHES
                        out_buf[start : start + PATCHES, :] = acc[j * ROWS : j * ROWS + PATCHES]

            gf = g.astype(F32)
            dx_ref[...] = (gf + norm_back(dh, xhat, scale, row_of(gain_ref))).reshape(FPS, ROWS, WIDTH)
            gv_ref[0:1] += colsum(dh * xhat)
            gv_ref[1:2] += colsum(dh)
            gv_ref[2:3] += colsum(gf)

    def matrix(unit, left_ref, right_ref):
        t_buf[...] = left_ref[...].T
        for s in range(2):
            got = nn(t_buf[...], right_ref[:, s * WIDTH : (s + 1) * WIDTH]).astype(BF)
            for w in range(CHUNKS):
                put_chunk(own_ref, oth_ref, me, w, 2 * unit + jnp.bitwise_xor(s, swap), got[w * 96 : (w + 1) * 96])

    @pl.when(step == row_steps)
    def _():
        matrix(0, h_buf, dpre_buf)
        if not first_call:
            out_ref[0] = out_buf[...].astype(BF)

    @pl.when(step == row_steps + 1)
    def _():
        if chained:
            line_stage()
        matrix(1, g_buf, act_buf)
        if chained:
            near_total()
        if first_call:
            wait(moves())
            last_move().wait()


def put_chunk(own_ref, oth_ref, me, w, unit, value):
    rel = jnp.bitwise_xor(me, w)
    place = rel // 2
    for c, ref in enumerate((own_ref, oth_ref)):

        @pl.when(rel % 2 == c)
        def _():
            ref[place, unit] = value


def space_back_kernel(*refs):
    refs = list(refs)

    def take(n):
        got = refs[:n]
        del refs[:n]
        return got

    dx_ref, dcls_ref, full_ref, z_ref, a_ref, gain_ref, wo_ref, w_ref, wt_ref = take(9)
    far_refs = take(2) if hosted() else None
    dy_ref, dz_ref, df_ref, dyt_ref, dot_ref, gv_ref = take(6)
    far_out = take(1)[0] if hosted() else None
    (do_ref,) = take(1)
    step = pl.program_id(0)
    plane = PlaneSum(*far_refs, *take(5)) if hosted() else None

    def begin():
        greet(PLANE)
        plane.stage0()

    def finish():
        plane.stage3()
        far_out[...] = plane.got[0]

    def checkpoint(plan):
        if hosted():
            for k, action in plan.items():
                pl.when(step == k)(action)

    @pl.when(step == 0)
    def _():
        gv_ref[...] = jnp.zeros_like(gv_ref)

    dx = dx_ref[...].reshape(STEP, WIDTH)
    row = lax.broadcasted_iota(jnp.int32, (STEP, WIDTH), 0) % ROWS
    dcls = dcls_ref[0, CLASS % 8 : CLASS % 8 + 1, :] * (1.0 / FRAMES)
    dy = jnp.where(row == CLASS, dcls, jnp.where(row < CLASS, dx, 0.0)).astype(BF)
    dy_ref[...] = dy.reshape(FPS, ROWS, WIDTH)
    gv_ref[0:1, :WIDTH] += colsum(dy)
    do_ref[...] = nt(dy, wo_ref[...]).astype(BF)
    for j in range(FPS):
        if j > 0:
            checkpoint({0: begin, 1: plane.stage1} if hosted() else {})
        units = [(j, g) for g in range(GROUPS)]
        dos = [head_masked(do_ref[j * ROWS : (j + 1) * ROWS, g * GW : (g + 1) * GW]) for j, g in units]
        das = [nt(do, z_ref[j, :, group_cols(g, 2)]) for do, (j, g) in zip(dos, units)]
        dvs = [tn(a_ref[j, g], do) for do, (j, g) in zip(dos, units)]
        dss = [score_back(a_ref[j, g], da) for da, (j, g) in zip(das, units)]
        for dv, (j, g) in zip(dvs, units):
            dz_ref[j, :, group_cols(g, 2)] = dv.astype(BF)
        dqs = [nn(ds, z_ref[j, :, group_cols(g, 1)]) for ds, (j, g) in zip(dss, units)]
        dks = [tn(ds, head_masked(z_ref[j, :, group_cols(g, 0)])) for ds, (j, g) in zip(dss, units)]
        for dq, dk, (j, g) in zip(dqs, dks, units):
            dz_ref[j, :, group_cols(g, 0)] = (head_select(dq) * HEAD_DIM**-0.5).astype(BF)
            dz_ref[j, :, group_cols(g, 1)] = dk.astype(BF)
    dz = dz_ref[...].reshape(STEP, 3 * WIDTH)
    gv_ref[1:2, :] += colsum(dz)
    dh = nt(dz, w_ref[...])
    xhat, scale = normed(full_ref[...].reshape(STEP, WIDTH))
    gv_ref[2:3, :WIDTH] += colsum(dh * xhat)
    gv_ref[3:4, :WIDTH] += colsum(dh)
    df = dx + norm_back(dh, xhat, scale, row_of(gain_ref))
    df_ref[...] = df.reshape(FPS, ROWS, WIDTH)
    dyt = jnp.where(row < CLASS, df, 0.0).astype(BF)
    dyt_ref[...] = dyt.reshape(FPS, ROWS, WIDTH)
    gv_ref[4:5, :WIDTH] += colsum(dyt)
    dot_ref[...] = nt(dyt, wt_ref[...]).astype(BF).reshape(FPS, ROWS, WIDTH)
    checkpoint({2: plane.stage2, 3: finish} if hosted() else {})


def space_grad_kernel(dz_ref, h_ref, dy_ref, o_ref, dyt_ref, ot_ref, own_ref, oth_out, *refs):
    oth_ref = refs[0] if hosted() else oth_out
    step = pl.program_id(0)
    me = own_index()
    half = CHUNKS // 2

    def exchange(k):
        rows = (pl.ds(0, 288), pl.ds(288, 96), pl.ds(384, 96))[k]
        return send(oth_ref.at[:, rows], oth_out.at[:, rows], refs[1], k, "wide", 1)

    @pl.when(step < 2)
    def _():
        got = tn(dz_ref[...], h_ref[...]).astype(BF)
        for i in range(half):
            w = step * half + i
            put_rows(own_ref, oth_ref, me, w, 0, got[i * 288 : (i + 1) * 288])

    if hosted():

        @pl.when(step == 1)
        def _():
            greet((("wide", 1),))
            exchange(0).start()

    for k, left, right in ((2, dy_ref, o_ref), (3, dyt_ref, ot_ref)):

        @pl.when(step == k)
        def _():
            got = tn(left[...], right[...]).astype(BF)
            for w in range(CHUNKS):
                put_rows(own_ref, oth_ref, me, w, 96 * (k + 1), got[w * 96 : (w + 1) * 96])
            if hosted():
                exchange(k - 1).start()

    if hosted():

        @pl.when(step == 3)
        def _():
            for k in range(3):
                exchange(k).wait()


def put_rows(own_ref, oth_ref, me, w, start, value):
    rel = jnp.bitwise_xor(me, w)
    place = rel // 2
    for c, ref in enumerate((own_ref, oth_ref)):

        @pl.when(rel % 2 == c)
        def _():
            ref[place, start : start + value.shape[0], :] = value


PIECE = (CHUNKS // 2, 384, WIDTH)
SPACE_ROWS = 480
TIME_ROWS = 288


def time_back_kernel(*refs):
    refs = list(refs)

    def take(n):
        got = refs[:n]
        del refs[:n]
        return got

    z_ref, a_ref, do_ref, h_any = take(4)
    space_refs = take(2) if hosted() else None
    near_ref, far_ref = take(2) if hosted() else (None, None)
    dz_ref, own_ref, oth_out = take(3)
    parts_ref, fc_ref = take(2) if hosted() else (None, None)
    dz_buf, h_buf, h_sem = take(3)
    oth_ref = oth_out
    step = pl.program_id(0)
    chunks = ROWS // TILE
    me = own_index()

    def load():
        return pltpu.make_async_copy(h_any, h_buf, h_sem)

    if hosted():
        plane = PlaneSum(*space_refs, *take(5))
        rz, zsem, oth_ref, x_sems = take(4)

        def line_copies():
            return [
                send(far_ref.at[m, pl.ds(96 * i, 96)], rz.at[m, i], zsem, 2 * m + i, "narrow", 2 + i)
                for m in range(2) for i in range(2)
            ]

        def exchange(k):
            base = pl.multiple_of(2 * jnp.bitwise_xor(me // 4, k), 2)
            place = pl.ds(base, 2)
            return send(oth_ref.at[place], oth_out.at[place], x_sems, k, "wide", 1)

        @pl.when(step == 0)
        def _():
            start(plane.load_both())

        @pl.when(step == 1)
        def _():
            greet()
            start(line_copies())
            plane.arrived()

        pl.when(step == chunks - 1)(plane.stage2)

    pl.when(step == 0)(lambda: load().start())

    @pl.when(step < chunks)
    def _():
        z = z_ref[...].reshape(FRAMES * TILE, 3 * WIDTH)
        dot = do_ref[...].reshape(FRAMES * TILE, WIDTH)
        groups = range(GROUPS)
        dos = [head_masked(dot[:, g * GW : (g + 1) * GW]) for g in groups]
        das = [nt(dos[g], z[:, group_cols(g, 2)]) for g in groups]
        dvs = [tn(a_ref[0, g], dos[g]) for g in groups]
        dss = [score_back(a_ref[0, g], das[g]) for g in groups]
        dqs = [nn(dss[g], z[:, group_cols(g, 1)]) for g in groups]
        dks = [tn(dss[g], head_masked(z[:, group_cols(g, 0)])) for g in groups]
        for g in groups:
            for which, v in enumerate((head_select(dqs[g]) * HEAD_DIM**-0.5, dks[g], dvs[g])):
                dz_ref[:, :, group_cols(g, which)] = v.astype(BF).reshape(FRAMES, TILE, GW)
        dz_buf[:, pl.ds(pl.multiple_of(step * TILE, TILE), TILE), :] = dz_ref[...]

    pl.when(step == chunks)(lambda: load().wait())
    half = CHUNKS // 2
    for k in range(2):

        @pl.when(step == chunks + k)
        def _():
            left = dz_buf[:, :, k * half * 288 : (k + 1) * half * 288]
            got = tn(left.reshape(FRAMES * ROWS, half * 288), h_buf[...]).astype(BF)
            for i in range(half):
                put_rows(own_ref, oth_ref, me, k * half + i, 0, got[i * 288 : (i + 1) * 288])
            if hosted():
                exchange(k).start()

    if hosted():

        @pl.when(step == chunks + 1)
        def _():
            wait(line_copies())
            for m in range(2):
                fc_ref[m] = near_ref[m] + rz[m, 0].astype(F32) + rz[m, 1].astype(F32)
            plane.stage3()
            cut_columns(plane.got, parts_ref)
            for k in range(2):
                exchange(k).wait()


def cut_columns(got, parts_ref):
    size = WIDTH // parts_ref.shape[0]
    for n in range(parts_ref.shape[0]):
        cols = slice(n * size, (n + 1) * size)
        parts_ref[n] = jnp.concatenate([got[0, 0, :, cols], got[0, 1, :, cols]], axis=1)


def turned(total):
    size = total.shape[1] // 2
    return jnp.concatenate([total[:, :size].T, total[:, size:].T], axis=1)


VEC_ROWS = 24


def time_out_kernel(*refs):
    refs = list(refs)

    def take(n):
        got = refs[:n]
        del refs[:n]
        return got

    dz_ref, p_ref, df_ref, gain_ref, w_ref = take(5)
    if hosted():
        time_refs = take(2)
        s_parts, gvm_ref, gvs_ref, gba_ref, gbb_ref = take(5)
    dp_ref, gv_ref = take(2)
    step = pl.program_id(0)
    row_steps = FRAMES // FPS
    line = lax.axis_index("narrow")
    if hosted():
        sq_ref, sp_ref, tp_ref, tq_ref, share_ref, hid_ref = take(6)
        plane = PlaneSum(*time_refs, *take(5))
        (parts,) = take(1)
        s_line = LineSum(s_parts, *take(2))
        t_line = LineSum(parts, *take(2))
        vbuf, vrecv, vsem = take(3)

        @pl.when(step == 0)
        def _():
            start(plane.load_both())
            greet()
            start(s_line.copies())
            plane.arrived()

        pl.when(step == row_steps - 1)(plane.stage2)

    @pl.when(step == 0)
    def _():
        gv_ref[...] = jnp.zeros_like(gv_ref)
        dp_ref[0:1, 0, :] = jnp.zeros((1, WIDTH), F32)

    @pl.when(step < row_steps)
    def _():
        dz = dz_ref[...].reshape(STEP, 3 * WIDTH)
        gv_ref[0:1, :] += colsum(dz)
        dh = nt(dz, w_ref[...])
        xhat, scale = normed(p_ref[...].reshape(STEP, WIDTH).astype(F32))
        gv_ref[1:2, :WIDTH] += colsum(dh * xhat)
        gv_ref[2:3, :WIDTH] += colsum(dh)
        df = df_ref[...].reshape(STEP, WIDTH)
        dp = df + norm_back(dh, xhat, scale, row_of(gain_ref))
        for j in range(FPS):
            dp_ref[0:1, 0, :] += df[j * ROWS + CLASS : j * ROWS + CLASS + 1]
        for k in range(row_steps):

            @pl.when(step == k)
            def _():
                for j in range(FPS):
                    begin = 1 + (k * FPS + j) * PATCHES
                    dp_ref[begin : begin + PATCHES, 0, :] = dp[j * ROWS : j * ROWS + PATCHES]

    if hosted():

        @pl.when(step == row_steps)
        def _():
            vbuf[...] = jnp.zeros_like(vbuf)
            vbuf[0:3, :] = gvm_ref[0:3, :]
            for i, r, c in ((3, 0, 0), (4, 1, 0), (5, 1, 2), (6, 2, 0), (7, 3, 0), (8, 4, 0)):
                vbuf[i : i + 1, :] = gvs_ref[r : r + 1, c * WIDTH : (c + 1) * WIDTH]
            for i, r, c in ((9, 0, 0), (10, 0, 2), (11, 1, 0), (12, 2, 0)):
                vbuf[i : i + 1, :] = gv_ref[r : r + 1, c * WIDTH : (c + 1) * WIDTH]
            low = line < 2
            places = (line, jnp.bitwise_xor(line, 1), jnp.where(low, 2, 1), jnp.where(low, 3, 0))
            for place, (ref, r) in zip(places, ((gba_ref, 0), (gba_ref, 1), (gbb_ref, 0), (gbb_ref, 1))):
                vbuf[pl.ds(13 + place, 1), :] = ref[r : r + 1, :]

            def exchange(k, axis, bit):
                return send(vbuf, vrecv.at[k], vsem, k, axis, bit)

            def added(k, axis, bit):
                exchange(k, axis, bit).wait()
                vbuf[...] += vrecv[k]

            exchange(0, "wide", 1).start()
            plane.stage3()
            cut_columns(plane.got, parts)
            start(t_line.copies())
            added(0, "wide", 1)
            exchange(1, "wide", 2).start()
            added(1, "wide", 2)
            exchange(2, "wide", 4).start()
            total = turned(s_line.result())
            sq_ref[...] = total[:, :288]
            sp_ref[...] = total[:, 288:384]
            tp_ref[...] = total[:, 384:480]
            added(2, "wide", 4)
            for b in (1, 2, 3):
                exchange(2 + b, "narrow", b).start()
            for b in (1, 2, 3):
                exchange(2 + b, "narrow", b).wait()
            vectors = vbuf[...] + vrecv[3] + vrecv[4] + vrecv[5]
            size = WIDTH // 4
            share = vectors[:, :size]
            hidden = vectors[13:14, :]
            for n in range(1, 4):
                share = jnp.where(line == n, vectors[:, n * size : (n + 1) * size], share)
                hidden = jnp.where(line == n, vectors[13 + n : 14 + n, :], hidden)
            share_ref[...] = share
            hid_ref[...] = hidden
            tq_ref[...] = turned(t_line.result())


VECTORS = (11, 12, (9, 11), 8, 6, 7, (4, 6), 3, 0, 1, 2)


def outputs_kernel(share_ref, hid_ref, *refs):
    count = len(refs) - len(VECTORS) - 1
    ins, outs = refs[: count // 2], refs[count // 2 :]
    for src, dst in zip(ins, outs):
        dst[...] = src[...]
    outs = outs[len(ins) :]
    for rows, dst in zip(VECTORS, outs):
        if isinstance(rows, tuple):
            dst[...] = share_ref[rows[0] : rows[1], :]
        else:
            dst[...] = share_ref[rows : rows + 1, :].reshape(dst.shape)
    outs[-1][...] = hid_ref[0:1, :].reshape(outs[-1].shape)


def flip(value, axis, bit):
    return lax.ppermute(value, axis, [(i, i ^ bit) for i in range(lax.axis_size(axis))])


def unit_sum(own, oth):
    both = jnp.stack([own, oth], axis=1).reshape(CHUNKS, 4, 96, WIDTH)
    both = both.transpose(1, 0, 2, 3).reshape(4, WIDTH, WIDTH)
    both = lax.psum_scatter(both, "wide", scatter_dimension=1, tiled=True)
    return both.reshape(2, 2, -1, WIDTH)


def piece_sum(own, oth, sizes, me):
    both = jnp.stack([own, oth], axis=1).reshape(CHUNKS, -1, WIDTH)
    found, at = [], 0
    for size in sizes:
        rows = both[:, at * 96 : (at + size) * 96].reshape(size * WIDTH, WIDTH)
        at += size
        rows = lax.psum_scatter(rows, "wide", scatter_dimension=0, tiled=True)
        parts = rows.T.reshape(lax.axis_size("narrow"), -1, rows.shape[0])
        found.append(line_sum(parts, me))
    return found


def line_sum(parts, me):
    total = lax.dynamic_index_in_dim(parts, me, 0, False).astype(F32)
    for bit in (1, 2, 3):
        other = lax.dynamic_index_in_dim(parts, jnp.bitwise_xor(me, bit), 0, False)
        total = total + flip(other, "narrow", bit).astype(F32)
    return total


def local(
    video_clips, time_gain, time_shift, time_qkv, time_bias, time_proj, time_offset,
    space_gain, space_shift, space_qkv, space_bias, space_proj, space_offset,
    mlp_gain, mlp_shift, fc_in, in_bias, fc_out, out_bias, cotangent,
):
    slices = lax.axis_size("narrow")
    tokens = video_clips.shape[1]
    clip = video_clips[0]
    cot = cotangent[0]
    vec = pl.BlockSpec((WIDTH,), lambda *i: (0,), pipeline_mode=pl.Buffered(1))
    me_n = lax.axis_index("narrow")
    any_ref = pl.BlockSpec(memory_space=pl.ANY)
    message = (any_ref, jax.ShapeDtypeStruct((WIDTH // 2, WIDTH), BF))
    bias_rows = (any_ref, jax.ShapeDtypeStruct((4, TILE, WIDTH), BF))

    chunks = ROWS // TILE
    a_time = jax.ShapeDtypeStruct((chunks, GROUPS, GROUP * FRAMES * TILE, FRAMES * TILE), BF)

    def a_chunk(first):
        return pl.BlockSpec((1, *a_time.shape[1:]), lambda i: (jnp.clip(i - first, 0, chunks - 1), 0, 0, 0))

    a_space = (pl.BlockSpec((FPS, GROUPS, GROUP * ROWS, ROWS), lambda i: (i, 0, 0, 0)),
               jax.ShapeDtypeStruct((FRAMES, GROUPS, GROUP * ROWS, ROWS), BF))

    last = FRAMES // FPS - 1
    steps = last + 1
    rows = FRAMES * ROWS

    def row_in(width):
        return pl.BlockSpec((FPS, ROWS, width), lambda i: (jnp.minimum(i, last), 0, 0))

    def row_out(width, dtype):
        return row_in(width), jax.ShapeDtypeStruct((FRAMES, ROWS, width), dtype)

    def chunk(width, first):
        return pl.BlockSpec((FRAMES, TILE, width), lambda i: (0, jnp.clip(i - first, 0, chunks - 1), 0))

    def chunk_out(width, first):
        return chunk(width, first), jax.ShapeDtypeStruct((FRAMES, ROWS, width), BF)

    p, g, ht, zt, ot, at, near, near_x, far, mid, biases = call(
        time_kernel, "time", (steps + chunks,),
        [whole(tokens, WIDTH), whole(tokens, WIDTH), vec, vec, whole(2, WIDTH), whole(WIDTH, 3 * WIDTH),
         any_ref, any_ref, vec],
        [row_out(WIDTH, BF), row_out(WIDTH, BF), row_out(WIDTH, BF), row_out(3 * WIDTH, BF),
         chunk_out(WIDTH, steps), (a_chunk(steps), a_time)] + [message] * 4 + [bias_rows],
        scratch=[pltpu.VMEM((FRAMES, ROWS, 3 * WIDTH), BF), pltpu.VMEM((TILE, WIDTH), BF),
                 pltpu.SemaphoreType.DMA((2, 5)), pltpu.SemaphoreType.DMA((2, 4))],
        remote=1,
    )(clip, cot, time_gain, time_shift, time_bias, time_qkv, fc_in, fc_out, in_bias)
    full, hs, zs, a_s, o_s, xs, ycls, near_s, near_xs, far_x, far2 = call(
        space_kernel, "space", (steps,),
        [frames(WIDTH), frames(WIDTH), vec, vec, vec, vec, whole(2, WIDTH),
         whole(WIDTH, WIDTH), whole(WIDTH, 3 * WIDTH), whole(WIDTH, WIDTH)] + [any_ref] * 4,
        [frames_out(WIDTH, F32), frames_out(WIDTH, BF), frames_out(3 * WIDTH, BF), a_space,
         frames_out(WIDTH, BF), frames_out(WIDTH, F32),
         (pl.BlockSpec((FPS, 8, WIDTH), lambda i: (i, 0, 0)), jax.ShapeDtypeStruct((FRAMES, 8, WIDTH), F32))]
        + [message] * 4,
        scratch=[pltpu.SemaphoreType.DMA((2, 5))],
        remote=2,
    )(p, ot, time_offset, space_gain, space_shift, space_offset, space_bias, time_proj, space_qkv, space_proj, near, near_x,
      far, mid)
    unit_shape = (CHUNKS // 2, 4, 96, WIDTH)
    units = [(whole(*unit_shape), jax.ShapeDtypeStruct(unit_shape, BF))] * 2
    vec_out = [(whole(8, WIDTH), jax.ShapeDtypeStruct((8, WIDTH), F32))] * 2
    bufs = [
        pltpu.VMEM((2, 2, WIDTH, WIDTH), BF),
        pltpu.VMEM((rows, WIDTH), BF), pltpu.VMEM((rows, WIDTH), BF),
        pltpu.VMEM((rows, 2 * WIDTH), BF), pltpu.VMEM((rows, 2 * WIDTH), BF), pltpu.VMEM((WIDTH, rows), BF),
        pltpu.SemaphoreType.DMA((8,)),
    ]
    mlp_in = [row_in(WIDTH), whole(FRAMES, 8, WIDTH),
              pl.BlockSpec((1, TILE, WIDTH), lambda i: (0, CLASS // TILE, 0)), row_in(WIDTH), vec, vec, vec,
              whole(4, TILE, WIDTH)]
    mlp_args = (xs, ycls, p, g, mlp_gain, mlp_shift, out_bias, biases)
    hm, acc, dh, a_own, a_oth, gb_a, far_s, far_xs, far2_x, far2_s, far2_xs = call(
        partial(mlp_kernel, True), "mlp_near", (last + 3,),
        mlp_in + [whole(WIDTH, WIDTH), whole(WIDTH, WIDTH)] + [any_ref] * 7,
        [row_out(WIDTH, BF), row_out(WIDTH, F32), row_out(WIDTH, F32)] + units + vec_out[:1] + [message] * 5,
        scratch=bufs + [pltpu.SemaphoreType.DMA((2, 5))],
        remote=3,
    )(*mlp_args, fc_in, fc_out, near, near_x, near_s, near_xs, far, far_x, far2)
    units_in = []
    near_out = []
    near_args = []
    near_scratch = []
    if hosted():
        units_in = [any_ref] * 2
        near_args = [halves(a_own), halves(a_oth)]
        near_out = [(whole(2, 96, WIDTH), jax.ShapeDtypeStruct((2, 96, WIDTH), F32))]
        near_scratch = PlaneSum.scratch(384) + [pltpu.VMEM((2, 96, WIDTH), BF), pltpu.SemaphoreType.DMA((2, 2))]
    layer_out, dxs, b_own, b_oth, gv_m, gb_b, *near_sum = call(
        partial(mlp_kernel, False), "mlp_far", (last + 3,),
        mlp_in + [row_in(WIDTH), row_in(WIDTH), row_in(WIDTH)] + [any_ref] * 8 + units_in,
        [(whole(1, tokens, WIDTH), jax.ShapeDtypeStruct((1, tokens, WIDTH), BF)), row_out(WIDTH, F32)]
        + units + vec_out + near_out,
        scratch=bufs + [pltpu.VMEM((tokens, WIDTH), F32)] + near_scratch,
        remote=4 if hosted() else None,
    )(*mlp_args, hm, acc, dh, far, far_x, far_s, far_xs, far2, far2_x, far2_s, far2_xs, *near_args)

    far_in, far_args, far_out, far_scratch = [], [], [], []
    if hosted():
        far_in = [any_ref] * 2
        far_args = [halves(b_own), halves(b_oth)]
        far_out = [(whole(2, 192, WIDTH), jax.ShapeDtypeStruct((2, 192, WIDTH), BF))]
        far_scratch = PlaneSum.scratch(384)
    dys, dzs, df, dyt, dot, gv_s, *far_sum = call(
        space_back_kernel, "space_back", (steps,),
        [frames(WIDTH), pl.BlockSpec((1, 8, WIDTH), lambda i: (0, CLASS // 8, 0)), frames(WIDTH),
         frames(3 * WIDTH), a_space[0], vec,
         whole(WIDTH, WIDTH), whole(WIDTH, 3 * WIDTH), whole(WIDTH, WIDTH)] + far_in,
        [frames_out(WIDTH, BF), frames_out(3 * WIDTH, BF), frames_out(WIDTH, F32),
         frames_out(WIDTH, BF), frames_out(WIDTH, BF),
         (whole(8, 3 * WIDTH), jax.ShapeDtypeStruct((8, 3 * WIDTH), F32))] + far_out,
        scratch=[pltpu.VMEM((STEP, WIDTH), BF)] + far_scratch,
        remote=5 if hosted() else None,
    )(dxs, dxs, full, zs, a_s, space_gain, space_proj, space_qkv, time_proj, *far_args)

    def flat(value):
        return value.reshape(rows, value.shape[-1])

    piece = (CHUNKS // 2, SPACE_ROWS, WIDTH)
    s_own, s_oth = call(
        space_grad_kernel, "space_grad", (4,),
        [pl.BlockSpec((rows, 3 * WIDTH // 2), lambda i: (0, jnp.minimum(i, 1)))] + [whole(rows, WIDTH)] * 5,
        [(whole(*piece), jax.ShapeDtypeStruct(piece, BF)),
         (any_ref if hosted() else whole(*piece), jax.ShapeDtypeStruct(piece, BF))],
        scratch=[pltpu.VMEM(piece, BF), pltpu.SemaphoreType.DMA((2, 3))] if hosted() else [],
        remote=6 if hosted() else None,
    )(flat(dzs), flat(hs), flat(dys), flat(o_s), flat(dyt), flat(ot))

    s_parts = (slices, SPACE_ROWS // 2, 2 * WIDTH // slices)
    t_parts = (slices, TIME_ROWS // 2, 2 * WIDTH // slices)
    t_piece = (CHUNKS // 2, TIME_ROWS, WIDTH)
    share = WIDTH // slices
    back_in, back_args, back_out, back_scratch = [], [], [], []
    if hosted():
        back_in = [any_ref] * 2 + [whole(2, 96, WIDTH), any_ref]
        back_args = [halves(s_own), halves(s_oth), near_sum[0], far_sum[0]]
        back_out = [(whole(*s_parts), jax.ShapeDtypeStruct(s_parts, BF)),
                    (whole(2, 96, WIDTH), jax.ShapeDtypeStruct((2, 96, WIDTH), F32))]
        back_scratch = PlaneSum.scratch(SPACE_ROWS) + [
            pltpu.VMEM((2, 2, 96, WIDTH), BF), pltpu.SemaphoreType.DMA((2, 4)),
            pltpu.VMEM(t_piece, BF), pltpu.SemaphoreType.DMA((2, 2))]
    dzt, t_own, t_oth, *from_back = call(
        time_back_kernel, "time_back", (chunks + 2,),
        [chunk(3 * WIDTH, 0), a_chunk(0), chunk(WIDTH, 0), any_ref] + back_in,
        [chunk_out(3 * WIDTH, 0), (whole(*t_piece), jax.ShapeDtypeStruct(t_piece, BF)),
         (any_ref if hosted() else whole(*t_piece), jax.ShapeDtypeStruct(t_piece, BF))] + back_out,
        scratch=[pltpu.VMEM((FRAMES, ROWS, 3 * WIDTH), BF), pltpu.VMEM((rows, WIDTH), BF), pltpu.SemaphoreType.DMA]
        + back_scratch,
        remote=7 if hosted() else None,
    )(zt, at, dot, flat(ht), *back_args)

    out_in, out_args, out_out, out_scratch = [], [], [], []
    if hosted():
        out_in = [any_ref] * 2 + [whole(*s_parts), whole(8, WIDTH), whole(8, 3 * WIDTH)] + [whole(8, WIDTH)] * 2
        out_args = [halves(t_own), halves(t_oth), from_back[0], gv_m, gv_s, gb_a, gb_b]
        out_out = [
            (whole(*shape), jax.ShapeDtypeStruct(shape, F32))
            for shape in ((share, 288), (share, 96), (share, 96), (share, 288), (VEC_ROWS, share), (1, WIDTH))
        ]
        out_scratch = (
            PlaneSum.scratch(TIME_ROWS)
            + [pltpu.VMEM(t_parts, BF)]
            + LineSum.scratch(*s_parts[1:]) + LineSum.scratch(*t_parts[1:])
            + [pltpu.VMEM((VEC_ROWS, WIDTH), F32), pltpu.VMEM((6, VEC_ROWS, WIDTH), F32), pltpu.SemaphoreType.DMA((2, 6))]
        )
    grad_clips, gv_t, *sums = call(
        time_out_kernel, "time_out", (steps + (1 if hosted() else 0),),
        [row_in(3 * WIDTH), row_in(WIDTH), row_in(WIDTH), vec, whole(WIDTH, 3 * WIDTH)] + out_in,
        [(whole(tokens, 1, WIDTH), jax.ShapeDtypeStruct((tokens, 1, WIDTH), F32)),
         (whole(8, 3 * WIDTH), jax.ShapeDtypeStruct((8, 3 * WIDTH), F32))] + out_out,
        scratch=out_scratch,
        remote=8 if hosted() else None,
    )(dzt, p, df, time_gain, time_qkv, *out_args)
    grad_clips = grad_clips.reshape(1, tokens, WIDTH)

    if hosted():
        fc = from_back[1]
        *matrices, mine, hidden_row = sums
        outs = [(whole(*m.shape), jax.ShapeDtypeStruct(m.shape, F32)) for m in matrices]
        for v in VECTORS:
            shape = (2, share) if isinstance(v, tuple) else (share,)
            outs.append((whole(*shape), jax.ShapeDtypeStruct(shape, F32)))
        outs.append((whole(WIDTH), jax.ShapeDtypeStruct((WIDTH,), F32)))
        s_qkv, s_proj, t_proj, t_qkv, *found = call(
            outputs_kernel, "outputs", (1,), [whole(*v.shape) for v in (mine, hidden_row, *matrices)], outs,
        )(mine, hidden_row, *matrices)
        tg, tsh, tb, to, sg, ssh, sb, so, mg, msh, ob, grad_in_bias = found
    else:
        near_part = unit_sum(a_own, a_oth)
        far_part = unit_sum(b_own, b_oth)
        fc = near_part[:, 0].astype(F32) + flip(near_part[:, 1], "narrow", 1).astype(F32)
        fc = fc + flip(far_part[:, 0], "narrow", 2).astype(F32) + flip(far_part[:, 1], "narrow", 3).astype(F32)
        s_qkv, s_proj, t_proj = piece_sum(s_own, s_oth, (3, 1, 1), me_n)
        (t_qkv,) = piece_sum(t_own, t_oth, (3,), me_n)
        vectors = jnp.concatenate(
            [gv_m[0:3], gv_s[0:1, :WIDTH], gv_s[1:2, :WIDTH], gv_s[1:2, 2 * WIDTH :], gv_s[2:5, :WIDTH],
             gv_t[0:1, :WIDTH], gv_t[0:1, 2 * WIDTH :], gv_t[1:3, :WIDTH]]
        )
        lower = me_n < 2
        places = (me_n, jnp.bitwise_xor(me_n, 1), jnp.where(lower, 2, 1), jnp.where(lower, 3, 0))
        hidden_rows = jnp.zeros((slices, WIDTH), F32)
        for place, row in zip(places, (gb_a[0], gb_a[1], gb_b[0], gb_b[1])):
            hidden_rows = lax.dynamic_update_slice(hidden_rows, row[None], (place, 0))
        vectors = lax.psum(jnp.concatenate([vectors, hidden_rows], axis=0), ("wide", "narrow"))
        mine = lax.dynamic_slice(vectors, (0, me_n * share), (13, share))
        grad_in_bias = lax.dynamic_slice(vectors, (13 + me_n, 0), (1, WIDTH))[0]
        tg, tsh, tb, to, sg, ssh, sb, so, mg, msh, ob = [
            mine[v[0] : v[1]] if isinstance(v, tuple) else mine[v] for v in VECTORS
        ]
    return (
        layer_out, grad_clips, tg, tsh, t_qkv, tb, t_proj, to, sg, ssh, s_qkv, sb, s_proj, so, mg, msh,
        fc[0], grad_in_bias, fc[1].T, ob,
    )


def solution(mesh):
    rows = P(("wide", "narrow"), None, None)
    return jax.shard_map(
        local,
        mesh=mesh,
        in_specs=(rows,) + (P(),) * 14 + (P(None, "narrow"), P("narrow"), P("narrow", None), P(), rows),
        out_specs=(
            rows,
            rows,
            P("narrow"),
            P("narrow"),
            P("narrow", "wide"),
            P(None, "narrow"),
            P("narrow", "wide"),
            P("narrow"),
            P("narrow"),
            P("narrow"),
            P("narrow", "wide"),
            P(None, "narrow"),
            P("narrow", "wide"),
            P("narrow"),
            P("narrow"),
            P("narrow"),
            P("wide", "narrow"),
            P("narrow"),
            P("narrow", "wide"),
            P("narrow"),
        ),
        check_vma=False,
    )
```

```python
from functools import partial

import jax
import jax.numpy as jnp
from jax import lax
from jax.experimental import pallas as pl
from jax.experimental.pallas import tpu as pltpu
from jax.sharding import PartitionSpec as P

HEADS = 12
HEAD_DIM = 64
FRAMES = 8
PATCHES = 196
ROWS = 208
CLASS = 196
TILE = 16
WIDTH = 768
GROUP = 4
GW = GROUP * HEAD_DIM
GROUPS = HEADS // GROUP
FPS = 2
STEP = FPS * ROWS
EPSILON = 1e-06
F32 = jnp.float32
BF = jnp.bfloat16
NEG = -1e30
VMEM_LIMIT = 62 * 2**20
CHUNKS = 8


def dg(a, b, ca, cb):
    return lax.dot_general(a, b, (((ca,), (cb,)), ((), ())), preferred_element_type=F32)


def nn(a, b):
    return dg(a, b, 1, 0)


def nt(a, b):
    return dg(a, b, 1, 1)


def tn(a, b):
    return dg(a, b, 0, 0)


def call(kernel, name, grid, ins, outs, scratch=(), flops=0, nbytes=0, remote=None):
    extra = {} if remote is None else dict(collective_id=remote, has_side_effects=True)
    return pl.pallas_call(
        kernel,
        name=name,
        grid=grid,
        in_specs=[s for s in ins],
        out_specs=[s for s, _ in outs],
        out_shape=[t for _, t in outs],
        scratch_shapes=list(scratch),
        compiler_params=pltpu.CompilerParams(vmem_limit_bytes=VMEM_LIMIT, **extra),
        cost_estimate=pl.CostEstimate(flops=flops, bytes_accessed=nbytes, transcendentals=0),
    )


def whole(*shape):
    return pl.BlockSpec(shape, lambda *i: (0,) * len(shape), pipeline_mode=pl.Buffered(1))


def frames(width):
    return pl.BlockSpec((FPS, ROWS, width), lambda i: (i, 0, 0))


def frames_out(width, dtype):
    return frames(width), jax.ShapeDtypeStruct((FRAMES, ROWS, width), dtype)


def row_of(ref):
    return ref[...].astype(F32).reshape(1, ref.shape[0])


def normed(v):
    center = v - jnp.mean(v, axis=-1, keepdims=True)
    scale = lax.rsqrt(jnp.mean(center * center, axis=-1, keepdims=True) + EPSILON)
    return center * scale, scale


def norm_back(grad, xhat, scale, gain):
    g = grad * gain
    m1 = jnp.mean(g, axis=-1, keepdims=True)
    m2 = jnp.mean(g * xhat, axis=-1, keepdims=True)
    return scale * (g - m1 - xhat * m2)


def colsum(v):
    return jnp.sum(v.astype(F32), axis=0, keepdims=True)


def head_masked(block):
    lane = lax.broadcasted_iota(jnp.int32, block.shape, 1) // HEAD_DIM
    zero = jnp.zeros_like(block)
    return jnp.concatenate([jnp.where(lane == h, block, zero) for h in range(GROUP)], axis=0)


def head_select(stacked):
    rows = stacked.shape[0] // GROUP
    lane = lax.broadcasted_iota(jnp.int32, (rows, GW), 1) // HEAD_DIM
    out = stacked[:rows]
    for h in range(1, GROUP):
        out = jnp.where(lane == h, stacked[h * rows : (h + 1) * rows], out)
    return out


def softmax(scores):
    e = jnp.exp(scores - jnp.max(scores, axis=-1, keepdims=True))
    return (e * (1.0 / jnp.sum(e, axis=-1, keepdims=True))).astype(BF)


def score_back(a, da):
    af = a.astype(F32)
    return (af * (da - jnp.sum(af * da, axis=-1, keepdims=True))).astype(BF)


def group_cols(g, which):
    start = which * WIDTH + g * GW
    return slice(start, start + GW)


def hosted():
    return lax.axis_size("wide") == CHUNKS


def own_index():
    return lax.axis_index("wide") if hosted() else jnp.int32(0)


def peer(axis, bit):
    return {axis: jnp.bitwise_xor(lax.axis_index(axis), bit)}


RING = (("wide", 1), ("wide", 2), ("narrow", 1), ("narrow", 3))
RING_ALL = RING + (("narrow", 2),)
PLANE = (("wide", 1), ("wide", 2), ("wide", 4))
LINE = (("narrow", 1), ("narrow", 2), ("narrow", 3))
PEERS = PLANE + LINE
ALL_WIDE = tuple(("wide", b) for b in range(1, 8))


def inner():
    line = lax.axis_index("narrow")
    return (line == 1) | (line == 2)


def greet(peers=PEERS):
    barrier = pltpu.get_barrier_semaphore()
    for axis, bit in peers:
        pl.semaphore_signal(barrier, inc=1, device_id=peer(axis, bit), device_id_type=pl.DeviceIdType.MESH)
    pl.semaphore_wait(barrier, len(peers))


def half_rows():
    size = WIDTH // 2
    return pl.ds(pl.multiple_of(lax.rem(lax.axis_index("wide") // 2, 2) * size, size), size)


def send(src, dst, sems, k, axis, bit):
    return pltpu.make_async_remote_copy(
        src_ref=src, dst_ref=dst, send_sem=sems.at[0, k], recv_sem=sems.at[1, k],
        device_id=peer(axis, bit), device_id_type=pl.DeviceIdType.MESH,
    )


def start(copies):
    for c in copies:
        c.start()


def wait(copies):
    for c in copies:
        c.wait()


def plus(a, b):
    return a + b


class PlaneSum:
    SEMS = 7

    @staticmethod
    def scratch(rows):
        half = rows // 2
        return [
            pltpu.VMEM((4, 2, half, WIDTH), BF),
            pltpu.VMEM((4, 2, half, WIDTH), BF),
            pltpu.VMEM((2, 2, half, WIDTH), BF),
            pltpu.SemaphoreType.DMA((2, PlaneSum.SEMS)),
            pltpu.SemaphoreType.DMA,
        ]

    def __init__(self, own, oth, recv, got, near, sems, own_sem):
        self.own, self.oth, self.recv, self.got, self.near, self.sems = own, oth, recv, got, near, sems
        self.own_sem = own_sem

    def load(self):
        return [pltpu.make_async_copy(self.own, self.got, self.own_sem)]

    def chip(self):
        return [send(self.oth, self.recv, self.sems, 0, "wide", 1)]

    def first(self):
        got, near, sems = self.got, self.near, self.sems
        return [
            send(got.at[1, 0], near.at[0, 0], sems, 1, "wide", 2),
            send(got.at[3, 0], near.at[0, 1], sems, 2, "wide", 2),
            send(got.at[2, 1], near.at[1, 0], sems, 3, "wide", 4),
            send(got.at[3, 1], near.at[1, 1], sems, 4, "wide", 4),
        ]

    def second(self):
        got, recv, sems = self.got, self.recv, self.sems
        return [
            send(got.at[2, 0], recv.at[0, 0], sems, 5, "wide", 4),
            send(got.at[1, 1], recv.at[0, 1], sems, 6, "wide", 2),
        ]

    def load_both(self):
        return self.load() + [pltpu.make_async_copy(self.oth, self.recv, self.sems.at[0, 0])]

    def stage0(self):
        start(self.load())
        start(self.chip())

    def arrived(self):
        wait(self.load_both())
        self.sum_chip()

    def stage1(self):
        wait(self.load())
        wait(self.chip())
        self.sum_chip()

    def sum_chip(self):
        @pl.loop(0, 4)
        def _(q):
            for h in range(2):
                self.got[q, h] = plus(self.got[q, h], self.recv[q, h])

        start(self.first())

    def stage2(self):
        wait(self.first())
        for q, h, way, i in ((0, 0, 0, 0), (2, 0, 0, 1), (0, 1, 1, 0), (1, 1, 1, 1)):
            self.got[q, h] = plus(self.got[q, h], self.near[way, i])
        start(self.second())

    def stage3(self):
        wait(self.second())
        for h in range(2):
            self.got[0, h] = plus(self.got[0, h], self.recv[0, h])


def halves(piece):
    return piece.reshape(4, 2, -1, WIDTH)


class LineSum:
    def __init__(self, parts, recv, sems):
        self.parts, self.recv, self.sems = parts, recv, sems

    @staticmethod
    def scratch(rows, width):
        return [pltpu.VMEM((3, rows, width), BF), pltpu.SemaphoreType.DMA((2, 3))]

    def copies(self):
        line = lax.axis_index("narrow")
        return [
            send(self.parts.at[jnp.bitwise_xor(line, b)], self.recv.at[b - 1], self.sems, b - 1, "narrow", b)
            for b in (1, 2, 3)
        ]

    def result(self):
        wait(self.copies())
        total = self.parts[lax.axis_index("narrow")].astype(F32)
        for b in range(3):
            total = total + self.recv[b].astype(F32)
        return total


def shifted(src_ref, frame, first_row, class_on):
    start = 1 + frame * PATCHES
    base = jnp.minimum(start // TILE * TILE, src_ref.shape[0] // TILE * TILE - ROWS - TILE)
    base = pl.multiple_of(base, TILE)
    chunk = src_ref[pl.ds(base, ROWS + TILE), :]
    row = lax.broadcasted_iota(jnp.int32, (ROWS, ROWS + TILE), 0)
    col = lax.broadcasted_iota(jnp.int32, (ROWS, ROWS + TILE), 1)
    pick = ((col == row + (start - base)) & (row < PATCHES)).astype(F32).astype(BF)
    got = nn(pick, chunk)
    last = src_ref.shape[0] - 1
    end_row = src_ref[last : last + 1, :].astype(F32)
    tail = got[ROWS - TILE :]
    trow = lax.broadcasted_iota(jnp.int32, tail.shape, 0) + (ROWS - TILE)
    tail = jnp.where((trow == PATCHES - 1) & (frame == FRAMES - 1), end_row, tail)
    tail = jnp.where((trow == CLASS) & class_on, first_row, tail)
    return jnp.concatenate([got[: ROWS - TILE], tail], axis=0)


def time_kernel(
    clip_ref, cot_ref, gain_ref, shift_ref, bias_ref, w_ref, win_ref, wout_ref, bin_ref,
    p_ref, g_ref, h_ref, z_ref, o_ref, a_ref, near_ref, far_ref, rows_ref,
    z_buf, b_buf, sems, b_sems,
):
    step = pl.program_id(0)
    row_steps = FRAMES // FPS
    steps = pl.num_programs(0)
    core = lax.rem(lax.axis_index("wide"), 2)
    part = half_rows()

    def near(src):
        return send(src.at[part], near_ref, sems, 0, "narrow", 1)

    def middle(src):
        return send(src.at[part], far_ref, sems, 1, "narrow", 3)

    def biases():
        return [send(b_buf, rows_ref.at[b], b_sems, b, "narrow", b) for b in (1, 2, 3)]

    def own_bias():
        return pltpu.make_async_copy(b_buf, rows_ref.at[0], b_sems.at[0, 0])

    @pl.when(step == 0)
    def _():
        b_buf[...] = jnp.broadcast_to(row_of(bin_ref), b_buf.shape).astype(BF)
        greet(RING_ALL)
        for c, src in enumerate((win_ref, wout_ref)):

            @pl.when(core == c)
            def _():
                near(src).start()

            @pl.when((core == c) & inner())
            def _():
                middle(src).start()

        start(biases())
        own_bias().start()

    @pl.when(step < row_steps)
    def _():
        parts = []
        for j in range(FPS):
            frame = step * FPS + j
            p = shifted(clip_ref, frame, clip_ref[0:1, :].astype(F32), frame >= 0)
            p_ref[j] = p.astype(BF)
            xhat, _ = normed(p)
            parts.append((xhat * row_of(gain_ref) + row_of(shift_ref)).astype(BF))
            g_ref[j] = shifted(cot_ref, frame, cot_ref[0:1, :].astype(F32), frame == 0).astype(BF)
        h = jnp.concatenate(parts, axis=0)
        h_ref[...] = h.reshape(FPS, ROWS, WIDTH)
        project(h, w_ref, bias_ref, z_ref)
        z_buf[pl.ds(step * FPS, FPS)] = z_ref[...]

    @pl.when(step >= row_steps)
    def _():
        at = pl.multiple_of((step - row_steps) * TILE, TILE)
        time_attention(z_buf[:, pl.ds(at, TILE), :], o_ref, a_ref)

    @pl.when(step == steps - 1)
    def _():
        near(win_ref).wait()
        wait(biases())
        own_bias().wait()

        @pl.when(inner())
        def _():
            middle(win_ref).wait()


def project(h, w_ref, bias_ref, z_ref):
    for which in range(3):
        cols = slice(which * WIDTH, (which + 1) * WIDTH)
        z = nn(h, w_ref[:, cols])
        if which != 1:
            z = z + bias_ref[which // 2 : which // 2 + 1].astype(F32)
        z = z.astype(BF)
        if which == 0:
            z = z * jnp.asarray(HEAD_DIM**-0.5, BF)
        z_ref[:, :, cols] = z.reshape(FPS, ROWS, WIDTH)


def time_attention(z, o_ref, a_ref):
    z = z.reshape(FRAMES * TILE, 3 * WIDTH)
    row = lax.broadcasted_iota(jnp.int32, (GROUP * FRAMES * TILE, FRAMES * TILE), 0)
    col = lax.broadcasted_iota(jnp.int32, (GROUP * FRAMES * TILE, FRAMES * TILE), 1)
    same = (row % TILE) == (col % TILE)
    scores = [nt(head_masked(z[:, group_cols(g, 0)]), z[:, group_cols(g, 1)]) for g in range(GROUPS)]
    probs = [softmax(jnp.where(same, s, NEG)) for s in scores]
    mixed = [nn(probs[g], z[:, group_cols(g, 2)]) for g in range(GROUPS)]
    for g in range(GROUPS):
        a_ref[0, g] = probs[g]
        o = head_select(mixed[g]).astype(BF)
        o_ref[:, :, g * GW : (g + 1) * GW] = o.reshape(FRAMES, TILE, GW)


def space_kernel(
    p_ref, ot_ref, offset_ref, gain_ref, shift_ref, out_ref, bias_ref, wt_ref, w_ref, wo_ref,
    near_ref, held_ref,
    full_ref, h_ref, z_ref, a_ref, o_ref, x_ref, cls_ref, near_x_ref, near_s_ref, near_xs_ref, far_ref, mid_ref,
    sems,
):
    step = pl.program_id(0)

    def across():
        return send(near_ref, near_x_ref, sems, 0, "wide", 2)

    def siblings():
        return [send(near_ref, near_s_ref, sems, 1, "wide", 1), send(near_x_ref, near_xs_ref, sems, 2, "wide", 1)]

    def outward():
        return send(held_ref, far_ref, sems, 3, "narrow", 1)

    def middle():
        return send(near_ref, mid_ref, sems, 4, "narrow", 3)

    def keep():
        return pltpu.make_async_copy(held_ref, far_ref, sems.at[0, 5])

    @pl.when(step == 0)
    def _():
        greet(RING)
        across().start()

        @pl.when(inner())
        def _():
            outward().start()
            middle().start()
            keep().start()

    @pl.when(step == pl.num_programs(0) - 1)
    def _():
        across().wait()
        start(siblings())

    p = p_ref[...].reshape(STEP, WIDTH).astype(F32)
    mixed = p + nn(ot_ref[...].reshape(STEP, WIDTH), wt_ref[...]) + row_of(offset_ref)
    row = lax.broadcasted_iota(jnp.int32, (STEP, WIDTH), 0) % ROWS
    full = jnp.where(row == CLASS, p, mixed)
    full_ref[...] = full.reshape(FPS, ROWS, WIDTH)
    xhat, _ = normed(full)
    h = (xhat * row_of(gain_ref) + row_of(shift_ref)).astype(BF)
    h_ref[...] = h.reshape(FPS, ROWS, WIDTH)
    project(h, w_ref, bias_ref, z_ref)
    key = lax.broadcasted_iota(jnp.int32, (GROUP * ROWS, ROWS), 1)
    for j in range(FPS):
        units = [(j, g) for g in range(GROUPS)]
        scores = [nt(head_masked(z_ref[j, :, group_cols(g, 0)]), z_ref[j, :, group_cols(g, 1)]) for j, g in units]
        probs = [softmax(jnp.where(key <= CLASS, s, NEG)) for s in scores]
        mixed = [nn(a, z_ref[j, :, group_cols(g, 2)]) for a, (j, g) in zip(probs, units)]
        for a, m, (j, g) in zip(probs, mixed, units):
            a_ref[j, g] = a
            o_ref[j, :, g * GW : (g + 1) * GW] = head_select(m).astype(BF)
    y = nn(o_ref[...].reshape(STEP, WIDTH), wo_ref[...]) + row_of(out_ref)
    x_ref[...] = (full + y).reshape(FPS, ROWS, WIDTH)
    for j in range(FPS):
        at = j * ROWS + CLASS - CLASS % 8
        cls_ref[j] = y[at : at + 8]

    @pl.when(step == pl.num_programs(0) - 1)
    def _():
        wait(siblings())

        @pl.when(inner())
        def _():
            outward().wait_send()
            middle().wait()
            keep().wait()

        @pl.when(jnp.logical_not(inner()))
        def _():
            outward().wait_recv()


def mlp_kernel(first_call, *refs):
    refs = list(refs)

    def take(n):
        got = refs[:n]
        del refs[:n]
        return got

    step = pl.program_id(0)
    me = own_index()
    core = lax.rem(lax.axis_index("wide"), 2)
    row_steps = FRAMES // FPS
    chained = not first_call and hosted()
    x_ref, cls_ref, p_ref, g_ref, gain_ref, shift_ref, out_bias_ref, rows_ref = take(8)
    if first_call:
        win_ref, wout_ref = take(2)
        near_refs = take(4)
        far_ref, held_ref = take(2)
        h_ref, acc_ref, dh_ref, own_ref, oth_ref, gb_ref = take(6)
        far_x_ref, far_s_ref, far_xs_ref, far2_ref, far2_x_ref, far2_s_ref, far2_xs_ref = take(7)
        swap = jnp.int32(0)
        slots = [(1, *near_refs)]
    else:
        h_ref, acc_ref, dh_ref = take(3)
        slots = [(0, *take(4)), (1, *take(4))]
        near_refs = take(2) if chained else None
        out_ref, dx_ref, own_ref, oth_ref, gv_ref, gb_ref = take(6)
        near_out = take(1)[0] if chained else None
        swap = inner().astype(jnp.int32)
    w_buf, h_buf, g_buf, act_buf, dpre_buf, t_buf, sem = take(7)
    if first_call:
        (rsems,) = take(1)

        def move(k):
            return send(*((far_ref, far_x_ref), (far2_ref, far2_x_ref))[k], rsems, k, "wide", 2)

        def siblings(k):
            pairs = (((far_ref, far_s_ref), (far_x_ref, far_xs_ref)), ((far2_ref, far2_s_ref), (far2_x_ref, far2_xs_ref)))
            return [send(*pair, rsems, 2 + 2 * k + i, "wide", 1) for i, pair in enumerate(pairs[k])]

        def outward():
            return send(held_ref, far2_ref, rsems, 6, "narrow", 1)

        def keep():
            return pltpu.make_async_copy(held_ref, far2_ref, rsems.at[0, 7])

        @pl.when(step == 0)
        def _():
            greet(RING)
            move(0).start()

            @pl.when(inner())
            def _():
                outward().start()
                keep().start()

        @pl.when(step == 2)
        def _():
            @pl.when(inner())
            def _():
                keep().wait()

            @pl.when(jnp.logical_not(inner()))
            def _():
                outward().wait_recv()

            move(1).start()
            move(0).wait()
            start(siblings(0))

        @pl.when(step == row_steps + 1)
        def _():
            move(1).wait()
            start(siblings(1))

            @pl.when(inner())
            def _():
                outward().wait_send()

    else:
        (out_buf,) = take(1)
    if chained:
        plane = PlaneSum(*near_refs, *take(5))
        rz, zsem = take(2)

        def line_copies():
            return [send(plane.got.at[0, m, pl.ds(96, 96)], rz.at[m], zsem, m, "narrow", 1) for m in range(2)]

        def near_total():
            wait(line_copies())
            for m in range(2):
                near_out[m] = plane.got[0, m, 0:96].astype(F32) + rz[m].astype(F32)

        def line_stage():
            plane.stage3()
            start(line_copies())

        def begin():
            greet()
            plane.stage0()

    def checkpoint():
        if chained:
            for k, action in {0: begin, 1: plane.stage1, 3: plane.stage2}.items():
                pl.when(step == k)(action)

    @pl.when(step == 0)
    def _():
        if not first_call:
            gv_ref[...] = jnp.zeros_like(gv_ref)
        gb_ref[...] = jnp.zeros_like(gb_ref)

    part = half_rows()
    size = WIDTH // 2
    other = pl.ds(pl.multiple_of(size - part.start, size), size)

    def fetches(slot, mine, mine_x, sib, sib_x, c):
        into = ((mine, mine_x), (sib, sib_x)) if c == 0 else ((sib, sib_x), (mine, mine_x))
        return [
            pltpu.make_async_copy(into[m][i], w_buf.at[m, slot, rows], sem.at[4 * slot + 2 * m + i])
            for m in range(2) for i, rows in enumerate((part, other))
        ]

    @pl.when(step == 0)
    def _():
        for c in range(2):

            @pl.when(core == c)
            def _():
                for entry in slots:
                    start(fetches(*entry, c))

    def arrived(slot):
        for entry in slots:
            if entry[0] == slot:

                @pl.when(step == 0)
                def _():
                    wait(fetches(*entry, 0))

    def weight(m, slot):
        if first_call and slot == 0:
            return (win_ref, wout_ref)[m][...]
        return w_buf[m, slot]

    def bias(slot):
        if first_call:
            return rows_ref[slot, 0:1].astype(F32)
        return rows_ref[2 + jnp.bitwise_xor(slot, swap), 0:1].astype(F32)

    @pl.when(step < row_steps)
    def _():
        at = pl.ds(pl.multiple_of(step * STEP, STEP), STEP)
        x = x_ref[...].reshape(STEP, WIDTH)
        mean_cls = jnp.mean(cls_ref[:, CLASS % 8, :], axis=0, keepdims=True)
        first = p_ref[0, CLASS % TILE : CLASS % TILE + 1, :].astype(F32) + mean_cls
        row = lax.broadcasted_iota(jnp.int32, (STEP, WIDTH), 0) % ROWS
        x = jnp.where(row == CLASS, first, x)
        xhat, scale = normed(x)
        g = g_ref[...].reshape(STEP, WIDTH)
        if first_call:
            h = (xhat * row_of(gain_ref) + row_of(shift_ref)).astype(BF)
            h_ref[...] = h.reshape(FPS, ROWS, WIDTH)
            acc = x + row_of(out_bias_ref)
            dh = None
        else:
            h = h_ref[...].reshape(STEP, WIDTH)
            acc = acc_ref[...].reshape(STEP, WIDTH)
            dh = dh_ref[...].reshape(STEP, WIDTH)
        h_buf[at, :] = h
        g_buf[at, :] = g
        for s in range(2):
            arrived(s)
            if s == 1:
                checkpoint()
            cols = slice(s * WIDTH, (s + 1) * WIDTH)
            pre = nn(h, weight(0, s)) + bias(s)
            cdf = 0.5 + 0.5 * lax.erf(pre * (0.5**0.5))
            act = (pre * cdf).astype(BF)
            slope = cdf + pre * (jnp.exp(-0.5 * pre * pre) * 0.3989422804014327)
            act_buf[at, cols] = act
            dpre = (nt(g, weight(1, s)) * slope).astype(BF)
            dpre_buf[at, cols] = dpre
            gb_ref[s : s + 1, :] += colsum(dpre)
            acc = acc + nn(act, weight(1, s))
            back = nt(dpre, weight(0, s))
            dh = back if dh is None else dh + back
        if first_call:
            acc_ref[...] = acc.reshape(FPS, ROWS, WIDTH)
            dh_ref[...] = dh.reshape(FPS, ROWS, WIDTH)
        else:
            for k in range(row_steps):

                @pl.when(step == k)
                def _():
                    if k == 0:
                        out_buf[0:1, :] = acc[CLASS : CLASS + 1]
                    for j in range(FPS):
                        start = 1 + (k * FPS + j) * PATCHES
                        out_buf[start : start + PATCHES, :] = acc[j * ROWS : j * ROWS + PATCHES]

            gf = g.astype(F32)
            dx_ref[...] = (gf + norm_back(dh, xhat, scale, row_of(gain_ref))).reshape(FPS, ROWS, WIDTH)
            gv_ref[0:1] += colsum(dh * xhat)
            gv_ref[1:2] += colsum(dh)
            gv_ref[2:3] += colsum(gf)

    def matrix(unit, left_ref, right_ref):
        t_buf[...] = left_ref[...].T
        for s in range(2):
            got = nn(t_buf[...], right_ref[:, s * WIDTH : (s + 1) * WIDTH]).astype(BF)
            for w in range(CHUNKS):
                put_chunk(own_ref, oth_ref, me, w, 2 * unit + jnp.bitwise_xor(s, swap), got[w * 96 : (w + 1) * 96])

    @pl.when(step == row_steps)
    def _():
        matrix(0, h_buf, dpre_buf)
        if not first_call:
            out_ref[0] = out_buf[...].astype(BF)

    @pl.when(step == row_steps + 1)
    def _():
        if chained:
            line_stage()
        matrix(1, g_buf, act_buf)
        if chained:
            near_total()
        if first_call:
            wait(siblings(0))
            wait(siblings(1))


def put_chunk(own_ref, oth_ref, me, w, unit, value):
    rel = jnp.bitwise_xor(me, w)
    place = rel // 2
    for c, ref in enumerate((own_ref, oth_ref)):

        @pl.when(rel % 2 == c)
        def _():
            ref[place, unit] = value


def space_back_kernel(*refs):
    refs = list(refs)

    def take(n):
        got = refs[:n]
        del refs[:n]
        return got

    dx_ref, dcls_ref, full_ref, z_ref, a_ref, gain_ref, wo_ref, w_ref, wt_ref = take(9)
    far_refs = take(2) if hosted() else None
    dy_ref, dz_ref, df_ref, dyt_ref, dot_ref, gv_ref = take(6)
    far_out = take(1)[0] if hosted() else None
    (do_ref,) = take(1)
    step = pl.program_id(0)
    plane = PlaneSum(*far_refs, *take(5)) if hosted() else None

    def begin():
        greet(PLANE)
        plane.stage0()

    def finish():
        plane.stage3()
        far_out[...] = plane.got[0]

    def checkpoint(plan):
        if hosted():
            for k, action in plan.items():
                pl.when(step == k)(action)

    @pl.when(step == 0)
    def _():
        gv_ref[...] = jnp.zeros_like(gv_ref)

    dx = dx_ref[...].reshape(STEP, WIDTH)
    row = lax.broadcasted_iota(jnp.int32, (STEP, WIDTH), 0) % ROWS
    dcls = dcls_ref[0, CLASS % 8 : CLASS % 8 + 1, :] * (1.0 / FRAMES)
    dy = jnp.where(row == CLASS, dcls, jnp.where(row < CLASS, dx, 0.0)).astype(BF)
    dy_ref[...] = dy.reshape(FPS, ROWS, WIDTH)
    gv_ref[0:1, :WIDTH] += colsum(dy)
    do_ref[...] = nt(dy, wo_ref[...]).astype(BF)
    for j in range(FPS):
        if j > 0:
            checkpoint({0: begin, 1: plane.stage1} if hosted() else {})
        units = [(j, g) for g in range(GROUPS)]
        dos = [head_masked(do_ref[j * ROWS : (j + 1) * ROWS, g * GW : (g + 1) * GW]) for j, g in units]
        das = [nt(do, z_ref[j, :, group_cols(g, 2)]) for do, (j, g) in zip(dos, units)]
        dvs = [tn(a_ref[j, g], do) for do, (j, g) in zip(dos, units)]
        dss = [score_back(a_ref[j, g], da) for da, (j, g) in zip(das, units)]
        for dv, (j, g) in zip(dvs, units):
            dz_ref[j, :, group_cols(g, 2)] = dv.astype(BF)
        dqs = [nn(ds, z_ref[j, :, group_cols(g, 1)]) for ds, (j, g) in zip(dss, units)]
        dks = [tn(ds, head_masked(z_ref[j, :, group_cols(g, 0)])) for ds, (j, g) in zip(dss, units)]
        for dq, dk, (j, g) in zip(dqs, dks, units):
            dz_ref[j, :, group_cols(g, 0)] = (head_select(dq) * HEAD_DIM**-0.5).astype(BF)
            dz_ref[j, :, group_cols(g, 1)] = dk.astype(BF)
    dz = dz_ref[...].reshape(STEP, 3 * WIDTH)
    gv_ref[1:2, :] += colsum(dz)
    dh = nt(dz, w_ref[...])
    xhat, scale = normed(full_ref[...].reshape(STEP, WIDTH))
    gv_ref[2:3, :WIDTH] += colsum(dh * xhat)
    gv_ref[3:4, :WIDTH] += colsum(dh)
    df = dx + norm_back(dh, xhat, scale, row_of(gain_ref))
    df_ref[...] = df.reshape(FPS, ROWS, WIDTH)
    dyt = jnp.where(row < CLASS, df, 0.0).astype(BF)
    dyt_ref[...] = dyt.reshape(FPS, ROWS, WIDTH)
    gv_ref[4:5, :WIDTH] += colsum(dyt)
    dot_ref[...] = nt(dyt, wt_ref[...]).astype(BF).reshape(FPS, ROWS, WIDTH)
    checkpoint({2: plane.stage2, 3: finish} if hosted() else {})


def put_rows(own_ref, oth_ref, me, w, start, value):
    rel = jnp.bitwise_xor(me, w)
    place = rel // 2
    for c, ref in enumerate((own_ref, oth_ref)):

        @pl.when(rel % 2 == c)
        def _():
            ref[place, start : start + value.shape[0], :] = value


PIECE = (CHUNKS // 2, 384, WIDTH)
QKV_ROWS = 288
PROJ_ROWS = 192


def time_back_kernel(*refs):
    refs = list(refs)

    def take(n):
        got = refs[:n]
        del refs[:n]
        return got

    z_ref, a_ref, do_ref, h_any, dzs_ref, hs_ref = take(6)
    near_ref, far_ref = take(2) if hosted() else (None, None)
    dz_ref, own_ref, oth_out = take(3)
    parts_ref, fc_ref = take(2) if hosted() else (None, None)
    s_own, s_oth = (None, None) if hosted() else take(2)
    dz_buf, h_buf, h_sem = take(3)
    oth_ref = oth_out
    chunks = ROWS // TILE
    step = pl.program_id(0) - 2
    me = own_index()
    half = CHUNKS // 2

    def load():
        return pltpu.make_async_copy(h_any, h_buf, h_sem)

    if hosted():
        s_own, s_oth = take(2)
        plane = PlaneSum(halves_ref(s_own), halves_ref(s_oth), *take(5))
        rz, zsem, oth_ref, x_sems = take(4)

        def line_copies():
            return [
                send(far_ref.at[m, pl.ds(96 * i, 96)], rz.at[m, i], zsem, 2 * m + i, "narrow", 2 + i)
                for m in range(2) for i in range(2)
            ]

        def exchange(k):
            base = pl.multiple_of(2 * jnp.bitwise_xor(me // 4, k), 2)
            place = pl.ds(base, 2)
            return send(oth_ref.at[place], oth_out.at[place], x_sems, k, "wide", 1)

        @pl.when(step == -2)
        def _():
            greet()
            start(line_copies())

    for k in range(2):

        @pl.when(step == k - 2)
        def _():
            got = tn(dzs_ref[...], hs_ref[...]).astype(BF)
            for i in range(half):
                put_rows(s_own, s_oth, me, k * half + i, 0, got[i * QKV_ROWS : (i + 1) * QKV_ROWS])

    if hosted():
        pl.when(step == 0)(plane.stage0)
        pl.when(step == 4)(plane.stage1)
        pl.when(step == chunks - 1)(plane.stage2)

    pl.when(step == 0)(lambda: load().start())

    @pl.when((step >= 0) & (step < chunks))
    def _():
        z = z_ref[...].reshape(FRAMES * TILE, 3 * WIDTH)
        dot = do_ref[...].reshape(FRAMES * TILE, WIDTH)
        groups = range(GROUPS)
        dos = [head_masked(dot[:, g * GW : (g + 1) * GW]) for g in groups]
        das = [nt(dos[g], z[:, group_cols(g, 2)]) for g in groups]
        dvs = [tn(a_ref[0, g], dos[g]) for g in groups]
        dss = [score_back(a_ref[0, g], das[g]) for g in groups]
        dqs = [nn(dss[g], z[:, group_cols(g, 1)]) for g in groups]
        dks = [tn(dss[g], head_masked(z[:, group_cols(g, 0)])) for g in groups]
        for g in groups:
            for which, v in enumerate((head_select(dqs[g]) * HEAD_DIM**-0.5, dks[g], dvs[g])):
                dz_ref[:, :, group_cols(g, which)] = v.astype(BF).reshape(FRAMES, TILE, GW)
        dz_buf[:, pl.ds(pl.multiple_of(step * TILE, TILE), TILE), :] = dz_ref[...]

    pl.when(step == chunks)(lambda: load().wait())
    for k in range(2):

        @pl.when(step == chunks + k)
        def _():
            left = dz_buf[:, :, k * half * 288 : (k + 1) * half * 288]
            got = tn(left.reshape(FRAMES * ROWS, half * 288), h_buf[...]).astype(BF)
            for i in range(half):
                put_rows(own_ref, oth_ref, me, k * half + i, 0, got[i * 288 : (i + 1) * 288])
            if hosted():
                exchange(k).start()

    if hosted():

        @pl.when(step == chunks + 1)
        def _():
            wait(line_copies())
            for m in range(2):
                fc_ref[m] = near_ref[m] + rz[m, 0].astype(F32) + rz[m, 1].astype(F32)
            plane.stage3()
            cut_columns(plane.got, parts_ref)
            for k in range(2):
                exchange(k).wait()


def halves_ref(ref):
    return ref.reshape(4, 2, ref.shape[1] // 2, WIDTH)


def cut_columns(got, parts_ref):
    size = WIDTH // parts_ref.shape[0]
    for n in range(parts_ref.shape[0]):
        cols = slice(n * size, (n + 1) * size)
        parts_ref[n] = jnp.concatenate([got[0, 0, :, cols], got[0, 1, :, cols]], axis=1)


def turned(total):
    size = total.shape[1] // 2
    return jnp.concatenate([total[:, :size].T, total[:, size:].T], axis=1)


VEC_ROWS = 32


def time_out_kernel(*refs):
    refs = list(refs)

    def take(n):
        got = refs[:n]
        del refs[:n]
        return got

    dz_ref, p_ref, df_ref, gain_ref, w_ref = take(5)
    grads_in = take(4)
    if hosted():
        time_refs = take(2)
        s_parts, gvm_ref, gvs_ref, gba_ref, gbb_ref = take(5)
    dp_ref, gv_ref = take(2)
    if hosted():
        sq_ref, sp_ref, tp_ref, tq_ref, share_ref, hid_ref = take(6)
        p_own, p_oth = take(2)
    else:
        p_own, p_oth = take(2)
    dp_buf, dp_sem, g_bufs, g_sems = take(4)
    step = pl.program_id(0)
    row_steps = FRAMES // FPS
    line = lax.axis_index("narrow")
    me = own_index()
    if hosted():
        plane = PlaneSum(*time_refs, *take(5))
        p_plane = PlaneSum(halves_ref(p_own), halves_ref(p_oth), *take(5))
        parts, p_parts = take(2)
        s_line = LineSum(s_parts, *take(2))
        t_line = LineSum(parts, *take(2))
        p_line = LineSum(p_parts, *take(2))
        vbuf, vrecv, vlow, vlow_recv, vsem, lbuf, lrecv, lsem = take(8)

        def early(k):
            axis, bit = (("wide", 1), ("wide", 2), ("wide", 4))[k]
            return send(vbuf, vrecv.at[k], vsem, k, axis, bit)

        def early_add(k):
            early(k).wait()
            vbuf[...] += vrecv[k]

        def early_line():
            return [send(vlow, vlow_recv.at[b - 1], vsem, 2 + b, "narrow", b) for b in (1, 2, 3)]

        def late_wide():
            return [send(lbuf, lrecv.at[b - 1], lsem, b - 1, "wide", b) for b in range(1, CHUNKS)]

        def late_line():
            return [send(lrecv.at[0], lrecv.at[6 + b], lsem, 6 + b, "narrow", b) for b in (1, 2, 3)]

        @pl.when(step == 0)
        def _():
            start(plane.load_both())
            greet(ALL_WIDE + LINE)
            start(s_line.copies())
            plane.arrived()
            vbuf[...] = jnp.zeros_like(vbuf)
            vbuf[0:3, :] = gvm_ref[0:3, :]
            for i, r, c in ((3, 0, 0), (4, 1, 0), (5, 1, 2), (6, 2, 0), (7, 3, 0), (8, 4, 0)):
                vbuf[i : i + 1, :] = gvs_ref[r : r + 1, c * WIDTH : (c + 1) * WIDTH]
            low = line < 2
            places = (line, jnp.bitwise_xor(line, 1), jnp.where(low, 2, 1), jnp.where(low, 3, 0))
            for place, (ref, r) in zip(places, ((gba_ref, 0), (gba_ref, 1), (gbb_ref, 0), (gbb_ref, 1))):
                vbuf[pl.ds(13 + place, 1), :] = ref[r : r + 1, :]
            early(0).start()

        @pl.when(step == 1)
        def _():
            early_add(0)
            early(1).start()

        @pl.when(step == 3)
        def _():
            plane.stage2()
            p_plane.stage0()
            early_add(1)
            early(2).start()

        @pl.when(step == 4)
        def _():
            p_plane.stage1()
            plane.stage3()
            cut_columns(plane.got, parts)
            start(t_line.copies())
            early_add(2)
            vlow[...] = vbuf[...].astype(BF)
            start(early_line())

    def load(i):
        return pltpu.make_async_copy(grads_in[i], g_bufs.at[i], g_sems.at[i])

    def saves(k):
        rows = pl.ds(1 + k * FPS * PATCHES, FPS * PATCHES)
        return pltpu.make_async_copy(dp_buf.at[rows], dp_ref.at[rows], dp_sem.at[k])

    def save_class():
        return pltpu.make_async_copy(dp_buf.at[pl.ds(0, 1)], dp_ref.at[pl.ds(0, 1)], dp_sem.at[row_steps])

    @pl.when(step == 0)
    def _():
        start([load(i) for i in range(4)])
        gv_ref[...] = jnp.zeros_like(gv_ref)
        dp_buf[0:1, 0, :] = jnp.zeros((1, WIDTH), F32)

    for k in range(2):

        @pl.when(step == 1 + k)
        def _():
            for i in (2 * k, 2 * k + 1):
                load(i).wait()
            got = tn(g_bufs[2 * k], g_bufs[2 * k + 1]).astype(BF)
            for w in range(CHUNKS):
                put_rows(p_own, p_oth, me, w, 96 * k, got[w * 96 : (w + 1) * 96])

    @pl.when((step == 0) | ((step > 2) & (step < row_steps + 2)))
    def _():
        dz = dz_ref[...].reshape(STEP, 3 * WIDTH)
        gv_ref[0:1, :] += colsum(dz)
        dh = nt(dz, w_ref[...])
        xhat, scale = normed(p_ref[...].reshape(STEP, WIDTH).astype(F32))
        gv_ref[1:2, :WIDTH] += colsum(dh * xhat)
        gv_ref[2:3, :WIDTH] += colsum(dh)
        df = df_ref[...].reshape(STEP, WIDTH)
        dp = df + norm_back(dh, xhat, scale, row_of(gain_ref))
        for j in range(FPS):
            dp_buf[0:1, 0, :] += df[j * ROWS + CLASS : j * ROWS + CLASS + 1]
        for k in range(row_steps):

            @pl.when(step == (0 if k == 0 else k + 2))
            def _():
                for j in range(FPS):
                    begin = 1 + (k * FPS + j) * PATCHES
                    dp_buf[begin : begin + PATCHES, 0, :] = dp[j * ROWS : j * ROWS + PATCHES]
                saves(k).start()

    @pl.when(step == row_steps + 1)
    def _():
        save_class().start()

    if hosted():

        @pl.when(step == row_steps + 2)
        def _():
            lbuf[...] = jnp.zeros_like(lbuf)
            for i, r, c in ((0, 0, 0), (1, 0, 2), (2, 1, 0), (3, 2, 0)):
                lbuf[i : i + 1, :] = gv_ref[r : r + 1, c * WIDTH : (c + 1) * WIDTH]
            start(late_wide())
            p_plane.stage2()
            sq_ref[...] = turned(s_line.result())
            wait(late_wide())
            late = lbuf[...]
            for b in range(CHUNKS - 1):
                late = late + lrecv[b]
            lrecv[0] = late
            start(late_line())
            p_plane.stage3()
            cut_columns(p_plane.got, p_parts)
            start(p_line.copies())
            wait(early_line())
            vectors = vbuf[...] + vlow_recv[0].astype(F32) + vlow_recv[1].astype(F32) + vlow_recv[2].astype(F32)
            tq_ref[...] = turned(t_line.result())
            wait(late_line())
            late = lrecv[0] + lrecv[7] + lrecv[8] + lrecv[9]
            vectors = jnp.concatenate([vectors[0:9], late[0:4], vectors[13:]], axis=0)
            size = WIDTH // 4
            share = vectors[:, :size]
            hidden = vectors[13:14, :]
            for n in range(1, 4):
                share = jnp.where(line == n, vectors[:, n * size : (n + 1) * size], share)
                hidden = jnp.where(line == n, vectors[13 + n : 14 + n, :], hidden)
            share_ref[...] = share
            hid_ref[...] = hidden
            total = turned(p_line.result())
            sp_ref[...] = total[:, :96]
            tp_ref[...] = total[:, 96:]

    @pl.when(step == pl.num_programs(0) - 1)
    def _():
        for k in range(row_steps):
            saves(k).wait()
        save_class().wait()


VECTORS = (11, 12, (9, 11), 8, 6, 7, (4, 6), 3, 0, 1, 2)


def outputs_kernel(share_ref, hid_ref, *refs):
    count = len(refs) - len(VECTORS) - 1
    ins, outs = refs[: count // 2], refs[count // 2 :]
    for src, dst in zip(ins, outs):
        dst[...] = src[...]
    outs = outs[len(ins) :]
    for rows, dst in zip(VECTORS, outs):
        if isinstance(rows, tuple):
            dst[...] = share_ref[rows[0] : rows[1], :]
        else:
            dst[...] = share_ref[rows : rows + 1, :].reshape(dst.shape)
    outs[-1][...] = hid_ref[0:1, :].reshape(outs[-1].shape)


def flip(value, axis, bit):
    return lax.ppermute(value, axis, [(i, i ^ bit) for i in range(lax.axis_size(axis))])


def unit_sum(own, oth):
    both = jnp.stack([own, oth], axis=1).reshape(CHUNKS, 4, 96, WIDTH)
    both = both.transpose(1, 0, 2, 3).reshape(4, WIDTH, WIDTH)
    both = lax.psum_scatter(both, "wide", scatter_dimension=1, tiled=True)
    return both.reshape(2, 2, -1, WIDTH)


def piece_sum(own, oth, sizes, me):
    both = jnp.stack([own, oth], axis=1).reshape(CHUNKS, -1, WIDTH)
    found, at = [], 0
    for size in sizes:
        rows = both[:, at * 96 : (at + size) * 96].reshape(size * WIDTH, WIDTH)
        at += size
        rows = lax.psum_scatter(rows, "wide", scatter_dimension=0, tiled=True)
        parts = rows.T.reshape(lax.axis_size("narrow"), -1, rows.shape[0])
        found.append(line_sum(parts, me))
    return found


def line_sum(parts, me):
    total = lax.dynamic_index_in_dim(parts, me, 0, False).astype(F32)
    for bit in (1, 2, 3):
        other = lax.dynamic_index_in_dim(parts, jnp.bitwise_xor(me, bit), 0, False)
        total = total + flip(other, "narrow", bit).astype(F32)
    return total


def local(
    video_clips, time_gain, time_shift, time_qkv, time_bias, time_proj, time_offset,
    space_gain, space_shift, space_qkv, space_bias, space_proj, space_offset,
    mlp_gain, mlp_shift, fc_in, in_bias, fc_out, out_bias, cotangent,
):
    slices = lax.axis_size("narrow")
    tokens = video_clips.shape[1]
    clip = video_clips[0]
    cot = cotangent[0]
    vec = pl.BlockSpec((WIDTH,), lambda *i: (0,), pipeline_mode=pl.Buffered(1))
    me_n = lax.axis_index("narrow")
    any_ref = pl.BlockSpec(memory_space=pl.ANY)
    message = (any_ref, jax.ShapeDtypeStruct((WIDTH // 2, WIDTH), BF))
    bias_rows = (any_ref, jax.ShapeDtypeStruct((4, TILE, WIDTH), BF))

    chunks = ROWS // TILE
    a_time = jax.ShapeDtypeStruct((chunks, GROUPS, GROUP * FRAMES * TILE, FRAMES * TILE), BF)

    def a_chunk(first):
        return pl.BlockSpec((1, *a_time.shape[1:]), lambda i: (jnp.clip(i - first, 0, chunks - 1), 0, 0, 0))

    a_space = (pl.BlockSpec((FPS, GROUPS, GROUP * ROWS, ROWS), lambda i: (i, 0, 0, 0)),
               jax.ShapeDtypeStruct((FRAMES, GROUPS, GROUP * ROWS, ROWS), BF))

    last = FRAMES // FPS - 1
    steps = last + 1
    rows = FRAMES * ROWS

    def row_in(width):
        return pl.BlockSpec((FPS, ROWS, width), lambda i: (jnp.minimum(i, last), 0, 0))

    def row_out(width, dtype):
        return row_in(width), jax.ShapeDtypeStruct((FRAMES, ROWS, width), dtype)

    def chunk(width, first):
        return pl.BlockSpec((FRAMES, TILE, width), lambda i: (0, jnp.clip(i - first, 0, chunks - 1), 0))

    def chunk_out(width, first):
        return chunk(width, first), jax.ShapeDtypeStruct((FRAMES, ROWS, width), BF)

    p, g, ht, zt, ot, at, near, held, biases = call(
        time_kernel, "time", (steps + chunks,),
        [whole(tokens, WIDTH), whole(tokens, WIDTH), vec, vec, whole(2, WIDTH), whole(WIDTH, 3 * WIDTH),
         any_ref, any_ref, vec],
        [row_out(WIDTH, BF), row_out(WIDTH, BF), row_out(WIDTH, BF), row_out(3 * WIDTH, BF),
         chunk_out(WIDTH, steps), (a_chunk(steps), a_time)] + [message] * 2 + [bias_rows],
        scratch=[pltpu.VMEM((FRAMES, ROWS, 3 * WIDTH), BF), pltpu.VMEM((TILE, WIDTH), BF),
                 pltpu.SemaphoreType.DMA((2, 2)), pltpu.SemaphoreType.DMA((2, 4))],
        remote=1,
    )(clip, cot, time_gain, time_shift, time_bias, time_qkv, fc_in, fc_out, in_bias)
    full, hs, zs, a_s, o_s, xs, ycls, near_x, near_s, near_xs, far, held2 = call(
        space_kernel, "space", (steps,),
        [frames(WIDTH), frames(WIDTH), vec, vec, vec, vec, whole(2, WIDTH),
         whole(WIDTH, WIDTH), whole(WIDTH, 3 * WIDTH), whole(WIDTH, WIDTH)] + [any_ref] * 2,
        [frames_out(WIDTH, F32), frames_out(WIDTH, BF), frames_out(3 * WIDTH, BF), a_space,
         frames_out(WIDTH, BF), frames_out(WIDTH, F32),
         (pl.BlockSpec((FPS, 8, WIDTH), lambda i: (i, 0, 0)), jax.ShapeDtypeStruct((FRAMES, 8, WIDTH), F32))]
        + [message] * 5,
        scratch=[pltpu.SemaphoreType.DMA((2, 6))],
        remote=2,
    )(p, ot, time_offset, space_gain, space_shift, space_offset, space_bias, time_proj, space_qkv, space_proj, near, held)
    unit_shape = (CHUNKS // 2, 4, 96, WIDTH)
    units = [(whole(*unit_shape), jax.ShapeDtypeStruct(unit_shape, BF))] * 2
    vec_out = [(whole(8, WIDTH), jax.ShapeDtypeStruct((8, WIDTH), F32))] * 2
    bufs = [
        pltpu.VMEM((2, 2, WIDTH, WIDTH), BF),
        pltpu.VMEM((rows, WIDTH), BF), pltpu.VMEM((rows, WIDTH), BF),
        pltpu.VMEM((rows, 2 * WIDTH), BF), pltpu.VMEM((rows, 2 * WIDTH), BF), pltpu.VMEM((WIDTH, rows), BF),
        pltpu.SemaphoreType.DMA((8,)),
    ]
    mlp_in = [row_in(WIDTH), whole(FRAMES, 8, WIDTH),
              pl.BlockSpec((1, TILE, WIDTH), lambda i: (0, CLASS // TILE, 0)), row_in(WIDTH), vec, vec, vec,
              whole(4, TILE, WIDTH)]
    mlp_args = (xs, ycls, p, g, mlp_gain, mlp_shift, out_bias, biases)
    hm, acc, dh, a_own, a_oth, gb_a, far_x, far_s, far_xs, far2, far2_x, far2_s, far2_xs = call(
        partial(mlp_kernel, True), "mlp_near", (last + 3,),
        mlp_in + [whole(WIDTH, WIDTH), whole(WIDTH, WIDTH)] + [any_ref] * 6,
        [row_out(WIDTH, BF), row_out(WIDTH, F32), row_out(WIDTH, F32)] + units + vec_out[:1] + [message] * 7,
        scratch=bufs + [pltpu.SemaphoreType.DMA((2, 8))],
        remote=3,
    )(*mlp_args, fc_in, fc_out, near, near_x, near_s, near_xs, far, held2)
    units_in = []
    near_out = []
    near_args = []
    near_scratch = []
    if hosted():
        units_in = [any_ref] * 2
        near_args = [halves(a_own), halves(a_oth)]
        near_out = [(whole(2, 96, WIDTH), jax.ShapeDtypeStruct((2, 96, WIDTH), F32))]
        near_scratch = PlaneSum.scratch(384) + [pltpu.VMEM((2, 96, WIDTH), BF), pltpu.SemaphoreType.DMA((2, 2))]
    layer_out, dxs, b_own, b_oth, gv_m, gb_b, *near_sum = call(
        partial(mlp_kernel, False), "mlp_far", (last + 3,),
        mlp_in + [row_in(WIDTH), row_in(WIDTH), row_in(WIDTH)] + [any_ref] * 8 + units_in,
        [(whole(1, tokens, WIDTH), jax.ShapeDtypeStruct((1, tokens, WIDTH), BF)), row_out(WIDTH, F32)]
        + units + vec_out + near_out,
        scratch=bufs + [pltpu.VMEM((tokens, WIDTH), F32)] + near_scratch,
        remote=4 if hosted() else None,
    )(*mlp_args, hm, acc, dh, far, far_x, far_s, far_xs, far2, far2_x, far2_s, far2_xs, *near_args)

    far_in, far_args, far_out, far_scratch = [], [], [], []
    if hosted():
        far_in = [any_ref] * 2
        far_args = [halves(b_own), halves(b_oth)]
        far_out = [(whole(2, 192, WIDTH), jax.ShapeDtypeStruct((2, 192, WIDTH), BF))]
        far_scratch = PlaneSum.scratch(384)
    dys, dzs, df, dyt, dot, gv_s, *far_sum = call(
        space_back_kernel, "space_back", (steps,),
        [frames(WIDTH), pl.BlockSpec((1, 8, WIDTH), lambda i: (0, CLASS // 8, 0)), frames(WIDTH),
         frames(3 * WIDTH), a_space[0], vec,
         whole(WIDTH, WIDTH), whole(WIDTH, 3 * WIDTH), whole(WIDTH, WIDTH)] + far_in,
        [frames_out(WIDTH, BF), frames_out(3 * WIDTH, BF), frames_out(WIDTH, F32),
         frames_out(WIDTH, BF), frames_out(WIDTH, BF),
         (whole(8, 3 * WIDTH), jax.ShapeDtypeStruct((8, 3 * WIDTH), F32))] + far_out,
        scratch=[pltpu.VMEM((STEP, WIDTH), BF)] + far_scratch,
        remote=5 if hosted() else None,
    )(dxs, dxs, full, zs, a_s, space_gain, space_proj, space_qkv, time_proj, *far_args)

    def flat(value):
        return value.reshape(rows, value.shape[-1])

    share = WIDTH // slices
    q_piece = (CHUNKS // 2, QKV_ROWS, WIDTH)
    q_out = (whole(*q_piece), jax.ShapeDtypeStruct(q_piece, BF))
    q_parts = (slices, QKV_ROWS // 2, 2 * WIDTH // slices)
    p_piece = (CHUNKS // 2, PROJ_ROWS, WIDTH)
    p_out = (whole(*p_piece), jax.ShapeDtypeStruct(p_piece, BF))
    p_parts = (slices, PROJ_ROWS // 2, 2 * WIDTH // slices)
    back_in, back_args, back_scratch = [], [], []
    back_out = [q_out] * 4
    if hosted():
        back_in = [whole(2, 96, WIDTH), any_ref]
        back_args = [near_sum[0], far_sum[0]]
        back_out = [q_out, (any_ref, q_out[1]), (whole(*q_parts), jax.ShapeDtypeStruct(q_parts, BF)),
                    (whole(2, 96, WIDTH), jax.ShapeDtypeStruct((2, 96, WIDTH), F32))]
        back_scratch = [pltpu.VMEM(q_piece, BF)] * 2 + PlaneSum.scratch(QKV_ROWS) + [
            pltpu.VMEM((2, 2, 96, WIDTH), BF), pltpu.SemaphoreType.DMA((2, 4)),
            pltpu.VMEM(q_piece, BF), pltpu.SemaphoreType.DMA((2, 2))]
    dzt, t_own, t_oth, *from_back = call(
        time_back_kernel, "time_back", (2 + chunks + 2,),
        [chunk(3 * WIDTH, 2), a_chunk(2), chunk(WIDTH, 2), any_ref,
         pl.BlockSpec((rows, 3 * WIDTH // 2), lambda i: (0, jnp.minimum(i, 1))), whole(rows, WIDTH)] + back_in,
        [chunk_out(3 * WIDTH, 2)] + back_out,
        scratch=[pltpu.VMEM((FRAMES, ROWS, 3 * WIDTH), BF), pltpu.VMEM((rows, WIDTH), BF), pltpu.SemaphoreType.DMA]
        + back_scratch,
        remote=7 if hosted() else None,
    )(zt, at, dot, flat(ht), flat(dzs), flat(hs), *back_args)

    def late(width):
        return pl.BlockSpec((FPS, ROWS, width), lambda i: (jnp.clip(i - 2, 0, last), 0, 0))

    out_in, out_args, out_scratch = [], [], []
    out_out = [p_out] * 2
    if hosted():
        out_in = [any_ref] * 2 + [whole(*q_parts), whole(8, WIDTH), whole(8, 3 * WIDTH)] + [whole(8, WIDTH)] * 2
        out_args = [halves(t_own), halves(t_oth), from_back[0], gv_m, gv_s, gb_a, gb_b]
        out_out = [
            (whole(*shape), jax.ShapeDtypeStruct(shape, F32))
            for shape in ((share, 288), (share, 96), (share, 96), (share, 288), (VEC_ROWS, share), (1, WIDTH))
        ]
        out_scratch = (
            PlaneSum.scratch(QKV_ROWS) + PlaneSum.scratch(PROJ_ROWS)
            + [pltpu.VMEM(q_parts, BF), pltpu.VMEM(p_parts, BF)]
            + LineSum.scratch(*q_parts[1:]) * 2 + LineSum.scratch(*p_parts[1:])
            + [pltpu.VMEM((VEC_ROWS, WIDTH), F32), pltpu.VMEM((3, VEC_ROWS, WIDTH), F32),
               pltpu.VMEM((VEC_ROWS, WIDTH), BF), pltpu.VMEM((3, VEC_ROWS, WIDTH), BF),
               pltpu.SemaphoreType.DMA((2, 6)), pltpu.VMEM((8, WIDTH), F32), pltpu.VMEM((10, 8, WIDTH), F32),
               pltpu.SemaphoreType.DMA((2, 10))]
        )
    own_scratch = [pltpu.VMEM((tokens, 1, WIDTH), F32), pltpu.SemaphoreType.DMA((steps + 1,)),
                   pltpu.VMEM((4, rows, WIDTH), BF), pltpu.SemaphoreType.DMA((4,))]
    p_scratch = [pltpu.VMEM(p_piece, BF)] * 2 if hosted() else []
    grad_clips, gv_t, *sums = call(
        time_out_kernel, "time_out", (steps + 2 + (1 if hosted() else 0),),
        [late(3 * WIDTH), late(WIDTH), late(WIDTH), vec, whole(WIDTH, 3 * WIDTH)] + [any_ref] * 4 + out_in,
        [(any_ref, jax.ShapeDtypeStruct((tokens, 1, WIDTH), F32)),
         (whole(8, 3 * WIDTH), jax.ShapeDtypeStruct((8, 3 * WIDTH), F32))] + out_out,
        scratch=p_scratch + own_scratch + out_scratch,
        remote=8 if hosted() else None,
    )(dzt, p, df, time_gain, time_qkv, flat(dys), flat(o_s), flat(dyt), flat(ot), *out_args)
    grad_clips = grad_clips.reshape(1, tokens, WIDTH)

    if hosted():
        fc = from_back[1]
        *matrices, mine, hidden_row = sums
        outs = [(whole(*m.shape), jax.ShapeDtypeStruct(m.shape, F32)) for m in matrices]
        for v in VECTORS:
            shape = (2, share) if isinstance(v, tuple) else (share,)
            outs.append((whole(*shape), jax.ShapeDtypeStruct(shape, F32)))
        outs.append((whole(WIDTH), jax.ShapeDtypeStruct((WIDTH,), F32)))
        s_qkv, s_proj, t_proj, t_qkv, *found = call(
            outputs_kernel, "outputs", (1,), [whole(*v.shape) for v in (mine, hidden_row, *matrices)], outs,
        )(mine, hidden_row, *matrices)
        tg, tsh, tb, to, sg, ssh, sb, so, mg, msh, ob, grad_in_bias = found
    else:
        near_part = unit_sum(a_own, a_oth)
        far_part = unit_sum(b_own, b_oth)
        fc = near_part[:, 0].astype(F32) + flip(near_part[:, 1], "narrow", 1).astype(F32)
        fc = fc + flip(far_part[:, 0], "narrow", 2).astype(F32) + flip(far_part[:, 1], "narrow", 3).astype(F32)
        (s_qkv,) = piece_sum(*from_back, (3,), me_n)
        s_proj, t_proj = piece_sum(*sums, (1, 1), me_n)
        (t_qkv,) = piece_sum(t_own, t_oth, (3,), me_n)
        vectors = jnp.concatenate(
            [gv_m[0:3], gv_s[0:1, :WIDTH], gv_s[1:2, :WIDTH], gv_s[1:2, 2 * WIDTH :], gv_s[2:5, :WIDTH],
             gv_t[0:1, :WIDTH], gv_t[0:1, 2 * WIDTH :], gv_t[1:3, :WIDTH]]
        )
        lower = me_n < 2
        places = (me_n, jnp.bitwise_xor(me_n, 1), jnp.where(lower, 2, 1), jnp.where(lower, 3, 0))
        hidden_rows = jnp.zeros((slices, WIDTH), F32)
        for place, row in zip(places, (gb_a[0], gb_a[1], gb_b[0], gb_b[1])):
            hidden_rows = lax.dynamic_update_slice(hidden_rows, row[None], (place, 0))
        vectors = lax.psum(jnp.concatenate([vectors, hidden_rows], axis=0), ("wide", "narrow"))
        mine = lax.dynamic_slice(vectors, (0, me_n * share), (13, share))
        grad_in_bias = lax.dynamic_slice(vectors, (13 + me_n, 0), (1, WIDTH))[0]
        tg, tsh, tb, to, sg, ssh, sb, so, mg, msh, ob = [
            mine[v[0] : v[1]] if isinstance(v, tuple) else mine[v] for v in VECTORS
        ]
    return (
        layer_out, grad_clips, tg, tsh, t_qkv, tb, t_proj, to, sg, ssh, s_qkv, sb, s_proj, so, mg, msh,
        fc[0], grad_in_bias, fc[1].T, ob,
    )


def solution(mesh):
    rows = P(("wide", "narrow"), None, None)
    return jax.shard_map(
        local,
        mesh=mesh,
        in_specs=(rows,) + (P(),) * 14 + (P(None, "narrow"), P("narrow"), P("narrow", None), P(), rows),
        out_specs=(
            rows,
            rows,
            P("narrow"),
            P("narrow"),
            P("narrow", "wide"),
            P(None, "narrow"),
            P("narrow", "wide"),
            P("narrow"),
            P("narrow"),
            P("narrow"),
            P("narrow", "wide"),
            P(None, "narrow"),
            P("narrow", "wide"),
            P("narrow"),
            P("narrow"),
            P("narrow"),
            P("wide", "narrow"),
            P("narrow"),
            P("narrow", "wide"),
            P("narrow"),
        ),
        check_vma=False,
    )
```

```python
from functools import partial

import jax
import jax.numpy as jnp
from jax import lax
from jax.experimental import pallas as pl
from jax.experimental.pallas import tpu as pltpu
from jax.sharding import PartitionSpec as P

HEADS = 12
HEAD_DIM = 64
FRAMES = 8
PATCHES = 196
ROWS = 208
CLASS = 196
TILE = 16
WIDTH = 768
GROUP = 4
GW = GROUP * HEAD_DIM
GROUPS = HEADS // GROUP
FPS = 2
STEP = FPS * ROWS
EPSILON = 1e-06
F32 = jnp.float32
BF = jnp.bfloat16
NEG = -1e30
VMEM_LIMIT = 62 * 2**20
CHUNKS = 8


def dg(a, b, ca, cb):
    return lax.dot_general(a, b, (((ca,), (cb,)), ((), ())), preferred_element_type=F32)


def nn(a, b):
    return dg(a, b, 1, 0)


def nt(a, b):
    return dg(a, b, 1, 1)


def tn(a, b):
    return dg(a, b, 0, 0)


def call(kernel, name, grid, ins, outs, scratch=(), flops=0, nbytes=0, remote=None):
    extra = {} if remote is None else dict(collective_id=remote, has_side_effects=True)
    return pl.pallas_call(
        kernel,
        name=name,
        grid=grid,
        in_specs=[s for s in ins],
        out_specs=[s for s, _ in outs],
        out_shape=[t for _, t in outs],
        scratch_shapes=list(scratch),
        compiler_params=pltpu.CompilerParams(vmem_limit_bytes=VMEM_LIMIT, **extra),
        cost_estimate=pl.CostEstimate(flops=flops, bytes_accessed=nbytes, transcendentals=0),
    )


def whole(*shape):
    return pl.BlockSpec(shape, lambda *i: (0,) * len(shape), pipeline_mode=pl.Buffered(1))


def frames(width):
    return pl.BlockSpec((FPS, ROWS, width), lambda i: (i, 0, 0))


def frames_out(width, dtype):
    return frames(width), jax.ShapeDtypeStruct((FRAMES, ROWS, width), dtype)


def row_of(ref):
    return ref[...].astype(F32).reshape(1, ref.shape[0])


def normed(v):
    center = v - jnp.mean(v, axis=-1, keepdims=True)
    scale = lax.rsqrt(jnp.mean(center * center, axis=-1, keepdims=True) + EPSILON)
    return center * scale, scale


def norm_back(grad, xhat, scale, gain):
    g = grad * gain
    m1 = jnp.mean(g, axis=-1, keepdims=True)
    m2 = jnp.mean(g * xhat, axis=-1, keepdims=True)
    return scale * (g - m1 - xhat * m2)


def colsum(v):
    return jnp.sum(v.astype(F32), axis=0, keepdims=True)


def head_masked(block):
    lane = lax.broadcasted_iota(jnp.int32, block.shape, 1) // HEAD_DIM
    zero = jnp.zeros_like(block)
    return jnp.concatenate([jnp.where(lane == h, block, zero) for h in range(GROUP)], axis=0)


def head_select(stacked):
    rows = stacked.shape[0] // GROUP
    lane = lax.broadcasted_iota(jnp.int32, (rows, GW), 1) // HEAD_DIM
    out = stacked[:rows]
    for h in range(1, GROUP):
        out = jnp.where(lane == h, stacked[h * rows : (h + 1) * rows], out)
    return out


def softmax(scores):
    e = jnp.exp(scores - jnp.max(scores, axis=-1, keepdims=True))
    return (e * (1.0 / jnp.sum(e, axis=-1, keepdims=True))).astype(BF)


def score_back(a, da):
    af = a.astype(F32)
    return (af * (da - jnp.sum(af * da, axis=-1, keepdims=True))).astype(BF)


def group_cols(g, which):
    start = which * WIDTH + g * GW
    return slice(start, start + GW)


def hosted():
    return lax.axis_size("wide") == CHUNKS


def own_index():
    return lax.axis_index("wide") if hosted() else jnp.int32(0)


def peer(axis, bit):
    return {axis: jnp.bitwise_xor(lax.axis_index(axis), bit)}


RING = (("wide", 1), ("wide", 2), ("narrow", 1), ("narrow", 3))
RING_ALL = RING + (("narrow", 2),)
PLANE = (("wide", 1), ("wide", 2), ("wide", 4))
LINE = (("narrow", 1), ("narrow", 2), ("narrow", 3))
PEERS = PLANE + LINE
ALL_WIDE = tuple(("wide", b) for b in range(1, 8))


def inner():
    line = lax.axis_index("narrow")
    return (line == 1) | (line == 2)


def greet(peers=PEERS):
    barrier = pltpu.get_barrier_semaphore()
    for axis, bit in peers:
        pl.semaphore_signal(barrier, inc=1, device_id=peer(axis, bit), device_id_type=pl.DeviceIdType.MESH)
    pl.semaphore_wait(barrier, len(peers))


def half_rows():
    size = WIDTH // 2
    return pl.ds(pl.multiple_of(lax.rem(lax.axis_index("wide") // 2, 2) * size, size), size)


def send(src, dst, sems, k, axis, bit):
    return pltpu.make_async_remote_copy(
        src_ref=src, dst_ref=dst, send_sem=sems.at[0, k], recv_sem=sems.at[1, k],
        device_id=peer(axis, bit), device_id_type=pl.DeviceIdType.MESH,
    )


def start(copies):
    for c in copies:
        c.start()


def wait(copies):
    for c in copies:
        c.wait()


def plus(a, b):
    return a + b


class PlaneSum:
    SEMS = 7

    @staticmethod
    def scratch(rows):
        half = rows // 2
        return [
            pltpu.VMEM((4, 2, half, WIDTH), BF),
            pltpu.VMEM((4, 2, half, WIDTH), BF),
            pltpu.VMEM((2, 2, half, WIDTH), BF),
            pltpu.SemaphoreType.DMA((2, PlaneSum.SEMS)),
            pltpu.SemaphoreType.DMA,
        ]

    def __init__(self, own, oth, recv, got, near, sems, own_sem):
        self.own, self.oth, self.recv, self.got, self.near, self.sems = own, oth, recv, got, near, sems
        self.own_sem = own_sem

    def load(self):
        return [pltpu.make_async_copy(self.own, self.got, self.own_sem)]

    def chip(self):
        return [send(self.oth, self.recv, self.sems, 0, "wide", 1)]

    def first(self):
        got, near, sems = self.got, self.near, self.sems
        return [
            send(got.at[1, 0], near.at[0, 0], sems, 1, "wide", 2),
            send(got.at[3, 0], near.at[0, 1], sems, 2, "wide", 2),
            send(got.at[2, 1], near.at[1, 0], sems, 3, "wide", 4),
            send(got.at[3, 1], near.at[1, 1], sems, 4, "wide", 4),
        ]

    def second(self):
        got, recv, sems = self.got, self.recv, self.sems
        return [
            send(got.at[2, 0], recv.at[0, 0], sems, 5, "wide", 4),
            send(got.at[1, 1], recv.at[0, 1], sems, 6, "wide", 2),
        ]

    def load_both(self):
        return self.load() + [pltpu.make_async_copy(self.oth, self.recv, self.sems.at[0, 0])]

    def stage0(self):
        start(self.load())
        start(self.chip())

    def arrived(self):
        wait(self.load_both())
        self.sum_chip()

    def stage1(self):
        wait(self.load())
        wait(self.chip())
        self.sum_chip()

    def sum_chip(self):
        @pl.loop(0, 4)
        def _(q):
            for h in range(2):
                self.got[q, h] = plus(self.got[q, h], self.recv[q, h])

        start(self.first())

    def stage2(self):
        wait(self.first())
        for q, h, way, i in ((0, 0, 0, 0), (2, 0, 0, 1), (0, 1, 1, 0), (1, 1, 1, 1)):
            self.got[q, h] = plus(self.got[q, h], self.near[way, i])
        start(self.second())

    def stage3(self):
        wait(self.second())
        for h in range(2):
            self.got[0, h] = plus(self.got[0, h], self.recv[0, h])


def halves(piece):
    return piece.reshape(4, 2, -1, WIDTH)


class LineSum:
    def __init__(self, parts, recv, sems):
        self.parts, self.recv, self.sems = parts, recv, sems

    @staticmethod
    def scratch(rows, width):
        return [pltpu.VMEM((3, rows, width), BF), pltpu.SemaphoreType.DMA((2, 3))]

    def copies(self):
        line = lax.axis_index("narrow")
        return [
            send(self.parts.at[jnp.bitwise_xor(line, b)], self.recv.at[b - 1], self.sems, b - 1, "narrow", b)
            for b in (1, 2, 3)
        ]

    def result(self):
        wait(self.copies())
        total = self.parts[lax.axis_index("narrow")].astype(F32)
        for b in range(3):
            total = total + self.recv[b].astype(F32)
        return total


def shifted(src_ref, frame, first_row, class_on):
    start = 1 + frame * PATCHES
    base = jnp.minimum(start // TILE * TILE, src_ref.shape[0] // TILE * TILE - ROWS - TILE)
    base = pl.multiple_of(base, TILE)
    chunk = src_ref[pl.ds(base, ROWS + TILE), :]
    row = lax.broadcasted_iota(jnp.int32, (ROWS, ROWS + TILE), 0)
    col = lax.broadcasted_iota(jnp.int32, (ROWS, ROWS + TILE), 1)
    pick = ((col == row + (start - base)) & (row < PATCHES)).astype(F32).astype(BF)
    got = nn(pick, chunk)
    last = src_ref.shape[0] - 1
    end_row = src_ref[last : last + 1, :].astype(F32)
    tail = got[ROWS - TILE :]
    trow = lax.broadcasted_iota(jnp.int32, tail.shape, 0) + (ROWS - TILE)
    tail = jnp.where((trow == PATCHES - 1) & (frame == FRAMES - 1), end_row, tail)
    tail = jnp.where((trow == CLASS) & class_on, first_row, tail)
    return jnp.concatenate([got[: ROWS - TILE], tail], axis=0)


def time_kernel(
    clip_ref, cot_ref, gain_ref, shift_ref, bias_ref, w_ref, win_ref, wout_ref, bin_ref,
    p_ref, g_ref, h_ref, z_ref, o_ref, a_ref, near_ref, far_ref, rows_ref,
    z_buf, b_buf, sems, b_sems,
):
    step = pl.program_id(0)
    row_steps = FRAMES // FPS
    steps = pl.num_programs(0)
    core = lax.rem(lax.axis_index("wide"), 2)
    part = half_rows()

    def near(src):
        return send(src.at[part], near_ref, sems, 0, "narrow", 1)

    def middle(src):
        return send(src.at[part], far_ref, sems, 1, "narrow", 3)

    def biases():
        return [send(b_buf, rows_ref.at[b], b_sems, b, "narrow", b) for b in (1, 2, 3)]

    def own_bias():
        return pltpu.make_async_copy(b_buf, rows_ref.at[0], b_sems.at[0, 0])

    @pl.when(step == 0)
    def _():
        b_buf[...] = jnp.broadcast_to(row_of(bin_ref), b_buf.shape).astype(BF)
        greet(RING_ALL)
        for c, src in enumerate((win_ref, wout_ref)):

            @pl.when(core == c)
            def _():
                near(src).start()

            @pl.when((core == c) & inner())
            def _():
                middle(src).start()

        start(biases())
        own_bias().start()

    @pl.when(step < row_steps)
    def _():
        parts = []
        for j in range(FPS):
            frame = step * FPS + j
            p = shifted(clip_ref, frame, clip_ref[0:1, :].astype(F32), frame >= 0)
            p_ref[j] = p.astype(BF)
            xhat, _ = normed(p)
            parts.append((xhat * row_of(gain_ref) + row_of(shift_ref)).astype(BF))
            g_ref[j] = shifted(cot_ref, frame, cot_ref[0:1, :].astype(F32), frame == 0).astype(BF)
        h = jnp.concatenate(parts, axis=0)
        h_ref[...] = h.reshape(FPS, ROWS, WIDTH)
        project(h, w_ref, bias_ref, z_ref)
        z_buf[pl.ds(step * FPS, FPS)] = z_ref[...]

    @pl.when(step >= row_steps)
    def _():
        at = pl.multiple_of((step - row_steps) * TILE, TILE)
        time_attention(z_buf[:, pl.ds(at, TILE), :], o_ref, a_ref)

    @pl.when(step == steps - 1)
    def _():
        near(win_ref).wait()
        wait(biases())
        own_bias().wait()

        @pl.when(inner())
        def _():
            middle(win_ref).wait()


def project(h, w_ref, bias_ref, z_ref):
    for which in range(3):
        cols = slice(which * WIDTH, (which + 1) * WIDTH)
        z = nn(h, w_ref[:, cols])
        if which != 1:
            z = z + bias_ref[which // 2 : which // 2 + 1].astype(F32)
        z = z.astype(BF)
        if which == 0:
            z = z * jnp.asarray(HEAD_DIM**-0.5, BF)
        z_ref[:, :, cols] = z.reshape(FPS, ROWS, WIDTH)


def time_attention(z, o_ref, a_ref):
    z = z.reshape(FRAMES * TILE, 3 * WIDTH)
    row = lax.broadcasted_iota(jnp.int32, (GROUP * FRAMES * TILE, FRAMES * TILE), 0)
    col = lax.broadcasted_iota(jnp.int32, (GROUP * FRAMES * TILE, FRAMES * TILE), 1)
    same = (row % TILE) == (col % TILE)
    scores = [nt(head_masked(z[:, group_cols(g, 0)]), z[:, group_cols(g, 1)]) for g in range(GROUPS)]
    probs = [softmax(jnp.where(same, s, NEG)) for s in scores]
    mixed = [nn(probs[g], z[:, group_cols(g, 2)]) for g in range(GROUPS)]
    for g in range(GROUPS):
        a_ref[0, g] = probs[g]
        o = head_select(mixed[g]).astype(BF)
        o_ref[:, :, g * GW : (g + 1) * GW] = o.reshape(FRAMES, TILE, GW)


def space_kernel(
    p_ref, ot_ref, offset_ref, gain_ref, shift_ref, out_ref, bias_ref, wt_ref, w_ref, wo_ref,
    near_ref, held_ref,
    full_ref, h_ref, z_ref, a_ref, o_ref, x_ref, cls_ref, near_x_ref, near_s_ref, near_xs_ref, far_ref, mid_ref,
    sems,
):
    step = pl.program_id(0)

    def across():
        return send(near_ref, near_x_ref, sems, 0, "wide", 2)

    def siblings():
        return [send(near_ref, near_s_ref, sems, 1, "wide", 1), send(near_x_ref, near_xs_ref, sems, 2, "wide", 1)]

    def outward():
        return send(held_ref, far_ref, sems, 3, "narrow", 1)

    def middle():
        return send(near_ref, mid_ref, sems, 4, "narrow", 3)

    def keep():
        return pltpu.make_async_copy(held_ref, far_ref, sems.at[0, 5])

    @pl.when(step == 0)
    def _():
        greet(RING)
        across().start()

        @pl.when(inner())
        def _():
            outward().start()
            middle().start()
            keep().start()

    @pl.when(step == pl.num_programs(0) - 1)
    def _():
        across().wait()
        start(siblings())

    p = p_ref[...].reshape(STEP, WIDTH).astype(F32)
    mixed = p + nn(ot_ref[...].reshape(STEP, WIDTH), wt_ref[...]) + row_of(offset_ref)
    row = lax.broadcasted_iota(jnp.int32, (STEP, WIDTH), 0) % ROWS
    full = jnp.where(row == CLASS, p, mixed)
    full_ref[...] = full.reshape(FPS, ROWS, WIDTH)
    xhat, _ = normed(full)
    h = (xhat * row_of(gain_ref) + row_of(shift_ref)).astype(BF)
    h_ref[...] = h.reshape(FPS, ROWS, WIDTH)
    project(h, w_ref, bias_ref, z_ref)
    key = lax.broadcasted_iota(jnp.int32, (GROUP * ROWS, ROWS), 1)
    units = [(j, g) for j in range(FPS) for g in range(GROUPS)]
    scores = [nt(head_masked(z_ref[j, :, group_cols(g, 0)]), z_ref[j, :, group_cols(g, 1)]) for j, g in units]
    probs = [softmax(jnp.where(key <= CLASS, s, NEG)) for s in scores]
    mixed = [nn(a, z_ref[j, :, group_cols(g, 2)]) for a, (j, g) in zip(probs, units)]
    for a, m, (j, g) in zip(probs, mixed, units):
        a_ref[j, g] = a
        o_ref[j, :, g * GW : (g + 1) * GW] = head_select(m).astype(BF)
    y = nn(o_ref[...].reshape(STEP, WIDTH), wo_ref[...]) + row_of(out_ref)
    x_ref[...] = (full + y).reshape(FPS, ROWS, WIDTH)
    for j in range(FPS):
        at = j * ROWS + CLASS - CLASS % 8
        cls_ref[j] = y[at : at + 8]

    @pl.when(step == pl.num_programs(0) - 1)
    def _():
        wait(siblings())

        @pl.when(inner())
        def _():
            outward().wait_send()
            middle().wait()
            keep().wait()

        @pl.when(jnp.logical_not(inner()))
        def _():
            outward().wait_recv()


def mlp_kernel(first_call, *refs):
    refs = list(refs)

    def take(n):
        got = refs[:n]
        del refs[:n]
        return got

    step = pl.program_id(0)
    me = own_index()
    core = lax.rem(lax.axis_index("wide"), 2)
    row_steps = FRAMES // FPS
    chained = not first_call and hosted()
    x_ref, cls_ref, p_ref, g_ref, gain_ref, shift_ref, out_bias_ref, rows_ref = take(8)
    if first_call:
        win_ref, wout_ref = take(2)
        near_refs = take(4)
        far_ref, held_ref = take(2)
        h_ref, acc_ref, dh_ref, own_ref, oth_ref, gb_ref = take(6)
        far_x_ref, far_s_ref, far_xs_ref, far2_ref, far2_x_ref, far2_s_ref, far2_xs_ref = take(7)
        swap = jnp.int32(0)
        slots = [(1, *near_refs)]
    else:
        h_ref, acc_ref, dh_ref = take(3)
        slots = [(0, *take(4)), (1, *take(4))]
        near_refs = take(2) if chained else None
        out_ref, dx_ref, own_ref, oth_ref, gv_ref, gb_ref = take(6)
        near_out = take(1)[0] if chained else None
        swap = inner().astype(jnp.int32)
    w_buf, h_buf, g_buf, act_buf, dpre_buf, t_buf, sem = take(7)
    if first_call:
        (rsems,) = take(1)

        def move(k):
            return send(*((far_ref, far_x_ref), (far2_ref, far2_x_ref))[k], rsems, k, "wide", 2)

        def siblings(k):
            pairs = (((far_ref, far_s_ref), (far_x_ref, far_xs_ref)), ((far2_ref, far2_s_ref), (far2_x_ref, far2_xs_ref)))
            return [send(*pair, rsems, 2 + 2 * k + i, "wide", 1) for i, pair in enumerate(pairs[k])]

        def outward():
            return send(held_ref, far2_ref, rsems, 6, "narrow", 1)

        def keep():
            return pltpu.make_async_copy(held_ref, far2_ref, rsems.at[0, 7])

        @pl.when(step == 0)
        def _():
            greet(RING)
            move(0).start()

            @pl.when(inner())
            def _():
                outward().start()
                keep().start()

        @pl.when(step == 2)
        def _():
            @pl.when(inner())
            def _():
                keep().wait()

            @pl.when(jnp.logical_not(inner()))
            def _():
                outward().wait_recv()

            move(1).start()
            move(0).wait()
            start(siblings(0))

        @pl.when(step == row_steps + 1)
        def _():
            move(1).wait()
            start(siblings(1))

            @pl.when(inner())
            def _():
                outward().wait_send()

    else:
        (out_buf,) = take(1)
    if chained:
        plane = PlaneSum(*near_refs, *take(5))
        rz, zsem = take(2)

        def line_copies():
            return [send(plane.got.at[0, m, pl.ds(96, 96)], rz.at[m], zsem, m, "narrow", 1) for m in range(2)]

        def near_total():
            wait(line_copies())
            for m in range(2):
                near_out[m] = plane.got[0, m, 0:96].astype(F32) + rz[m].astype(F32)

        def line_stage():
            plane.stage3()
            start(line_copies())

        def begin():
            greet()
            plane.stage0()

    def checkpoint():
        if chained:
            for k, action in {0: begin, 1: plane.stage1, 3: plane.stage2}.items():
                pl.when(step == k)(action)

    @pl.when(step == 0)
    def _():
        if not first_call:
            gv_ref[...] = jnp.zeros_like(gv_ref)
        gb_ref[...] = jnp.zeros_like(gb_ref)

    part = half_rows()
    size = WIDTH // 2
    other = pl.ds(pl.multiple_of(size - part.start, size), size)

    def fetches(slot, mine, mine_x, sib, sib_x, c):
        into = ((mine, mine_x), (sib, sib_x)) if c == 0 else ((sib, sib_x), (mine, mine_x))
        return [
            pltpu.make_async_copy(into[m][i], w_buf.at[m, slot, rows], sem.at[4 * slot + 2 * m + i])
            for m in range(2) for i, rows in enumerate((part, other))
        ]

    @pl.when(step == 0)
    def _():
        for c in range(2):

            @pl.when(core == c)
            def _():
                for entry in slots:
                    start(fetches(*entry, c))

    def arrived(slot):
        for entry in slots:
            if entry[0] == slot:

                @pl.when(step == 0)
                def _():
                    wait(fetches(*entry, 0))

    def weight(m, slot):
        if first_call and slot == 0:
            return (win_ref, wout_ref)[m][...]
        return w_buf[m, slot]

    def bias(slot):
        if first_call:
            return rows_ref[slot, 0:1].astype(F32)
        return rows_ref[2 + jnp.bitwise_xor(slot, swap), 0:1].astype(F32)

    @pl.when(step < row_steps)
    def _():
        at = pl.ds(pl.multiple_of(step * STEP, STEP), STEP)
        x = x_ref[...].reshape(STEP, WIDTH)
        mean_cls = jnp.mean(cls_ref[:, CLASS % 8, :], axis=0, keepdims=True)
        first = p_ref[0, CLASS % TILE : CLASS % TILE + 1, :].astype(F32) + mean_cls
        row = lax.broadcasted_iota(jnp.int32, (STEP, WIDTH), 0) % ROWS
        x = jnp.where(row == CLASS, first, x)
        xhat, scale = normed(x)
        g = g_ref[...].reshape(STEP, WIDTH)
        if first_call:
            h = (xhat * row_of(gain_ref) + row_of(shift_ref)).astype(BF)
            h_ref[...] = h.reshape(FPS, ROWS, WIDTH)
            acc = x + row_of(out_bias_ref)
            dh = None
        else:
            h = h_ref[...].reshape(STEP, WIDTH)
            acc = acc_ref[...].reshape(STEP, WIDTH)
            dh = dh_ref[...].reshape(STEP, WIDTH)
        h_buf[at, :] = h
        g_buf[at, :] = g
        for s in range(2):
            arrived(s)
            if s == 1:
                checkpoint()
            cols = slice(s * WIDTH, (s + 1) * WIDTH)
            pre = nn(h, weight(0, s)) + bias(s)
            cdf = 0.5 + 0.5 * lax.erf(pre * (0.5**0.5))
            act = (pre * cdf).astype(BF)
            slope = cdf + pre * (jnp.exp(-0.5 * pre * pre) * 0.3989422804014327)
            act_buf[at, cols] = act
            dpre = (nt(g, weight(1, s)) * slope).astype(BF)
            dpre_buf[at, cols] = dpre
            gb_ref[s : s + 1, :] += colsum(dpre)
            acc = acc + nn(act, weight(1, s))
            back = nt(dpre, weight(0, s))
            dh = back if dh is None else dh + back
        if first_call:
            acc_ref[...] = acc.reshape(FPS, ROWS, WIDTH)
            dh_ref[...] = dh.reshape(FPS, ROWS, WIDTH)
        else:
            for k in range(row_steps):

                @pl.when(step == k)
                def _():
                    if k == 0:
                        out_buf[0:1, :] = acc[CLASS : CLASS + 1]
                    for j in range(FPS):
                        start = 1 + (k * FPS + j) * PATCHES
                        out_buf[start : start + PATCHES, :] = acc[j * ROWS : j * ROWS + PATCHES]

            gf = g.astype(F32)
            dx_ref[...] = (gf + norm_back(dh, xhat, scale, row_of(gain_ref))).reshape(FPS, ROWS, WIDTH)
            gv_ref[0:1] += colsum(dh * xhat)
            gv_ref[1:2] += colsum(dh)
            gv_ref[2:3] += colsum(gf)

    def matrix(unit, left_ref, right_ref):
        t_buf[...] = left_ref[...].T
        for s in range(2):
            got = nn(t_buf[...], right_ref[:, s * WIDTH : (s + 1) * WIDTH]).astype(BF)
            for w in range(CHUNKS):
                put_chunk(own_ref, oth_ref, me, w, 2 * unit + jnp.bitwise_xor(s, swap), got[w * 96 : (w + 1) * 96])

    @pl.when(step == row_steps)
    def _():
        matrix(0, h_buf, dpre_buf)
        if not first_call:
            out_ref[0] = out_buf[...].astype(BF)

    @pl.when(step == row_steps + 1)
    def _():
        if chained:
            line_stage()
        matrix(1, g_buf, act_buf)
        if chained:
            near_total()
        if first_call:
            wait(siblings(0))
            wait(siblings(1))


def put_chunk(own_ref, oth_ref, me, w, unit, value):
    rel = jnp.bitwise_xor(me, w)
    place = rel // 2
    for c, ref in enumerate((own_ref, oth_ref)):

        @pl.when(rel % 2 == c)
        def _():
            ref[place, unit] = value


def space_back_kernel(*refs):
    refs = list(refs)

    def take(n):
        got = refs[:n]
        del refs[:n]
        return got

    dx_ref, dcls_ref, full_ref, z_ref, a_ref, gain_ref, wo_ref, w_ref, wt_ref = take(9)
    far_refs = take(2) if hosted() else None
    dy_ref, dz_ref, df_ref, dyt_ref, dot_ref, gv_ref = take(6)
    far_out = take(1)[0] if hosted() else None
    (do_ref,) = take(1)
    step = pl.program_id(0)
    plane = PlaneSum(*far_refs, *take(5)) if hosted() else None

    def begin():
        greet(PLANE)
        plane.stage0()

    def finish():
        plane.stage3()
        far_out[...] = plane.got[0]

    def checkpoint(plan):
        if hosted():
            for k, action in plan.items():
                pl.when(step == k)(action)

    @pl.when(step == 0)
    def _():
        gv_ref[...] = jnp.zeros_like(gv_ref)

    dx = dx_ref[...].reshape(STEP, WIDTH)
    row = lax.broadcasted_iota(jnp.int32, (STEP, WIDTH), 0) % ROWS
    dcls = dcls_ref[0, CLASS % 8 : CLASS % 8 + 1, :] * (1.0 / FRAMES)
    dy = jnp.where(row == CLASS, dcls, jnp.where(row < CLASS, dx, 0.0)).astype(BF)
    dy_ref[...] = dy.reshape(FPS, ROWS, WIDTH)
    gv_ref[0:1, :WIDTH] += colsum(dy)
    do_ref[...] = nt(dy, wo_ref[...]).astype(BF)
    for j in range(FPS):
        if j > 0:
            checkpoint({0: begin, 1: plane.stage1} if hosted() else {})
        units = [(j, g) for g in range(GROUPS)]
        dos = [head_masked(do_ref[j * ROWS : (j + 1) * ROWS, g * GW : (g + 1) * GW]) for j, g in units]
        das = [nt(do, z_ref[j, :, group_cols(g, 2)]) for do, (j, g) in zip(dos, units)]
        dvs = [tn(a_ref[j, g], do) for do, (j, g) in zip(dos, units)]
        dss = [score_back(a_ref[j, g], da) for da, (j, g) in zip(das, units)]
        for dv, (j, g) in zip(dvs, units):
            dz_ref[j, :, group_cols(g, 2)] = dv.astype(BF)
        dqs = [nn(ds, z_ref[j, :, group_cols(g, 1)]) for ds, (j, g) in zip(dss, units)]
        dks = [tn(ds, head_masked(z_ref[j, :, group_cols(g, 0)])) for ds, (j, g) in zip(dss, units)]
        for dq, dk, (j, g) in zip(dqs, dks, units):
            dz_ref[j, :, group_cols(g, 0)] = (head_select(dq) * HEAD_DIM**-0.5).astype(BF)
            dz_ref[j, :, group_cols(g, 1)] = dk.astype(BF)
    dz = dz_ref[...].reshape(STEP, 3 * WIDTH)
    gv_ref[1:2, :] += colsum(dz)
    dh = nt(dz, w_ref[...])
    xhat, scale = normed(full_ref[...].reshape(STEP, WIDTH))
    gv_ref[2:3, :WIDTH] += colsum(dh * xhat)
    gv_ref[3:4, :WIDTH] += colsum(dh)
    df = dx + norm_back(dh, xhat, scale, row_of(gain_ref))
    df_ref[...] = df.reshape(FPS, ROWS, WIDTH)
    dyt = jnp.where(row < CLASS, df, 0.0).astype(BF)
    dyt_ref[...] = dyt.reshape(FPS, ROWS, WIDTH)
    gv_ref[4:5, :WIDTH] += colsum(dyt)
    dot_ref[...] = nt(dyt, wt_ref[...]).astype(BF).reshape(FPS, ROWS, WIDTH)
    checkpoint({2: plane.stage2, 3: finish} if hosted() else {})


def put_rows(own_ref, oth_ref, me, w, start, value):
    rel = jnp.bitwise_xor(me, w)
    place = rel // 2
    for c, ref in enumerate((own_ref, oth_ref)):

        @pl.when(rel % 2 == c)
        def _():
            ref[place, start : start + value.shape[0], :] = value


PIECE = (CHUNKS // 2, 384, WIDTH)
QKV_ROWS = 288
PROJ_ROWS = 192


def time_back_kernel(*refs):
    refs = list(refs)

    def take(n):
        got = refs[:n]
        del refs[:n]
        return got

    z_ref, a_ref, do_ref, h_any, dzs_ref, hs_ref = take(6)
    near_ref, far_ref = take(2) if hosted() else (None, None)
    dz_ref, own_ref, oth_out = take(3)
    parts_ref, fc_ref = take(2) if hosted() else (None, None)
    s_own, s_oth = (None, None) if hosted() else take(2)
    dz_buf, h_buf, h_sem = take(3)
    oth_ref = oth_out
    chunks = ROWS // TILE
    step = pl.program_id(0) - 2
    me = own_index()
    half = CHUNKS // 2

    def load():
        return pltpu.make_async_copy(h_any, h_buf, h_sem)

    if hosted():
        s_own, s_oth = take(2)
        plane = PlaneSum(halves_ref(s_own), halves_ref(s_oth), *take(5))
        rz, zsem, oth_ref, x_sems = take(4)

        def line_copies():
            return [
                send(far_ref.at[m, pl.ds(96 * i, 96)], rz.at[m, i], zsem, 2 * m + i, "narrow", 2 + i)
                for m in range(2) for i in range(2)
            ]

        def exchange(k):
            base = pl.multiple_of(2 * jnp.bitwise_xor(me // 4, k), 2)
            place = pl.ds(base, 2)
            return send(oth_ref.at[place], oth_out.at[place], x_sems, k, "wide", 1)

        @pl.when(step == -2)
        def _():
            greet()
            start(line_copies())

    for k in range(2):

        @pl.when(step == k - 2)
        def _():
            got = tn(dzs_ref[...], hs_ref[...]).astype(BF)
            for i in range(half):
                put_rows(s_own, s_oth, me, k * half + i, 0, got[i * QKV_ROWS : (i + 1) * QKV_ROWS])

    if hosted():
        pl.when(step == 0)(plane.stage0)
        pl.when(step == 4)(plane.stage1)
        pl.when(step == chunks - 1)(plane.stage2)

    pl.when(step == 0)(lambda: load().start())

    @pl.when((step >= 0) & (step < chunks))
    def _():
        z = z_ref[...].reshape(FRAMES * TILE, 3 * WIDTH)
        dot = do_ref[...].reshape(FRAMES * TILE, WIDTH)
        groups = range(GROUPS)
        dos = [head_masked(dot[:, g * GW : (g + 1) * GW]) for g in groups]
        das = [nt(dos[g], z[:, group_cols(g, 2)]) for g in groups]
        dvs = [tn(a_ref[0, g], dos[g]) for g in groups]
        dss = [score_back(a_ref[0, g], das[g]) for g in groups]
        dqs = [nn(dss[g], z[:, group_cols(g, 1)]) for g in groups]
        dks = [tn(dss[g], head_masked(z[:, group_cols(g, 0)])) for g in groups]
        for g in groups:
            for which, v in enumerate((head_select(dqs[g]) * HEAD_DIM**-0.5, dks[g], dvs[g])):
                dz_ref[:, :, group_cols(g, which)] = v.astype(BF).reshape(FRAMES, TILE, GW)
        dz_buf[:, pl.ds(pl.multiple_of(step * TILE, TILE), TILE), :] = dz_ref[...]

    pl.when(step == chunks)(lambda: load().wait())
    for k in range(2):

        @pl.when(step == chunks + k)
        def _():
            left = dz_buf[:, :, k * half * 288 : (k + 1) * half * 288]
            got = tn(left.reshape(FRAMES * ROWS, half * 288), h_buf[...]).astype(BF)
            for i in range(half):
                put_rows(own_ref, oth_ref, me, k * half + i, 0, got[i * 288 : (i + 1) * 288])
            if hosted():
                exchange(k).start()

    if hosted():

        @pl.when(step == chunks + 1)
        def _():
            wait(line_copies())
            for m in range(2):
                fc_ref[m] = near_ref[m] + rz[m, 0].astype(F32) + rz[m, 1].astype(F32)
            plane.stage3()
            cut_columns(plane.got, parts_ref)
            for k in range(2):
                exchange(k).wait()


def halves_ref(ref):
    return ref.reshape(4, 2, ref.shape[1] // 2, WIDTH)


def cut_columns(got, parts_ref):
    size = WIDTH // parts_ref.shape[0]
    for n in range(parts_ref.shape[0]):
        cols = slice(n * size, (n + 1) * size)
        parts_ref[n] = jnp.concatenate([got[0, 0, :, cols], got[0, 1, :, cols]], axis=1)


def turned(total):
    size = total.shape[1] // 2
    return jnp.concatenate([total[:, :size].T, total[:, size:].T], axis=1)


VEC_ROWS = 32


def time_out_kernel(*refs):
    refs = list(refs)

    def take(n):
        got = refs[:n]
        del refs[:n]
        return got

    dz_ref, p_ref, df_ref, gain_ref, w_ref = take(5)
    grads_in = take(4)
    if hosted():
        time_refs = take(2)
        s_parts, gvm_ref, gvs_ref, gba_ref, gbb_ref = take(5)
    dp_ref, gv_ref = take(2)
    if hosted():
        sq_ref, sp_ref, tp_ref, tq_ref, share_ref, hid_ref = take(6)
        p_own, p_oth = take(2)
    else:
        p_own, p_oth = take(2)
    dp_buf, dp_sem, g_bufs, g_sems = take(4)
    step = pl.program_id(0)
    row_steps = FRAMES // FPS
    line = lax.axis_index("narrow")
    me = own_index()
    if hosted():
        plane = PlaneSum(*time_refs, *take(5))
        p_plane = PlaneSum(halves_ref(p_own), halves_ref(p_oth), *take(5))
        parts, p_parts = take(2)
        s_line = LineSum(s_parts, *take(2))
        t_line = LineSum(parts, *take(2))
        p_line = LineSum(p_parts, *take(2))
        vbuf, vrecv, vlow, vlow_recv, vsem, lbuf, lrecv, lsem = take(8)

        def early(k):
            axis, bit = (("wide", 1), ("wide", 2), ("wide", 4))[k]
            return send(vbuf, vrecv.at[k], vsem, k, axis, bit)

        def early_add(k):
            early(k).wait()
            vbuf[...] += vrecv[k]

        def early_line():
            return [send(vlow, vlow_recv.at[b - 1], vsem, 2 + b, "narrow", b) for b in (1, 2, 3)]

        def late_wide():
            return [send(lbuf, lrecv.at[b - 1], lsem, b - 1, "wide", b) for b in range(1, CHUNKS)]

        def late_line():
            return [send(lrecv.at[0], lrecv.at[6 + b], lsem, 6 + b, "narrow", b) for b in (1, 2, 3)]

        @pl.when(step == 0)
        def _():
            start(plane.load_both())
            greet(ALL_WIDE + LINE)
            start(s_line.copies())
            plane.arrived()
            vbuf[...] = jnp.zeros_like(vbuf)
            vbuf[0:3, :] = gvm_ref[0:3, :]
            for i, r, c in ((3, 0, 0), (4, 1, 0), (5, 1, 2), (6, 2, 0), (7, 3, 0), (8, 4, 0)):
                vbuf[i : i + 1, :] = gvs_ref[r : r + 1, c * WIDTH : (c + 1) * WIDTH]
            low = line < 2
            places = (line, jnp.bitwise_xor(line, 1), jnp.where(low, 2, 1), jnp.where(low, 3, 0))
            for place, (ref, r) in zip(places, ((gba_ref, 0), (gba_ref, 1), (gbb_ref, 0), (gbb_ref, 1))):
                vbuf[pl.ds(13 + place, 1), :] = ref[r : r + 1, :]
            early(0).start()

        @pl.when(step == 1)
        def _():
            early_add(0)
            early(1).start()

        pl.when(step == 2)(p_plane.stage0)

        @pl.when(step == 3)
        def _():
            plane.stage2()
            p_plane.stage1()
            early_add(1)
            early(2).start()

        @pl.when(step == 4)
        def _():
            plane.stage3()
            cut_columns(plane.got, parts)
            start(t_line.copies())
            early_add(2)
            vlow[...] = vbuf[...].astype(BF)
            start(early_line())

    def load(i):
        return pltpu.make_async_copy(grads_in[i], g_bufs.at[i], g_sems.at[i])

    def saves(k):
        rows = pl.ds(1 + k * FPS * PATCHES, FPS * PATCHES)
        return pltpu.make_async_copy(dp_buf.at[rows], dp_ref.at[rows], dp_sem.at[k])

    def save_class():
        return pltpu.make_async_copy(dp_buf.at[pl.ds(0, 1)], dp_ref.at[pl.ds(0, 1)], dp_sem.at[row_steps])

    @pl.when(step == 0)
    def _():
        start([load(i) for i in range(4)])
        gv_ref[...] = jnp.zeros_like(gv_ref)
        dp_buf[0:1, 0, :] = jnp.zeros((1, WIDTH), F32)

    for k in range(2):

        @pl.when(step == k)
        def _():
            for i in (2 * k, 2 * k + 1):
                load(i).wait()
            got = tn(g_bufs[2 * k], g_bufs[2 * k + 1]).astype(BF)
            for w in range(CHUNKS):
                put_rows(p_own, p_oth, me, w, 96 * k, got[w * 96 : (w + 1) * 96])

    @pl.when((step >= 2) & (step < row_steps + 2))
    def _():
        dz = dz_ref[...].reshape(STEP, 3 * WIDTH)
        gv_ref[0:1, :] += colsum(dz)
        dh = nt(dz, w_ref[...])
        xhat, scale = normed(p_ref[...].reshape(STEP, WIDTH).astype(F32))
        gv_ref[1:2, :WIDTH] += colsum(dh * xhat)
        gv_ref[2:3, :WIDTH] += colsum(dh)
        df = df_ref[...].reshape(STEP, WIDTH)
        dp = df + norm_back(dh, xhat, scale, row_of(gain_ref))
        for j in range(FPS):
            dp_buf[0:1, 0, :] += df[j * ROWS + CLASS : j * ROWS + CLASS + 1]
        for k in range(row_steps):

            @pl.when(step == k + 2)
            def _():
                for j in range(FPS):
                    begin = 1 + (k * FPS + j) * PATCHES
                    dp_buf[begin : begin + PATCHES, 0, :] = dp[j * ROWS : j * ROWS + PATCHES]
                saves(k).start()

    @pl.when(step == row_steps + 1)
    def _():
        save_class().start()

    if hosted():

        @pl.when(step == row_steps + 2)
        def _():
            lbuf[...] = jnp.zeros_like(lbuf)
            for i, r, c in ((0, 0, 0), (1, 0, 2), (2, 1, 0), (3, 2, 0)):
                lbuf[i : i + 1, :] = gv_ref[r : r + 1, c * WIDTH : (c + 1) * WIDTH]
            start(late_wide())
            p_plane.stage2()
            sq_ref[...] = turned(s_line.result())
            wait(late_wide())
            late = lbuf[...]
            for b in range(CHUNKS - 1):
                late = late + lrecv[b]
            lrecv[0] = late
            start(late_line())
            p_plane.stage3()
            cut_columns(p_plane.got, p_parts)
            start(p_line.copies())
            wait(early_line())
            vectors = vbuf[...] + vlow_recv[0].astype(F32) + vlow_recv[1].astype(F32) + vlow_recv[2].astype(F32)
            tq_ref[...] = turned(t_line.result())
            wait(late_line())
            late = lrecv[0] + lrecv[7] + lrecv[8] + lrecv[9]
            vectors = jnp.concatenate([vectors[0:9], late[0:4], vectors[13:]], axis=0)
            size = WIDTH // 4
            share = vectors[:, :size]
            hidden = vectors[13:14, :]
            for n in range(1, 4):
                share = jnp.where(line == n, vectors[:, n * size : (n + 1) * size], share)
                hidden = jnp.where(line == n, vectors[13 + n : 14 + n, :], hidden)
            share_ref[...] = share
            hid_ref[...] = hidden
            total = turned(p_line.result())
            sp_ref[...] = total[:, :96]
            tp_ref[...] = total[:, 96:]

    @pl.when(step == pl.num_programs(0) - 1)
    def _():
        for k in range(row_steps):
            saves(k).wait()
        save_class().wait()


VECTORS = (11, 12, (9, 11), 8, 6, 7, (4, 6), 3, 0, 1, 2)


def outputs_kernel(share_ref, hid_ref, *refs):
    count = len(refs) - len(VECTORS) - 1
    ins, outs = refs[: count // 2], refs[count // 2 :]
    for src, dst in zip(ins, outs):
        dst[...] = src[...]
    outs = outs[len(ins) :]
    for rows, dst in zip(VECTORS, outs):
        if isinstance(rows, tuple):
            dst[...] = share_ref[rows[0] : rows[1], :]
        else:
            dst[...] = share_ref[rows : rows + 1, :].reshape(dst.shape)
    outs[-1][...] = hid_ref[0:1, :].reshape(outs[-1].shape)


def flip(value, axis, bit):
    return lax.ppermute(value, axis, [(i, i ^ bit) for i in range(lax.axis_size(axis))])


def unit_sum(own, oth):
    both = jnp.stack([own, oth], axis=1).reshape(CHUNKS, 4, 96, WIDTH)
    both = both.transpose(1, 0, 2, 3).reshape(4, WIDTH, WIDTH)
    both = lax.psum_scatter(both, "wide", scatter_dimension=1, tiled=True)
    return both.reshape(2, 2, -1, WIDTH)


def piece_sum(own, oth, sizes, me):
    both = jnp.stack([own, oth], axis=1).reshape(CHUNKS, -1, WIDTH)
    found, at = [], 0
    for size in sizes:
        rows = both[:, at * 96 : (at + size) * 96].reshape(size * WIDTH, WIDTH)
        at += size
        rows = lax.psum_scatter(rows, "wide", scatter_dimension=0, tiled=True)
        parts = rows.T.reshape(lax.axis_size("narrow"), -1, rows.shape[0])
        found.append(line_sum(parts, me))
    return found


def line_sum(parts, me):
    total = lax.dynamic_index_in_dim(parts, me, 0, False).astype(F32)
    for bit in (1, 2, 3):
        other = lax.dynamic_index_in_dim(parts, jnp.bitwise_xor(me, bit), 0, False)
        total = total + flip(other, "narrow", bit).astype(F32)
    return total


def local(
    video_clips, time_gain, time_shift, time_qkv, time_bias, time_proj, time_offset,
    space_gain, space_shift, space_qkv, space_bias, space_proj, space_offset,
    mlp_gain, mlp_shift, fc_in, in_bias, fc_out, out_bias, cotangent,
):
    slices = lax.axis_size("narrow")
    tokens = video_clips.shape[1]
    clip = video_clips[0]
    cot = cotangent[0]
    vec = pl.BlockSpec((WIDTH,), lambda *i: (0,), pipeline_mode=pl.Buffered(1))
    me_n = lax.axis_index("narrow")
    any_ref = pl.BlockSpec(memory_space=pl.ANY)
    message = (any_ref, jax.ShapeDtypeStruct((WIDTH // 2, WIDTH), BF))
    bias_rows = (any_ref, jax.ShapeDtypeStruct((4, TILE, WIDTH), BF))

    chunks = ROWS // TILE
    a_time = jax.ShapeDtypeStruct((chunks, GROUPS, GROUP * FRAMES * TILE, FRAMES * TILE), BF)

    def a_chunk(first):
        return pl.BlockSpec((1, *a_time.shape[1:]), lambda i: (jnp.clip(i - first, 0, chunks - 1), 0, 0, 0))

    a_space = (pl.BlockSpec((FPS, GROUPS, GROUP * ROWS, ROWS), lambda i: (i, 0, 0, 0)),
               jax.ShapeDtypeStruct((FRAMES, GROUPS, GROUP * ROWS, ROWS), BF))

    last = FRAMES // FPS - 1
    steps = last + 1
    rows = FRAMES * ROWS

    def row_in(width):
        return pl.BlockSpec((FPS, ROWS, width), lambda i: (jnp.minimum(i, last), 0, 0))

    def row_out(width, dtype):
        return row_in(width), jax.ShapeDtypeStruct((FRAMES, ROWS, width), dtype)

    def chunk(width, first):
        return pl.BlockSpec((FRAMES, TILE, width), lambda i: (0, jnp.clip(i - first, 0, chunks - 1), 0))

    def chunk_out(width, first):
        return chunk(width, first), jax.ShapeDtypeStruct((FRAMES, ROWS, width), BF)

    p, g, ht, zt, ot, at, near, held, biases = call(
        time_kernel, "time", (steps + chunks,),
        [whole(tokens, WIDTH), whole(tokens, WIDTH), vec, vec, whole(2, WIDTH), whole(WIDTH, 3 * WIDTH),
         any_ref, any_ref, vec],
        [row_out(WIDTH, BF), row_out(WIDTH, BF), row_out(WIDTH, BF), row_out(3 * WIDTH, BF),
         chunk_out(WIDTH, steps), (a_chunk(steps), a_time)] + [message] * 2 + [bias_rows],
        scratch=[pltpu.VMEM((FRAMES, ROWS, 3 * WIDTH), BF), pltpu.VMEM((TILE, WIDTH), BF),
                 pltpu.SemaphoreType.DMA((2, 2)), pltpu.SemaphoreType.DMA((2, 4))],
        remote=1,
    )(clip, cot, time_gain, time_shift, time_bias, time_qkv, fc_in, fc_out, in_bias)
    full, hs, zs, a_s, o_s, xs, ycls, near_x, near_s, near_xs, far, held2 = call(
        space_kernel, "space", (steps,),
        [frames(WIDTH), frames(WIDTH), vec, vec, vec, vec, whole(2, WIDTH),
         whole(WIDTH, WIDTH), whole(WIDTH, 3 * WIDTH), whole(WIDTH, WIDTH)] + [any_ref] * 2,
        [frames_out(WIDTH, F32), frames_out(WIDTH, BF), frames_out(3 * WIDTH, BF), a_space,
         frames_out(WIDTH, BF), frames_out(WIDTH, F32),
         (pl.BlockSpec((FPS, 8, WIDTH), lambda i: (i, 0, 0)), jax.ShapeDtypeStruct((FRAMES, 8, WIDTH), F32))]
        + [message] * 5,
        scratch=[pltpu.SemaphoreType.DMA((2, 6))],
        remote=2,
    )(p, ot, time_offset, space_gain, space_shift, space_offset, space_bias, time_proj, space_qkv, space_proj, near, held)
    unit_shape = (CHUNKS // 2, 4, 96, WIDTH)
    units = [(whole(*unit_shape), jax.ShapeDtypeStruct(unit_shape, BF))] * 2
    vec_out = [(whole(8, WIDTH), jax.ShapeDtypeStruct((8, WIDTH), F32))] * 2
    bufs = [
        pltpu.VMEM((2, 2, WIDTH, WIDTH), BF),
        pltpu.VMEM((rows, WIDTH), BF), pltpu.VMEM((rows, WIDTH), BF),
        pltpu.VMEM((rows, 2 * WIDTH), BF), pltpu.VMEM((rows, 2 * WIDTH), BF), pltpu.VMEM((WIDTH, rows), BF),
        pltpu.SemaphoreType.DMA((8,)),
    ]
    mlp_in = [row_in(WIDTH), whole(FRAMES, 8, WIDTH),
              pl.BlockSpec((1, TILE, WIDTH), lambda i: (0, CLASS // TILE, 0)), row_in(WIDTH), vec, vec, vec,
              whole(4, TILE, WIDTH)]
    mlp_args = (xs, ycls, p, g, mlp_gain, mlp_shift, out_bias, biases)
    hm, acc, dh, a_own, a_oth, gb_a, far_x, far_s, far_xs, far2, far2_x, far2_s, far2_xs = call(
        partial(mlp_kernel, True), "mlp_near", (last + 3,),
        mlp_in + [whole(WIDTH, WIDTH), whole(WIDTH, WIDTH)] + [any_ref] * 6,
        [row_out(WIDTH, BF), row_out(WIDTH, F32), row_out(WIDTH, F32)] + units + vec_out[:1] + [message] * 7,
        scratch=bufs + [pltpu.SemaphoreType.DMA((2, 8))],
        remote=3,
    )(*mlp_args, fc_in, fc_out, near, near_x, near_s, near_xs, far, held2)
    units_in = []
    near_out = []
    near_args = []
    near_scratch = []
    if hosted():
        units_in = [any_ref] * 2
        near_args = [halves(a_own), halves(a_oth)]
        near_out = [(whole(2, 96, WIDTH), jax.ShapeDtypeStruct((2, 96, WIDTH), F32))]
        near_scratch = PlaneSum.scratch(384) + [pltpu.VMEM((2, 96, WIDTH), BF), pltpu.SemaphoreType.DMA((2, 2))]
    layer_out, dxs, b_own, b_oth, gv_m, gb_b, *near_sum = call(
        partial(mlp_kernel, False), "mlp_far", (last + 3,),
        mlp_in + [row_in(WIDTH), row_in(WIDTH), row_in(WIDTH)] + [any_ref] * 8 + units_in,
        [(whole(1, tokens, WIDTH), jax.ShapeDtypeStruct((1, tokens, WIDTH), BF)), row_out(WIDTH, F32)]
        + units + vec_out + near_out,
        scratch=bufs + [pltpu.VMEM((tokens, WIDTH), F32)] + near_scratch,
        remote=4 if hosted() else None,
    )(*mlp_args, hm, acc, dh, far, far_x, far_s, far_xs, far2, far2_x, far2_s, far2_xs, *near_args)

    far_in, far_args, far_out, far_scratch = [], [], [], []
    if hosted():
        far_in = [any_ref] * 2
        far_args = [halves(b_own), halves(b_oth)]
        far_out = [(whole(2, 192, WIDTH), jax.ShapeDtypeStruct((2, 192, WIDTH), BF))]
        far_scratch = PlaneSum.scratch(384)
    dys, dzs, df, dyt, dot, gv_s, *far_sum = call(
        space_back_kernel, "space_back", (steps,),
        [frames(WIDTH), pl.BlockSpec((1, 8, WIDTH), lambda i: (0, CLASS // 8, 0)), frames(WIDTH),
         frames(3 * WIDTH), a_space[0], vec,
         whole(WIDTH, WIDTH), whole(WIDTH, 3 * WIDTH), whole(WIDTH, WIDTH)] + far_in,
        [frames_out(WIDTH, BF), frames_out(3 * WIDTH, BF), frames_out(WIDTH, F32),
         frames_out(WIDTH, BF), frames_out(WIDTH, BF),
         (whole(8, 3 * WIDTH), jax.ShapeDtypeStruct((8, 3 * WIDTH), F32))] + far_out,
        scratch=[pltpu.VMEM((STEP, WIDTH), BF)] + far_scratch,
        remote=5 if hosted() else None,
    )(dxs, dxs, full, zs, a_s, space_gain, space_proj, space_qkv, time_proj, *far_args)

    def flat(value):
        return value.reshape(rows, value.shape[-1])

    share = WIDTH // slices
    q_piece = (CHUNKS // 2, QKV_ROWS, WIDTH)
    q_out = (whole(*q_piece), jax.ShapeDtypeStruct(q_piece, BF))
    q_parts = (slices, QKV_ROWS // 2, 2 * WIDTH // slices)
    p_piece = (CHUNKS // 2, PROJ_ROWS, WIDTH)
    p_out = (whole(*p_piece), jax.ShapeDtypeStruct(p_piece, BF))
    p_parts = (slices, PROJ_ROWS // 2, 2 * WIDTH // slices)
    back_in, back_args, back_scratch = [], [], []
    back_out = [q_out] * 4
    if hosted():
        back_in = [whole(2, 96, WIDTH), any_ref]
        back_args = [near_sum[0], far_sum[0]]
        back_out = [q_out, (any_ref, q_out[1]), (whole(*q_parts), jax.ShapeDtypeStruct(q_parts, BF)),
                    (whole(2, 96, WIDTH), jax.ShapeDtypeStruct((2, 96, WIDTH), F32))]
        back_scratch = [pltpu.VMEM(q_piece, BF)] * 2 + PlaneSum.scratch(QKV_ROWS) + [
            pltpu.VMEM((2, 2, 96, WIDTH), BF), pltpu.SemaphoreType.DMA((2, 4)),
            pltpu.VMEM(q_piece, BF), pltpu.SemaphoreType.DMA((2, 2))]
    dzt, t_own, t_oth, *from_back = call(
        time_back_kernel, "time_back", (2 + chunks + 2,),
        [chunk(3 * WIDTH, 2), a_chunk(2), chunk(WIDTH, 2), any_ref,
         pl.BlockSpec((rows, 3 * WIDTH // 2), lambda i: (0, jnp.minimum(i, 1))), whole(rows, WIDTH)] + back_in,
        [chunk_out(3 * WIDTH, 2)] + back_out,
        scratch=[pltpu.VMEM((FRAMES, ROWS, 3 * WIDTH), BF), pltpu.VMEM((rows, WIDTH), BF), pltpu.SemaphoreType.DMA]
        + back_scratch,
        remote=7 if hosted() else None,
    )(zt, at, dot, flat(ht), flat(dzs), flat(hs), *back_args)

    def late(width):
        return pl.BlockSpec((FPS, ROWS, width), lambda i: (jnp.clip(i - 2, 0, last), 0, 0))

    out_in, out_args, out_scratch = [], [], []
    out_out = [p_out] * 2
    if hosted():
        out_in = [any_ref] * 2 + [whole(*q_parts), whole(8, WIDTH), whole(8, 3 * WIDTH)] + [whole(8, WIDTH)] * 2
        out_args = [halves(t_own), halves(t_oth), from_back[0], gv_m, gv_s, gb_a, gb_b]
        out_out = [
            (whole(*shape), jax.ShapeDtypeStruct(shape, F32))
            for shape in ((share, 288), (share, 96), (share, 96), (share, 288), (VEC_ROWS, share), (1, WIDTH))
        ]
        out_scratch = (
            PlaneSum.scratch(QKV_ROWS) + PlaneSum.scratch(PROJ_ROWS)
            + [pltpu.VMEM(q_parts, BF), pltpu.VMEM(p_parts, BF)]
            + LineSum.scratch(*q_parts[1:]) * 2 + LineSum.scratch(*p_parts[1:])
            + [pltpu.VMEM((VEC_ROWS, WIDTH), F32), pltpu.VMEM((3, VEC_ROWS, WIDTH), F32),
               pltpu.VMEM((VEC_ROWS, WIDTH), BF), pltpu.VMEM((3, VEC_ROWS, WIDTH), BF),
               pltpu.SemaphoreType.DMA((2, 6)), pltpu.VMEM((8, WIDTH), F32), pltpu.VMEM((10, 8, WIDTH), F32),
               pltpu.SemaphoreType.DMA((2, 10))]
        )
    own_scratch = [pltpu.VMEM((tokens, 1, WIDTH), F32), pltpu.SemaphoreType.DMA((steps + 1,)),
                   pltpu.VMEM((4, rows, WIDTH), BF), pltpu.SemaphoreType.DMA((4,))]
    p_scratch = [pltpu.VMEM(p_piece, BF)] * 2 if hosted() else []
    grad_clips, gv_t, *sums = call(
        time_out_kernel, "time_out", (steps + 2 + (1 if hosted() else 0),),
        [late(3 * WIDTH), late(WIDTH), late(WIDTH), vec, whole(WIDTH, 3 * WIDTH)] + [any_ref] * 4 + out_in,
        [(any_ref, jax.ShapeDtypeStruct((tokens, 1, WIDTH), F32)),
         (whole(8, 3 * WIDTH), jax.ShapeDtypeStruct((8, 3 * WIDTH), F32))] + out_out,
        scratch=p_scratch + own_scratch + out_scratch,
        remote=8 if hosted() else None,
    )(dzt, p, df, time_gain, time_qkv, flat(dys), flat(o_s), flat(dyt), flat(ot), *out_args)
    grad_clips = grad_clips.reshape(1, tokens, WIDTH)

    if hosted():
        fc = from_back[1]
        *matrices, mine, hidden_row = sums
        outs = [(whole(*m.shape), jax.ShapeDtypeStruct(m.shape, F32)) for m in matrices]
        for v in VECTORS:
            shape = (2, share) if isinstance(v, tuple) else (share,)
            outs.append((whole(*shape), jax.ShapeDtypeStruct(shape, F32)))
        outs.append((whole(WIDTH), jax.ShapeDtypeStruct((WIDTH,), F32)))
        s_qkv, s_proj, t_proj, t_qkv, *found = call(
            outputs_kernel, "outputs", (1,), [whole(*v.shape) for v in (mine, hidden_row, *matrices)], outs,
        )(mine, hidden_row, *matrices)
        tg, tsh, tb, to, sg, ssh, sb, so, mg, msh, ob, grad_in_bias = found
    else:
        near_part = unit_sum(a_own, a_oth)
        far_part = unit_sum(b_own, b_oth)
        fc = near_part[:, 0].astype(F32) + flip(near_part[:, 1], "narrow", 1).astype(F32)
        fc = fc + flip(far_part[:, 0], "narrow", 2).astype(F32) + flip(far_part[:, 1], "narrow", 3).astype(F32)
        (s_qkv,) = piece_sum(*from_back, (3,), me_n)
        s_proj, t_proj = piece_sum(*sums, (1, 1), me_n)
        (t_qkv,) = piece_sum(t_own, t_oth, (3,), me_n)
        vectors = jnp.concatenate(
            [gv_m[0:3], gv_s[0:1, :WIDTH], gv_s[1:2, :WIDTH], gv_s[1:2, 2 * WIDTH :], gv_s[2:5, :WIDTH],
             gv_t[0:1, :WIDTH], gv_t[0:1, 2 * WIDTH :], gv_t[1:3, :WIDTH]]
        )
        lower = me_n < 2
        places = (me_n, jnp.bitwise_xor(me_n, 1), jnp.where(lower, 2, 1), jnp.where(lower, 3, 0))
        hidden_rows = jnp.zeros((slices, WIDTH), F32)
        for place, row in zip(places, (gb_a[0], gb_a[1], gb_b[0], gb_b[1])):
            hidden_rows = lax.dynamic_update_slice(hidden_rows, row[None], (place, 0))
        vectors = lax.psum(jnp.concatenate([vectors, hidden_rows], axis=0), ("wide", "narrow"))
        mine = lax.dynamic_slice(vectors, (0, me_n * share), (13, share))
        grad_in_bias = lax.dynamic_slice(vectors, (13 + me_n, 0), (1, WIDTH))[0]
        tg, tsh, tb, to, sg, ssh, sb, so, mg, msh, ob = [
            mine[v[0] : v[1]] if isinstance(v, tuple) else mine[v] for v in VECTORS
        ]
    return (
        layer_out, grad_clips, tg, tsh, t_qkv, tb, t_proj, to, sg, ssh, s_qkv, sb, s_proj, so, mg, msh,
        fc[0], grad_in_bias, fc[1].T, ob,
    )


def solution(mesh):
    rows = P(("wide", "narrow"), None, None)
    return jax.shard_map(
        local,
        mesh=mesh,
        in_specs=(rows,) + (P(),) * 14 + (P(None, "narrow"), P("narrow"), P("narrow", None), P(), rows),
        out_specs=(
            rows,
            rows,
            P("narrow"),
            P("narrow"),
            P("narrow", "wide"),
            P(None, "narrow"),
            P("narrow", "wide"),
            P("narrow"),
            P("narrow"),
            P("narrow"),
            P("narrow", "wide"),
            P(None, "narrow"),
            P("narrow", "wide"),
            P("narrow"),
            P("narrow"),
            P("narrow"),
            P("wide", "narrow"),
            P("narrow"),
            P("narrow", "wide"),
            P("narrow"),
        ),
        check_vma=False,
    )
```
